256 devices in a mesh: ctx: 8 (over y, x_hi), exp: 32 (over x_lo, z, core).
Axes of the slice: x: 4 (x_hi: 2, x_lo: 2; x = x_hi * 2 + x_lo), y: 4, z: 8, core: 2. Of those that a mesh axis runs over, the one named last changes fastest.
Arguments:
- states: bfloat16 [32, 128, 2560], P('exp'), may hold values from -13 to 13
- out_grad: bfloat16 [32, 128, 2560], P('exp'), may hold values from -6 to 6
- doc_keys: bfloat16 [32, 1024, 2560], P('exp', 'ctx'), may hold values from -60 to 60
- doc_values: bfloat16 [32, 1024, 2560], P('exp', 'ctx'), may hold values from -18 to 18
- norm_gain: float32 [2560], replicated, may hold values from 0.5 to 1.5
- expert_ids: int32 [32, 128, 2], P('exp'), may hold values from 0 to 31, all different within a row; in each aligned block of 128 rows (0 to 127, 128 to 255, ..., all dimensions but the last counted through in order) at most 16 rows name the same one
- gate_values: float32 [32, 128, 2], P('exp'), may hold values from 0.5 to 2.5
- expert_weights: bfloat16 [32, 2048, 2, 2560], P('exp', 'ctx'), may hold values from -0.125 to 0.125
Outputs:
- states_grad: bfloat16 [32, 128, 2560], P('exp')
- keys_grad: bfloat16 [32, 1024, 2560], P('exp', 'ctx')
- values_grad: bfloat16 [32, 1024, 2560], P('exp', 'ctx')
- weights_grad: bfloat16 [32, 2048, 2, 2560], P('exp', 'ctx')
The draws below stay inside these ranges and needn't reach their ends.
Inputs may be any that keep to these rules, and one draw needn't show every extreme that they name: `expert_ids`: within one sequence's 128 tokens, every expert is named by at most 16 tokens.
All inputs are finite; a program needn't handle non-finite values.
Results may differ from the reference program's by a relative error of at most 0.04.
Values may be sent and summed in bfloat16 or wider, within the bound.
No kernel may reach another device: no remote copies, remote signals or barrier semaphores. Data moves between devices by JAX's collectives and lax.ppermute only.
A program may use at most 128 MiB of HBM per device.

```python
import math
import jax
import jax.numpy as jnp
import numpy as np
from jax import lax

HEADS = 20
HEAD = 128
D = 2560
EXPERT_FF = 2048
TOP = 2
EXPERTS = 32
DEC_DEV = 128
SEQS = 32
DOC_LEN = 1024
CAP = 16
N_CTX = 8


def shared_states(key):
    base = jax.random.normal(jax.random.fold_in(key, 11), (SEQS, DEC_DEV, D), jnp.float32)
    return jnp.clip(base, -4.5, 4.5)


def draw_states(key, part):
    return shared_states(key).astype(jnp.bfloat16)


def draw_doc_keys(key, part):
    noise = jax.random.normal(jax.random.fold_in(key, 23), (SEQS, DOC_LEN, D), jnp.float32)
    noise = jnp.clip(noise, -6.0, 6.0) * 2.0
    return noise.astype(jnp.bfloat16)


def steps_of(own_key, shape, cuts, low, top_value):
    level = 1.0
    for axis_at, parts in cuts:
        draws = jax.random.uniform(jax.random.fold_in(jax.random.fold_in(own_key, 6), axis_at), (parts,), jnp.float32, low / len(cuts), top_value / len(cuts))
        level = level * jnp.repeat(jnp.exp(draws), shape[axis_at] // parts).reshape((-1,) + (1,) * (len(shape) - 1 - axis_at))
    return level


def assign_block(rng, own, number, rows, number_of, top, limit, slope):
    ranking = jax.random.permutation(rng, number_of)
    heavy_load, usual = load_shares(number_of, rows * top, limit, slope, True), load_shares(number_of, rows * top, limit, slope, False)
    places = jnp.arange(number_of)

    def named(sizes, offset_by):
        used = int((sizes > 0).sum())
        fixed = max(1, used // 4)
        shifted = fixed + (places - fixed + offset_by * (used - fixed)) % max(1, number_of - fixed)
        return jnp.zeros((number_of,), jnp.int32).at[ranking[jnp.where(places < fixed, places, shifted)]].set(jnp.asarray(sizes, jnp.int32))

    sizes = jnp.where(number % 4 == 0, named(heavy_load, number // 4), named(usual, number - number // 4 - 1))
    mixed = jax.random.permutation(jax.random.fold_in(own, 3), number_of)
    source_of, receiver = mixed[0:number_of // 2 * 2:2], mixed[1:number_of // 2 * 2:2]
    room = jnp.minimum(sizes[source_of] - 1, limit - sizes[receiver]) // 2
    room = jnp.where((source_of == ranking[0]) | (receiver == ranking[0]) | (sizes[receiver] == 0), 0, jnp.maximum(room, 0))
    shifted = jax.random.randint(jax.random.fold_in(own, 4), (number_of // 2,), 0, 1 << 20) % (room + 1)
    sizes = sizes.at[source_of].add(-shifted).at[receiver].add(shifted)
    items = jnp.searchsorted(jnp.cumsum(sizes), jnp.arange(rows * top), side="right").astype(jnp.int32)
    grid = items.reshape(top, rows).T
    grid = grid[jax.random.permutation(jax.random.fold_in(own, 1), rows)]
    offset_by = jax.random.randint(jax.random.fold_in(own, 2), (rows, 1), 0, top)
    return jnp.take_along_axis(grid, (jnp.arange(top)[None, :] + offset_by) % top, axis=1)


def load_shares(number_of, total, reach, slope, full):
    loads = [(1 << 20) // math.isqrt(rank ** slope) + 1 for rank in range(1, number_of + 1)]
    largest = reach if full else min(reach, max(-(-total // number_of), total * loads[0] // sum(loads)))
    least = 1 if total - largest >= number_of - 1 else 0
    holding, surplus = [largest] + [least] * (number_of - 1), total - largest - least * (number_of - 1)
    while surplus > 0:
        candidates = [i for i in range(1, number_of) if holding[i] < largest] or [i for i in range(1, number_of) if holding[i] < reach]
        pool, remaining = sum([loads[i] for i in candidates]), surplus
        for i in candidates:
            extra = min(reach - holding[i], max(1, remaining * loads[i] // pool), surplus)
            holding[i] = holding[i] + extra
            surplus = surplus - extra
    return np.array(holding)


def bell_draw(rng, dims, scale, limit, shards=(), kind=jnp.bfloat16):
    result = scale * jax.random.normal(rng, dims, jnp.float32)
    if shards:
        result = result * steps_of(rng, dims, shards, -0.22, 0.18)
    return jnp.clip(result, -limit, limit).astype(kind)


def setup_inputs(seed: int = 0) -> dict:
    splits = jax.random.split(jax.random.key(seed), 9)
    states = draw_states(jax.random.fold_in(splits[8], 71), 0)
    out_grad = bell_draw(splits[1], (SEQS, DEC_DEV, D), 1.0, 6.0, ((0, 32),))
    doc_keys = draw_doc_keys(jax.random.fold_in(splits[8], 71), 0)
    doc_values = bell_draw(splits[3], (SEQS, DOC_LEN, D), 3.0, 18.0, ((0, 32), (1, 8)))
    norm_gain = jnp.clip(1.0 + 0.1 * jax.random.normal(splits[4], (D,), jnp.float32), 0.5, 1.5)
    expert_ids_keys = jax.random.split(jax.random.fold_in(splits[5], 1), SEQS * DEC_DEV // DEC_DEV)
    expert_ids_turns = jax.random.permutation(jax.random.fold_in(splits[5], 3), SEQS * DEC_DEV // DEC_DEV)
    expert_ids = jax.vmap(lambda own, number: assign_block(jax.random.fold_in(splits[5], 2), own, number, DEC_DEV, EXPERTS, TOP, CAP, 2))(expert_ids_keys, expert_ids_turns).reshape((SEQS, DEC_DEV, TOP))
    gate_values = jnp.clip(0.5 + 2.0 * jax.random.uniform(splits[6], (SEQS, DEC_DEV, TOP), jnp.float32) ** steps_of(splits[6], (SEQS, DEC_DEV, TOP), ((0, 32),), -0.2, 0.2), 0.5, 2.5)
    expert_weights = bell_draw(splits[7], (EXPERTS, EXPERT_FF, 2, D), D ** -0.5, 0.125, ((0, 32), (1, 8)))
    return dict(states=states, out_grad=out_grad, doc_keys=doc_keys, doc_values=doc_values, norm_gain=norm_gain, expert_ids=expert_ids, gate_values=gate_values, expert_weights=expert_weights)


EPSILON = 1e-05

def attend_back(items):
    normed, doc_keys, doc_values, upstream = items
    scale = HEAD ** (-0.5)
    queries = normed.reshape(DEC_DEV, HEADS, HEAD).astype(jnp.float32)
    key_heads = doc_keys.reshape(DOC_LEN, HEADS, HEAD).astype(jnp.float32)
    value_heads = doc_values.reshape(DOC_LEN, HEADS, HEAD).astype(jnp.float32)
    grad_heads = upstream.reshape(DEC_DEV, HEADS, HEAD).astype(jnp.float32)
    highest = lax.Precision.HIGHEST
    scores = jnp.einsum('qhd,khd->hqk', queries, key_heads, precision=highest) * scale
    peak = lax.optimization_barrier(jnp.max(scores, axis=-1, keepdims=True))
    weights = jnp.exp(scores - peak)
    probs = weights / lax.optimization_barrier(jnp.sum(weights, axis=-1, keepdims=True))
    slopes = jnp.einsum('qhd,khd->hqk', grad_heads, value_heads, precision=highest)
    delta = lax.optimization_barrier(jnp.sum(probs * slopes, axis=-1, keepdims=True))
    score_grad = (probs * (slopes - delta)).astype(jnp.bfloat16).astype(jnp.float32)
    probs_low = probs.astype(jnp.bfloat16).astype(jnp.float32)
    values_grad = jnp.einsum('hqk,qhd->khd', probs_low, grad_heads, precision=highest)
    keys_grad = jnp.einsum('hqk,qhd->khd', score_grad, queries, precision=highest) * scale
    query_grad = jnp.einsum('hqk,khd->qhd', score_grad, key_heads, precision=highest) * scale
    return (query_grad.reshape(DEC_DEV, D), keys_grad.reshape(DOC_LEN, D).astype(jnp.bfloat16), values_grad.reshape(DOC_LEN, D).astype(jnp.bfloat16))

def expert_back(normed, out_grad, expert_ids, gate_values, expert_weights):
    assigned = SEQS * DEC_DEV * TOP
    slot_total = SEQS * CAP
    group_width = EXPERT_FF // N_CTX
    flat_ids = expert_ids.reshape(assigned)
    gate_flat = gate_values.reshape(assigned).astype(jnp.float32)
    rows_all = normed.reshape(SEQS * DEC_DEV, D)
    grads_all = out_grad.reshape(SEQS * DEC_DEV, D)

    def step(carry, item):
        index, weights = item
        found = jnp.nonzero(flat_ids == index, size=slot_total, fill_value=assigned)[0].astype(jnp.int32)
        filled = found < assigned
        safe_index = jnp.minimum(found, assigned - 1)
        source = safe_index // TOP
        rows = jnp.where(filled[:, None], rows_all[source], jnp.zeros((), rows_all.dtype))
        gates = jnp.where(filled, gate_flat[safe_index], 0.0)
        douts = (gates[:, None] * grads_all[source].astype(jnp.float32)).astype(jnp.bfloat16)
        w_in = weights[:, 0, :]
        w_out = weights[:, 1, :]
        pre = jnp.dot(rows, w_in.T, preferred_element_type=jnp.float32)
        act, pull = jax.vjp(jax.nn.gelu, pre)
        act_low = act.astype(jnp.bfloat16)
        act_grad = jnp.dot(douts, w_out.T, preferred_element_type=jnp.float32)
        pre_grad = pull(act_grad)[0].astype(jnp.bfloat16)
        grad_in = jnp.dot(pre_grad.T, rows, preferred_element_type=jnp.float32)
        grad_out = jnp.dot(act_low.T, douts, preferred_element_type=jnp.float32)
        stacked = jnp.stack([grad_in, grad_out], axis=1).astype(jnp.bfloat16)
        pieces = jnp.einsum('sch,chd->scd', pre_grad.reshape(slot_total, N_CTX, group_width).astype(jnp.float32), w_in.reshape(N_CTX, group_width, D).astype(jnp.float32), precision=lax.Precision.HIGHEST)
        summed = lax.optimization_barrier(jnp.sum(pieces.astype(jnp.bfloat16).astype(jnp.float32), axis=1))
        carry = carry.at[source].add(jnp.where(filled[:, None], summed, 0.0))
        return (carry, stacked)
    start = jnp.zeros((SEQS * DEC_DEV, D), jnp.float32)
    moe_grad, weights_grad = lax.scan(step, start, (jnp.arange(EXPERTS, dtype=jnp.int32), expert_weights))
    return (moe_grad, weights_grad)

def reference(states, out_grad, doc_keys, doc_values, norm_gain, expert_ids, gate_values, expert_weights):
    inputs = states.astype(jnp.float32)
    inverse = lax.rsqrt(lax.optimization_barrier(jnp.mean(inputs * inputs, axis=-1, keepdims=True)) + EPSILON)
    unit = inputs * inverse
    normed = (unit * norm_gain).astype(jnp.bfloat16)
    query_grad, keys_grad, values_grad = lax.map(attend_back, (normed, doc_keys, doc_values, out_grad))
    moe_grad, weights_grad = expert_back(normed, out_grad, expert_ids, gate_values, expert_weights)
    total_grad = query_grad + moe_grad.reshape(SEQS, DEC_DEV, D)
    scaled = total_grad * norm_gain
    states_grad = out_grad.astype(jnp.float32) + inverse * (scaled - unit * lax.optimization_barrier(jnp.mean(scaled * unit, axis=-1, keepdims=True)))
    return (states_grad.astype(jnp.bfloat16), keys_grad, values_grad, weights_grad)
```

```python
import jax
import jax.numpy as jnp
from jax import lax
from jax.sharding import Mesh
from jax.sharding import PartitionSpec as P

HEADS = 20
HEAD = 128
TOP = 2
CTX = ("ctx_0", "ctx_1")


EPSILON = 1e-05


def all_in_one(array, axis):
    leaves = jax.tree.leaves(array)
    order = sorted(range(len(leaves)), key=lambda k: -leaves[k].size)
    width = (1, *leaves[order[0]].shape)[-1]
    lines = [
        jnp.pad(leaves[k].reshape(-1), (0, -leaves[k].size % width)).reshape(-1, width)
        for k in order
    ]
    both, at, found = (lax.all_gather(jnp.concatenate(lines), axis), 0, {})
    for k, line in zip(order, lines):
        share = both[:, at : at + len(line)].reshape(len(both), -1)
        found[k] = share[:, : leaves[k].size].reshape(-1, *leaves[k].shape)
        at += len(line)
    numbers = iter(range(len(leaves)))
    return jax.tree.map(lambda _: found[next(numbers)], array)


def joined_all(array, axes, combine):
    for axis in axes:
        pieces = all_in_one(array, axis)
        array = jax.tree.map(lambda part: part[0], pieces)
        for k in range(1, lax.axis_size(axis)):
            array = combine(array, jax.tree.map(lambda part: part[k], pieces))
    return array


def sent_together(arrays, axis, split_dim, concat_dim, along):
    both = jnp.concatenate(arrays, axis=along)
    filled, at, outs = (
        lax.all_to_all(both, axis, split_axis=split_dim, concat_axis=concat_dim, tiled=True),
        0,
        [],
    )
    for a in arrays:
        outs.append(lax.slice_in_dim(filled, at, at + a.shape[along], axis=along))
        at += a.shape[along]
    return tuple(outs)


def side_by_side(arrays, axis, dim, along):
    ends, at = ([], 0)
    for a in arrays[:-1]:
        at += a.shape[along]
        ends.append(at)
    both = jnp.concatenate(arrays, axis=along)
    return tuple(jnp.split(lax.all_gather(both, axis, axis=dim, tiled=True), ends, axis=along))


def total_of_pieces(array, axis):
    return lax.all_gather(array, axis).astype(jnp.float32).sum(0)


def combine_scores(one_side, other_side):
    top_score = jnp.maximum(one_side[0], other_side[0])
    factor_one = jnp.exp(one_side[0] - top_score)
    factor_two = jnp.exp(other_side[0] - top_score)
    summed = one_side[1] * factor_one + other_side[1] * factor_two
    weighted = one_side[2] * factor_one + other_side[2] * factor_two
    return (top_score, summed, weighted)


def on_device(
    states, out_grad, doc_keys, doc_values, norm_gain, expert_ids, gate_values, expert_weights
):
    tokens = states.shape[1]
    model_width = states.shape[2]
    key_count = doc_keys.shape[1]
    scale = HEAD ** (-0.5)
    inputs = states[0].astype(jnp.float32)
    inverse = lax.rsqrt(jnp.mean(inputs * inputs, axis=-1, keepdims=True) + EPSILON)
    unit = inputs * inverse
    normed = (unit * norm_gain).astype(jnp.bfloat16)
    upstream = out_grad[0]
    queries = normed.reshape(tokens, HEADS, HEAD)
    key_heads = doc_keys[0].reshape(key_count, HEADS, HEAD)
    value_heads = doc_values[0].reshape(key_count, HEADS, HEAD)
    grad_heads = upstream.reshape(tokens, HEADS, HEAD)
    scores = (
        jnp.einsum("qhd,khd->hqk", queries, key_heads, preferred_element_type=jnp.float32) * scale
    )
    local_peak = jnp.max(scores, axis=-1)
    local_weights = jnp.exp(scores - local_peak[..., None])
    local_total = jnp.sum(local_weights, axis=-1)
    slopes = jnp.einsum("qhd,khd->hqk", grad_heads, value_heads, preferred_element_type=jnp.float32)
    local_inner = jnp.sum(local_weights * slopes, axis=-1)
    peak, total, merged = joined_all((local_peak, local_total, local_inner), CTX, combine_scores)
    delta = merged / total
    probs = jnp.exp(scores - peak[..., None]) / total[..., None]
    score_grad = (probs * (slopes - delta[..., None])).astype(jnp.bfloat16)
    probs_low = probs.astype(jnp.bfloat16)
    values_grad = jnp.einsum(
        "hqk,qhd->khd", probs_low, grad_heads, preferred_element_type=jnp.float32
    )
    keys_grad = (
        jnp.einsum("hqk,qhd->khd", score_grad, queries, preferred_element_type=jnp.float32) * scale
    )
    query_grad = (
        jnp.einsum(
            "hqk,khd->qhd", score_grad, key_heads, preferred_element_type=jnp.float32
        ).reshape(tokens, model_width)
        * scale
    )
    ctx_count = lax.axis_size(CTX)
    expert_count = lax.axis_size("exp")
    capacity = ctx_count * (
        (5 * TOP * tokens + 4 * expert_count * ctx_count - 1) // (4 * expert_count * ctx_count)
    )
    assigned = tokens * TOP
    flat_ids = expert_ids[0].reshape(assigned)
    order = jnp.arange(assigned, dtype=jnp.int32)
    same = (flat_ids[:, None] == flat_ids[None, :]) & (order[None, :] < order[:, None])
    slot = jnp.sum(same.astype(jnp.int32), axis=1)
    placed = flat_ids * capacity + slot
    table = (
        jnp.full((expert_count * capacity,), assigned, jnp.int32)
        .at[placed]
        .set(jnp.arange(assigned, dtype=jnp.int32))
    )
    filled = table < assigned
    safe_index = jnp.minimum(table, assigned - 1)
    source = safe_index // TOP
    slot_gate = jnp.where(filled, gate_values[0].reshape(assigned)[safe_index], 0.0)
    send_rows = jnp.where(filled[:, None], normed[source], jnp.zeros((), jnp.bfloat16))
    send_rows = send_rows.reshape(expert_count, capacity, model_width)
    send_grads = (slot_gate[:, None] * upstream[source].astype(jnp.float32)).astype(jnp.bfloat16)
    send_grads = send_grads.reshape(expert_count, capacity, model_width)
    share = capacity // ctx_count
    offset = lax.axis_index(CTX) * share
    piece_rows = lax.dynamic_slice_in_dim(send_rows, offset, share, 1)
    piece_grads = lax.dynamic_slice_in_dim(send_grads, offset, share, 1)
    sent_rows, sent_grads = sent_together((piece_rows, piece_grads), "exp", 0, 0, 1)
    got_rows, got_grads = side_by_side((sent_rows, sent_grads), CTX, 1, 0)
    slot_rows = got_rows.shape[0] * got_rows.shape[1]
    rows = got_rows.reshape(slot_rows, model_width)
    douts = got_grads.reshape(slot_rows, model_width)
    w_in = expert_weights[0, :, 0, :]
    w_out = expert_weights[0, :, 1, :]
    pre = jnp.einsum("sd,hd->sh", rows, w_in, preferred_element_type=jnp.float32)
    activ, pull = jax.vjp(jax.nn.gelu, pre)
    activ_low = activ.astype(jnp.bfloat16)
    act_grad = jnp.einsum("sd,hd->sh", douts, w_out, preferred_element_type=jnp.float32)
    pre_grad = pull(act_grad)[0].astype(jnp.bfloat16)
    grad_in = jnp.einsum("sh,sd->hd", pre_grad, rows, preferred_element_type=jnp.float32)
    grad_proj = jnp.einsum("sh,sd->hd", activ_low, douts, preferred_element_type=jnp.float32)
    weights_grad = jnp.stack([grad_in, grad_proj], axis=1).astype(jnp.bfloat16)[None]
    partial_rows = jnp.einsum("sh,hd->sd", pre_grad, w_in, preferred_element_type=jnp.float32)
    partial_rows = partial_rows.astype(jnp.bfloat16).reshape(got_rows.shape)
    returned = lax.all_to_all(partial_rows, "exp", split_axis=0, concat_axis=0, tiled=True)
    picked_rows = returned.reshape(expert_count * capacity, model_width)[placed]
    moe_part = jnp.sum(picked_rows.astype(jnp.float32).reshape(tokens, TOP, model_width), axis=1)
    total_grad = total_of_pieces((query_grad + moe_part).astype(jnp.bfloat16), CTX).astype(
        jnp.float32
    )
    scaled = total_grad * norm_gain
    states_grad = upstream.astype(jnp.float32) + inverse * (
        scaled - unit * jnp.mean(scaled * unit, axis=-1, keepdims=True)
    )
    return (
        states_grad.astype(jnp.bfloat16)[None],
        keys_grad.reshape(key_count, model_width).astype(jnp.bfloat16)[None],
        values_grad.reshape(key_count, model_width).astype(jnp.bfloat16)[None],
        weights_grad,
    )


def solution(mesh):
    finer = Mesh(mesh.devices.reshape(4, 2, mesh.shape["exp"]), ("ctx_0", "ctx_1", "exp"))
    return jax.shard_map(
        on_device,
        mesh=finer,
        in_specs=(
            P("exp", None, None),
            P("exp", None, None),
            P("exp", CTX, None),
            P("exp", CTX, None),
            P(),
            P("exp", None, None),
            P("exp", None, None),
            P("exp", CTX, None, None),
        ),
        out_specs=(
            P("exp", None, None),
            P("exp", CTX, None),
            P("exp", CTX, None),
            P("exp", CTX, None, None),
        ),
        check_vma=False,
    )
```

```python
import math

import jax
import jax.numpy as jnp
from jax import lax
from jax.experimental import pallas as pl
from jax.experimental.pallas import tpu as pltpu
from jax.sharding import Mesh
from jax.sharding import PartitionSpec as P

HEADS = 20
HEAD = 128
D = 2560
HALF = 1280
TOKENS = 128
KEYS = 128
UNITS = 256
EXPERTS = 32
CTX_COUNT = 8
ROWS = 256
SLOTS = 512
CHUNK = 640
CTX = ("ctx_0", "ctx_1")
EPSILON = 1e-05
SCALE = HEAD**-0.5
BF16 = jnp.bfloat16
F32 = jnp.float32
VMEM_LIMIT = 56 * 2**20

VMEM = pl.BlockSpec(memory_space=pltpu.VMEM)
SMEM = pl.BlockSpec(memory_space=pltpu.SMEM)


def call(kernel, ins, outs, scratch=(), flops=0, moved=0):
    return pl.pallas_call(
        kernel,
        in_specs=ins,
        out_specs=[VMEM] * len(outs),
        out_shape=outs,
        scratch_shapes=list(scratch),
        compiler_params=pltpu.CompilerParams(vmem_limit_bytes=VMEM_LIMIT),
        cost_estimate=pl.CostEstimate(flops=flops, bytes_accessed=moved, transcendentals=0),
    )


def shape(dims, dtype=BF16):
    return jax.ShapeDtypeStruct(dims, dtype)


def dot(a, b, dims=((1,), (0,))):
    return lax.dot_general(a, b, (dims, ((), ())), preferred_element_type=F32)


def iota(dims, axis):
    return lax.broadcasted_iota(jnp.int32, dims, axis)


def one(mask):
    return jnp.where(mask, 1.0, 0.0).astype(BF16)


def route_kernel(c_ref, states, grads, gain, ids, gates, normed_out, send, even, odd):
    c = c_ref[0]
    x = states[...].astype(F32)
    inverse = lax.rsqrt(jnp.mean(x * x, axis=-1, keepdims=True) + EPSILON)
    normed_out[...] = (x * inverse * gain[...]).astype(BF16)
    expert = iota((ROWS, TOKENS), 0) // 8
    i = iota((ROWS, TOKENS), 0) % 8
    first = ids[0:1, :] == expert
    second = ids[1:2, :] == expert
    named = first | second
    before = one(iota((TOKENS, TOKENS), 0) < iota((TOKENS, TOKENS), 1))
    slot = dot(one(named), before).astype(jnp.int32)
    slot = jnp.where(named, slot, -1)
    even[...] = one(slot == 2 * i)
    odd[...] = one(slot == 2 * i + 1)
    mine = slot == 2 * c + i % 2
    gate = jnp.where(first, gates[0:1, :], 0.0) + jnp.where(second, gates[1:2, :], 0.0)
    gate = jnp.sum(jnp.where(mine, gate, 0.0), axis=1, keepdims=True)
    low = i < 4
    is_row = (i // 2) % 2 == 0
    row_low = one(mine & low & is_row)
    row_high = one(mine & (~low) & is_row)
    grad_low = one(mine & low & (~is_row))
    grad_high = one(mine & (~low) & (~is_row))
    rows = dot(row_low, normed_out[:, :HALF]) + dot(row_high, normed_out[:, HALF:])
    douts = dot(grad_low, grads[:, :HALF]) + dot(grad_high, grads[:, HALF:])
    send[...] = (rows + gate * douts).astype(BF16)


def scores_kernel(normed, grads, keys, values, weights_out, slopes_out, stats):
    for h in range(HEADS):
        at = slice(h * HEAD, (h + 1) * HEAD)
        s = dot(keys[:, at], normed[:, at], ((1,), (1,))) * SCALE
        peak = jnp.max(s, axis=0, keepdims=True)
        w = jnp.exp(s - peak)
        slopes = dot(values[:, at], grads[:, at], ((1,), (1,)))
        weights_out[h] = w
        slopes_out[h] = slopes
        stats[h : h + 1, :] = peak
        stats[24 + h : 25 + h, :] = jnp.sum(w, axis=0, keepdims=True)
        stats[48 + h : 49 + h, :] = jnp.sum(w * slopes, axis=0, keepdims=True)
    for part in range(3):
        at = 24 * part + HEADS
        stats[at : at + 4, :] = jnp.zeros((4, TOKENS), F32)


def merged(stats):
    peak = stats[0][:24]
    for one_side in stats[1:]:
        peak = jnp.maximum(peak, one_side[:24])
    total = inner = 0.0
    for one_side in stats:
        factor = jnp.exp(one_side[:24] - peak)
        total = total + one_side[24:48] * factor
        inner = inner + one_side[48:] * factor
    return jnp.concatenate([peak, total, inner], axis=0)


def pack(out, rows, left, right, tail_left, tail_right):
    lane = iota(tail_left(0).shape, 1)
    for f in range(CTX_COUNT):
        out[f, rows, 0:256] = left(f).astype(BF16)
        out[f, rows, 256:512] = right(f).astype(BF16)
    for g in range(CTX_COUNT // 2):
        a, b = tail_left(g), tail_right(g)
        out[2 * g, rows, 512:640] = jnp.where(lane < 64, a, pltpu.roll(b, 64, 1)).astype(BF16)
        out[2 * g + 1, rows, 512:640] = jnp.where(lane < 64, pltpu.roll(a, 64, 1), b).astype(BF16)


def score_grad_kernel(
    normed, grads, keys, weights, slopes, local, near, far, keys_grad, values_grad, query_pack, query
):
    peak = jnp.maximum(near[0:24, :], far[0:24, :])
    near_factor = jnp.exp(near[0:24, :] - peak)
    far_factor = jnp.exp(far[0:24, :] - peak)
    total = near[24:48, :] * near_factor + far[24:48, :] * far_factor
    inner = near[48:72, :] * near_factor + far[48:72, :] * far_factor
    total = jnp.where(iota((24, TOKENS), 0) < HEADS, total, 1.0)
    factor = jnp.exp(local[0:24, :] - peak) / total
    delta = inner / total
    for h in range(HEADS):
        at = slice(h * HEAD, (h + 1) * HEAD)
        probs = weights[h] * factor[h : h + 1, :]
        score_grad = (probs * (slopes[h] - delta[h : h + 1, :])).astype(BF16)
        values_grad[:, at] = dot(probs.astype(BF16), grads[:, at]).astype(BF16)
        keys_grad[:, at] = (dot(score_grad, normed[:, at]) * SCALE).astype(BF16)
        query[:, at] = dot(score_grad, keys[:, at], ((0,), (0,))) * SCALE
    pack(
        query_pack,
        slice(0, 64),
        lambda f: query[0:64, 256 * f : 256 * f + 256],
        lambda f: query[64:128, 256 * f : 256 * f + 256],
        lambda g: query[0:64, 2048 + 128 * g : 2176 + 128 * g],
        lambda g: query[64:128, 2048 + 128 * g : 2176 + 128 * g],
    )


def expert_kernel(at_ref, *refs):
    shards, (w_in, w_out, query_pack), (sums, rows, douts, act, pre_grad) = refs[:10], refs[10:13], refs[13:]
    to, source = iota((ROWS, ROWS), 0), iota((ROWS, ROWS), 1)
    order = one(source == 8 * (to % 32) + to // 32)
    whole, pieces = shards[:6], shards[6:]
    blocks = [lambda s=s: s[...] for s in whole]
    blocks += [
        lambda k=k: jnp.concatenate([pieces[k][...], pieces[k + 1][...]], axis=0) for k in (0, 2)
    ]
    for k, block in enumerate(blocks):
        c = at_ref[k]
        sorted_rows = dot(order, block()).astype(BF16)
        for q in range(2):
            where = pl.ds(pl.multiple_of(256 * q + 32 * c, 32), 32)
            for half in range(2):
                lanes = slice(HALF * half, HALF * half + HALF)
                first = 128 * half + 32 * q
                rows[where, lanes] = sorted_rows[first : first + 32, :]
                douts[where, lanes] = sorted_rows[first + 64 : first + 96, :]
    v = dot(rows[...], w_in[...], ((1,), (1,)))
    act_grad = dot(douts[...], w_out[...], ((1,), (1,)))
    root = math.sqrt(2 / math.pi)
    square = v * v
    t = jnp.tanh(root * (v + 0.044715 * (square * v)))
    act[...] = (0.5 * v * (1.0 + t)).astype(BF16)
    slope = 0.5 * (1.0 + t) + 0.5 * v * (1.0 - t * t) * (root * (1.0 + 3 * 0.044715 * square))
    pre_grad[...] = (act_grad * slope).astype(BF16)
    tails = dot(pre_grad[...], w_in[:, 2048:2560])
    chunks = [dot(pre_grad[...], w_in[:, 256 * f : 256 * f + 256]) for f in range(CTX_COUNT)]
    pack(
        sums,
        slice(0, 256),
        lambda f: chunks[f][0:256],
        lambda f: chunks[f][256:512],
        lambda g: tails[0:256, 128 * g : 128 * g + 128],
        lambda g: tails[256:512, 128 * g : 128 * g + 128],
    )
    sums[:, 256:320, :] = query_pack[...]


def weights_kernel(rows, douts, act, pre_grad, grad_in, grad_out):
    grad_in[...] = dot(pre_grad[...], rows[...], ((0,), (0,))).astype(BF16)
    grad_out[...] = dot(act[...], douts[...], ((0,), (0,))).astype(BF16)


def total_kernel(parts, back, query):
    total = parts[0].astype(F32)
    for k in range(1, CTX_COUNT):
        total = total + parts[k].astype(F32)
    to, source = iota((ROWS, ROWS), 0), iota((ROWS, ROWS), 1)
    order = one(source == 32 * (to % 8) + to // 8)
    back[...] = dot(order, total[0:256].astype(BF16)).astype(BF16)
    query[...] = total[256:320]


def tokens_kernel(returned, even, odd, query, out):
    a = dot(even[...], returned[...], ((0,), (0,)))
    b = dot(odd[...], returned[...], ((0,), (0,)))
    wide = a[:, 0:256] + b[:, 256:512]
    tail = a[:, 512:640] + pltpu.roll(b[:, 512:640], 64, 1)
    lane = iota((64, 128), 1)
    tail = jnp.where(lane < 64, tail[0:64], pltpu.roll(tail[64:128], 64, 1))
    out[:, 0:256] = (wide[0:64] + query[:, 0:256]).astype(BF16)
    out[:, 256:512] = (wide[64:128] + query[:, 256:512]).astype(BF16)
    out[:, 512:640] = (tail + query[:, 512:640]).astype(BF16)


def norm_grad_kernel(packs, states, grads, gain, out, total):
    for f in range(CTX_COUNT):
        at = slice(256 * f, 256 * f + 256)
        total[0:64, at] = packs[f, :, 0:256].astype(F32)
        total[64:128, at] = packs[f, :, 256:512].astype(F32)
    lane = iota((64, 128), 1)
    for g in range(CTX_COUNT // 2):
        at = slice(2048 + 128 * g, 2176 + 128 * g)
        a = packs[2 * g, :, 512:640].astype(F32)
        b = packs[2 * g + 1, :, 512:640].astype(F32)
        total[0:64, at] = jnp.where(lane < 64, a, pltpu.roll(b, 64, 1))
        total[64:128, at] = jnp.where(lane < 64, pltpu.roll(a, 64, 1), b)
    x = states[...].astype(F32)
    inverse = lax.rsqrt(jnp.mean(x * x, axis=-1, keepdims=True) + EPSILON)
    unit = x * inverse
    g = total[...] * gain[...]
    g = g - unit * jnp.mean(g * unit, axis=-1, keepdims=True)
    out[...] = (grads[...].astype(F32) + inverse * g).astype(BF16)


def moved_by(array, axis, step):
    count = lax.axis_size(axis)
    return lax.ppermute(array, axis, [(k, (k + step) % count) for k in range(count)])


def on_device(
    states, out_grad, doc_keys, doc_values, norm_gain, expert_ids, gate_values, expert_weights
):
    states, grads, keys, values = states[0], out_grad[0], doc_keys[0], doc_values[0]
    gain = norm_gain.reshape(1, D)
    y, x = lax.axis_index("ctx_0"), lax.axis_index("ctx_1")
    here = (2 * y + x).astype(jnp.int32)
    normed, send, even, odd = call(
        route_kernel,
        [SMEM] + [VMEM] * 5,
        [shape((TOKENS, D)), shape((ROWS, HALF)), shape((ROWS, TOKENS)), shape((ROWS, TOKENS))],
        flops=2 * 4 * ROWS * TOKENS * HALF,
        moved=3 * 2**20,
    )(here.reshape(1), states, grads, gain, expert_ids[0].T, gate_values[0].T)
    own = lax.all_to_all(
        send.reshape(EXPERTS, 8, HALF), "exp", split_axis=0, concat_axis=0, tiled=True
    ).reshape(ROWS, HALF)

    weights, slopes, stats = call(
        scores_kernel,
        [VMEM] * 4,
        [shape((HEADS, KEYS, TOKENS), F32), shape((HEADS, KEYS, TOKENS), F32), shape((72, TOKENS), F32)],
        flops=2 * 2 * KEYS * TOKENS * D,
        moved=5 * 2**20,
    )(normed, grads, keys, values)
    near = merged([stats] + [moved_by(stats, "ctx_0", k) for k in (1, 2, 3)])
    far = moved_by(near, "ctx_1", 1)
    keys_grad, values_grad, query_pack = call(
        score_grad_kernel,
        [VMEM] * 8,
        [shape((KEYS, D)), shape((KEYS, D)), shape((CTX_COUNT, 64, CHUNK))],
        [pltpu.VMEM((TOKENS, D), F32)],
        flops=3 * 2 * KEYS * TOKENS * D,
        moved=6 * 2**20,
    )(normed, grads, keys, weights, slopes, stats, near, far)

    up, down = moved_by(own, "ctx_0", 1), moved_by(own, "ctx_0", 3)
    partner = moved_by(own, "ctx_1", 1)
    across = [moved_by(up[:128], "ctx_0", 1), moved_by(down[128:], "ctx_0", 3)]
    partner_up, partner_down = moved_by(partner, "ctx_0", 1), moved_by(partner, "ctx_0", 3)
    partner_across = [
        moved_by(partner_up[:128], "ctx_0", 1),
        moved_by(partner_down[128:], "ctx_0", 3),
    ]
    shards = [own, up, down, partner, partner_up, partner_down, *across, *partner_across]
    places = [(0, 0), (-1, 0), (1, 0), (0, 1), (-1, 1), (1, 1), (2, 0), (2, 1)]
    at = jnp.stack([2 * ((y + a + 4) % 4) + (x + b) % 2 for a, b in places]).astype(jnp.int32)
    w_in, w_out = expert_weights[0, :, 0, :], expert_weights[0, :, 1, :]
    sums, rows, douts, act, pre_grad = call(
        expert_kernel,
        [SMEM] + [VMEM] * 13,
        [
            shape((CTX_COUNT, 320, CHUNK)),
            shape((SLOTS, D)),
            shape((SLOTS, D)),
            shape((SLOTS, UNITS)),
            shape((SLOTS, UNITS)),
        ],
        flops=2 * 3 * SLOTS * UNITS * D,
        moved=16 * 2**20,
    )(at, *shards, w_in, w_out, query_pack)
    parts = lax.all_to_all(sums, CTX, split_axis=0, concat_axis=0, tiled=True)
    grad_in, grad_out = call(
        weights_kernel,
        [VMEM] * 4,
        [shape((UNITS, D)), shape((UNITS, D))],
        flops=2 * 2 * SLOTS * UNITS * D,
        moved=8 * 2**20,
    )(rows, douts, act, pre_grad)
    weights_grad = jnp.stack([grad_in, grad_out], axis=1)[None]
    back, query = call(
        total_kernel,
        [VMEM],
        [shape((ROWS, CHUNK)), shape((64, CHUNK), F32)],
        moved=4 * 2**20,
    )(parts)
    returned = lax.all_to_all(
        back.reshape(EXPERTS, 8, CHUNK), "exp", split_axis=0, concat_axis=0, tiled=True
    ).reshape(ROWS, CHUNK)
    [total] = call(tokens_kernel, [VMEM] * 4, [shape((64, CHUNK))], moved=2**20)(
        returned, even, odd, query
    )
    packs = lax.all_gather(lax.all_gather(total, "ctx_1"), "ctx_0").reshape(CTX_COUNT, 64, CHUNK)
    [states_grad] = call(
        norm_grad_kernel,
        [VMEM] * 4,
        [shape((TOKENS, D))],
        [pltpu.VMEM((TOKENS, D), F32)],
        moved=3 * 2**20,
    )(packs, states, grads, gain)
    return states_grad[None], keys_grad[None], values_grad[None], weights_grad


def solution(mesh):
    finer = Mesh(mesh.devices.reshape(4, 2, mesh.shape["exp"]), (*CTX, "exp"))
    return jax.shard_map(
        on_device,
        mesh=finer,
        in_specs=(
            P("exp", None, None),
            P("exp", None, None),
            P("exp", CTX, None),
            P("exp", CTX, None),
            P(),
            P("exp", None, None),
            P("exp", None, None),
            P("exp", CTX, None, None),
        ),
        out_specs=(
            P("exp", None, None),
            P("exp", CTX, None),
            P("exp", CTX, None),
            P("exp", CTX, None, None),
        ),
        check_vma=False,
    )
```

```python
import math

import jax
import jax.numpy as jnp
from jax import lax
from jax.experimental import pallas as pl
from jax.experimental.pallas import tpu as pltpu
from jax.sharding import Mesh
from jax.sharding import PartitionSpec as P

HEADS = 20
HEAD = 128
D = 2560
HALF = 1280
TOKENS = 128
KEYS = 128
UNITS = 256
EXPERTS = 32
CTX_COUNT = 8
ROWS = 256
SLOTS = 512
CHUNK = 640
CTX = ("ctx_0", "ctx_1")
EPSILON = 1e-05
SCALE = HEAD**-0.5
BF16 = jnp.bfloat16
F32 = jnp.float32
VMEM_LIMIT = 40 * 2**20

VMEM = pl.BlockSpec(memory_space=pltpu.VMEM)
SMEM = pl.BlockSpec(memory_space=pltpu.SMEM)
ANY = pl.BlockSpec(memory_space=pl.ANY)


def call(kernel, ins, outs, scratch=(), flops=0, moved=0, places=None):
    return pl.pallas_call(
        kernel,
        in_specs=ins,
        out_specs=places or [VMEM] * len(outs),
        out_shape=outs,
        scratch_shapes=list(scratch),
        compiler_params=pltpu.CompilerParams(vmem_limit_bytes=VMEM_LIMIT),
        cost_estimate=pl.CostEstimate(flops=flops, bytes_accessed=moved, transcendentals=0),
    )


def shape(dims, dtype=BF16):
    return jax.ShapeDtypeStruct(dims, dtype)


def dot(a, b, dims=((1,), (0,))):
    return lax.dot_general(a, b, (dims, ((), ())), preferred_element_type=F32)


def iota(dims, axis):
    return lax.broadcasted_iota(jnp.int32, dims, axis)


def one(mask):
    return jnp.where(mask, 1.0, 0.0).astype(BF16)


def route_kernel(c_ref, states, grads, gain, ids, gates, normed_out, send, even, odd):
    c = c_ref[0]
    x = states[...].astype(F32)
    inverse = lax.rsqrt(jnp.mean(x * x, axis=-1, keepdims=True) + EPSILON)
    normed_out[...] = (x * inverse * gain[...].reshape(1, D)).astype(BF16)
    expert = iota((ROWS, TOKENS), 0) // 8
    i = iota((ROWS, TOKENS), 0) % 8
    first = ids[0:1, :] == expert
    second = ids[1:2, :] == expert
    named = first | second
    before = one(iota((TOKENS, TOKENS), 0) < iota((TOKENS, TOKENS), 1))
    slot = dot(one(named), before).astype(jnp.int32)
    slot = jnp.where(named, slot, -1)
    even[...] = one(slot == 2 * i)
    odd[...] = one(slot == 2 * i + 1)
    mine = slot == 2 * c + i % 2
    gate = jnp.where(first, gates[0:1, :], 0.0) + jnp.where(second, gates[1:2, :], 0.0)
    gate = jnp.sum(jnp.where(mine, gate, 0.0), axis=1, keepdims=True)
    low = i < 4
    is_row = (i // 2) % 2 == 0
    row_low = one(mine & low & is_row)
    row_high = one(mine & (~low) & is_row)
    grad_low = one(mine & low & (~is_row))
    grad_high = one(mine & (~low) & (~is_row))
    rows = dot(row_low, normed_out[:, :HALF]) + dot(row_high, normed_out[:, HALF:])
    douts = dot(grad_low, grads[:, :HALF]) + dot(grad_high, grads[:, HALF:])
    send[...] = (rows + gate * douts).astype(BF16)


def scores_kernel(normed, grads, keys, values, weights_out, slopes_out, stats):
    for h in range(HEADS):
        at = slice(h * HEAD, (h + 1) * HEAD)
        s = dot(keys[:, at], normed[:, at], ((1,), (1,))) * SCALE
        peak = jnp.max(s, axis=0, keepdims=True)
        w = jnp.exp(s - peak)
        slopes = dot(values[:, at], grads[:, at], ((1,), (1,)))
        weights_out[h] = w
        slopes_out[h] = slopes
        stats[h : h + 1, :] = peak
        stats[24 + h : 25 + h, :] = jnp.sum(w, axis=0, keepdims=True)
        stats[48 + h : 49 + h, :] = jnp.sum(w * slopes, axis=0, keepdims=True)
    for part in range(3):
        at = 24 * part + HEADS
        stats[at : at + 4, :] = jnp.zeros((4, TOKENS), F32)


def merged(stats):
    peak = stats[0][:24]
    for one_side in stats[1:]:
        peak = jnp.maximum(peak, one_side[:24])
    total = inner = 0.0
    for one_side in stats:
        factor = jnp.exp(one_side[:24] - peak)
        total = total + one_side[24:48] * factor
        inner = inner + one_side[48:] * factor
    return jnp.concatenate([peak, total, inner], axis=0)


def pack(out, rows, left, right, tail_left, tail_right):
    lane = iota(tail_left(0).shape, 1)
    for f in range(CTX_COUNT):
        out[f, rows, 0:256] = left(f).astype(BF16)
        out[f, rows, 256:512] = right(f).astype(BF16)
    for g in range(CTX_COUNT // 2):
        a, b = tail_left(g), tail_right(g)
        out[2 * g, rows, 512:640] = jnp.where(lane < 64, a, pltpu.roll(b, 64, 1)).astype(BF16)
        out[2 * g + 1, rows, 512:640] = jnp.where(lane < 64, pltpu.roll(a, 64, 1), b).astype(BF16)


def score_grad_kernel(
    normed, grads, keys, weights, slopes, local, near, far, keys_grad, values_grad, query_pack, query
):
    peak = jnp.maximum(near[0:24, :], far[0:24, :])
    near_factor = jnp.exp(near[0:24, :] - peak)
    far_factor = jnp.exp(far[0:24, :] - peak)
    total = near[24:48, :] * near_factor + far[24:48, :] * far_factor
    inner = near[48:72, :] * near_factor + far[48:72, :] * far_factor
    total = jnp.where(iota((24, TOKENS), 0) < HEADS, total, 1.0)
    factor = jnp.exp(local[0:24, :] - peak) / total
    delta = inner / total
    for h in range(HEADS):
        at = slice(h * HEAD, (h + 1) * HEAD)
        probs = weights[h] * factor[h : h + 1, :]
        score_grad = (probs * (slopes[h] - delta[h : h + 1, :])).astype(BF16)
        values_grad[:, at] = dot(probs.astype(BF16), grads[:, at]).astype(BF16)
        keys_grad[:, at] = (dot(score_grad, normed[:, at]) * SCALE).astype(BF16)
        query[:, at] = dot(score_grad, keys[:, at], ((0,), (0,))) * SCALE
    pack(
        query_pack,
        slice(0, 64),
        lambda f: query[0:64, 256 * f : 256 * f + 256],
        lambda f: query[64:128, 256 * f : 256 * f + 256],
        lambda g: query[0:64, 2048 + 128 * g : 2176 + 128 * g],
        lambda g: query[64:128, 2048 + 128 * g : 2176 + 128 * g],
    )


def expert_kernel(at_ref, *refs):
    given, results, held = refs[:13], refs[13:18], refs[18:]
    shards, w_in, w_out = held[:8], held[8], held[9]
    sums, rows, douts, act, pre_grad, arrived, left = held[10:]
    landing = [
        *shards[:6],
        shards[6].at[0:128],
        shards[6].at[128:256],
        shards[7].at[0:128],
        shards[7].at[128:256],
        w_in,
        w_out,
    ]
    loads = [
        pltpu.make_async_copy(given[k], landing[k], arrived.at[k]) for k in range(len(landing))
    ]
    for load in loads:
        load.start()
    stores = [
        pltpu.make_async_copy(given[12], results[0].at[:, 256:320, :], left.at[0]),
        *(
            pltpu.make_async_copy(held[11 + k], results[1 + k], left.at[1 + k])
            for k in range(4)
        ),
        *(
            pltpu.make_async_copy(sums.at[f], results[0].at[f, 0:256, :], left.at[5 + f])
            for f in range(CTX_COUNT)
        ),
    ]
    stores[0].start()
    to, source = iota((ROWS, ROWS), 0), iota((ROWS, ROWS), 1)
    order = one(source == 8 * (to % 32) + to // 32)
    for k, shard in enumerate(shards):
        for load in loads[k : k + 1] if k < 6 else loads[2 * k - 6 : 2 * k - 4]:
            load.wait()
        c = at_ref[k]
        sorted_rows = dot(order, shard[...]).astype(BF16)
        for q in range(2):
            where = pl.ds(pl.multiple_of(256 * q + 32 * c, 32), 32)
            for half in range(2):
                lanes = slice(HALF * half, HALF * half + HALF)
                first = 128 * half + 32 * q
                rows[where, lanes] = sorted_rows[first : first + 32, :]
                douts[where, lanes] = sorted_rows[first + 64 : first + 96, :]
    stores[1].start()
    stores[2].start()
    loads[10].wait()
    v = dot(rows[...], w_in[...], ((1,), (1,)))
    loads[11].wait()
    act_grad = dot(douts[...], w_out[...], ((1,), (1,)))
    root = math.sqrt(2 / math.pi)
    square = v * v
    t = jnp.tanh(root * (v + 0.044715 * (square * v)))
    act[...] = (0.5 * v * (1.0 + t)).astype(BF16)
    slope = 0.5 * (1.0 + t) + 0.5 * v * (1.0 - t * t) * (root * (1.0 + 3 * 0.044715 * square))
    pre_grad[...] = (act_grad * slope).astype(BF16)
    stores[3].start()
    stores[4].start()
    tails = dot(pre_grad[...], w_in[:, 2048:2560])
    lane = iota((256, 128), 1)
    for f in range(CTX_COUNT):
        part = dot(pre_grad[...], w_in[:, 256 * f : 256 * f + 256])
        sums[f, :, 0:256] = part[0:256].astype(BF16)
        sums[f, :, 256:512] = part[256:512].astype(BF16)
        tile = slice(128 * (f // 2), 128 * (f // 2) + 128)
        a, b = tails[0:256, tile], tails[256:512, tile]
        if f % 2 == 0:
            tail = jnp.where(lane < 64, a, pltpu.roll(b, 64, 1))
        else:
            tail = jnp.where(lane < 64, pltpu.roll(a, 64, 1), b)
        sums[f, :, 512:640] = tail.astype(BF16)
        stores[5 + f].start()
    for store in stores:
        store.wait()


def weights_kernel(rows, douts, act, pre_grad, grad_in, grad_out):
    grad_in[...] = dot(pre_grad[...], rows[...], ((0,), (0,))).astype(BF16)
    grad_out[...] = dot(act[...], douts[...], ((0,), (0,))).astype(BF16)


def total_kernel(given, back, query, parts, arrived):
    loads = [
        pltpu.make_async_copy(given.at[k], parts.at[k], arrived.at[k]) for k in range(CTX_COUNT)
    ]
    for load in loads:
        load.start()
    for load in loads[:4]:
        load.wait()
    total = (parts[0].astype(F32) + parts[1].astype(F32)) + (
        parts[2].astype(F32) + parts[3].astype(F32)
    )
    for load in loads[4:]:
        load.wait()
    total = total + (parts[4].astype(F32) + parts[5].astype(F32)) + (
        parts[6].astype(F32) + parts[7].astype(F32)
    )
    to, source = iota((ROWS, ROWS), 0), iota((ROWS, ROWS), 1)
    order = one(source == 32 * (to % 8) + to // 8)
    back[...] = dot(order, total[0:256].astype(BF16)).astype(BF16)
    query[...] = total[256:320]


def tokens_kernel(returned, even, odd, query, out):
    a = dot(even[...], returned[...], ((0,), (0,)))
    b = dot(odd[...], returned[...], ((0,), (0,)))
    wide = a[:, 0:256] + b[:, 256:512]
    tail = a[:, 512:640] + pltpu.roll(b[:, 512:640], 64, 1)
    lane = iota((64, 128), 1)
    tail = jnp.where(lane < 64, tail[0:64], pltpu.roll(tail[64:128], 64, 1))
    out[:, 0:256] = (wide[0:64] + query[:, 0:256]).astype(BF16)
    out[:, 256:512] = (wide[64:128] + query[:, 256:512]).astype(BF16)
    out[:, 512:640] = (tail + query[:, 512:640]).astype(BF16)


def norm_grad_kernel(place, *refs):
    packs, (states, grads, gain, out, total) = refs[:CTX_COUNT], refs[CTX_COUNT:]
    y, column = place[0], place[1]
    lane = iota((64, 128), 1)
    for k in range(4):
        row = (y + k) % 4
        for pack, side in ((packs[2 * k], column), (packs[2 * k + 1], 1 - column)):
            at = pl.ds(pl.multiple_of(256 * (2 * row + side), 256), 256)
            total[0:64, at] = pack[:, 0:256].astype(F32)
            total[64:128, at] = pack[:, 256:512].astype(F32)
        at = pl.ds(pl.multiple_of(2048 + 128 * row, 128), 128)
        near = packs[2 * k][:, 512:640].astype(F32)
        far = packs[2 * k + 1][:, 512:640].astype(F32)
        a, b = jnp.where(column == 0, near, far), jnp.where(column == 0, far, near)
        total[0:64, at] = jnp.where(lane < 64, a, pltpu.roll(b, 64, 1))
        total[64:128, at] = jnp.where(lane < 64, pltpu.roll(a, 64, 1), b)
    x = states[...].astype(F32)
    inverse = lax.rsqrt(jnp.mean(x * x, axis=-1, keepdims=True) + EPSILON)
    unit = x * inverse
    g = total[...] * gain[...].reshape(1, D)
    g = g - unit * jnp.mean(g * unit, axis=-1, keepdims=True)
    out[...] = (grads[...].astype(F32) + inverse * g).astype(BF16)


def moved_by(array, axis, step):
    count = lax.axis_size(axis)
    return lax.ppermute(array, axis, [(k, (k + step) % count) for k in range(count)])


def on_device(
    states, out_grad, doc_keys, doc_values, norm_gain, expert_ids, gate_values, expert_weights
):
    states, grads, keys, values = states[0], out_grad[0], doc_keys[0], doc_values[0]
    y, x = lax.axis_index("ctx_0"), lax.axis_index("ctx_1")
    here = (2 * y + x).astype(jnp.int32)
    normed, send, even, odd = call(
        route_kernel,
        [SMEM] + [VMEM] * 5,
        [shape((TOKENS, D)), shape((ROWS, HALF)), shape((ROWS, TOKENS)), shape((ROWS, TOKENS))],
        flops=2 * 4 * ROWS * TOKENS * HALF,
        moved=3 * 2**20,
    )(here.reshape(1), states, grads, norm_gain, expert_ids[0].T, gate_values[0].T)
    own = lax.all_to_all(
        send.reshape(EXPERTS, 8, HALF), "exp", split_axis=0, concat_axis=0, tiled=True
    ).reshape(ROWS, HALF)

    weights, slopes, stats = call(
        scores_kernel,
        [VMEM] * 4,
        [shape((HEADS, KEYS, TOKENS), F32), shape((HEADS, KEYS, TOKENS), F32), shape((72, TOKENS), F32)],
        flops=2 * 2 * KEYS * TOKENS * D,
        moved=5 * 2**20,
    )(normed, grads, keys, values)
    near = merged([stats] + [moved_by(stats, "ctx_0", k) for k in (1, 2, 3)])
    far = moved_by(near, "ctx_1", 1)
    keys_grad, values_grad, query_pack = call(
        score_grad_kernel,
        [VMEM] * 8,
        [shape((KEYS, D)), shape((KEYS, D)), shape((CTX_COUNT, 64, CHUNK))],
        [pltpu.VMEM((TOKENS, D), F32)],
        flops=3 * 2 * KEYS * TOKENS * D,
        moved=6 * 2**20,
    )(normed, grads, keys, weights, slopes, stats, near, far)

    up, down = moved_by(own, "ctx_0", 1), moved_by(own, "ctx_0", 3)
    partner = moved_by(own, "ctx_1", 1)
    across = [moved_by(up[:128], "ctx_0", 1), moved_by(down[128:], "ctx_0", 3)]
    partner_up, partner_down = moved_by(partner, "ctx_0", 1), moved_by(partner, "ctx_0", 3)
    partner_across = [moved_by(piece, "ctx_1", 1) for piece in across]
    shards = [own, up, down, partner, partner_up, partner_down, *across, *partner_across]
    places = [(0, 0), (-1, 0), (1, 0), (0, 1), (-1, 1), (1, 1), (2, 0), (2, 1)]
    at = jnp.stack([2 * ((y + a + 4) % 4) + (x + b) % 2 for a, b in places]).astype(jnp.int32)
    w_in, w_out = expert_weights[0, :, 0, :], expert_weights[0, :, 1, :]
    sums, rows, douts, act, pre_grad = call(
        expert_kernel,
        [SMEM] + [ANY] * 13,
        [
            shape((CTX_COUNT, 320, CHUNK)),
            shape((SLOTS, D)),
            shape((SLOTS, D)),
            shape((SLOTS, UNITS)),
            shape((SLOTS, UNITS)),
        ],
        [
            *[pltpu.VMEM((ROWS, HALF), BF16)] * 8,
            *[pltpu.VMEM((UNITS, D), BF16)] * 2,
            pltpu.VMEM((CTX_COUNT, ROWS, CHUNK), BF16),
            *[pltpu.VMEM((SLOTS, D), BF16)] * 2,
            *[pltpu.VMEM((SLOTS, UNITS), BF16)] * 2,
            pltpu.SemaphoreType.DMA((12,)),
            pltpu.SemaphoreType.DMA((13,)),
        ],
        places=[ANY] * 5,
        flops=2 * 3 * SLOTS * UNITS * D,
        moved=16 * 2**20,
    )(at, *shards, w_in, w_out, query_pack)
    parts = lax.all_to_all(sums, CTX, split_axis=0, concat_axis=0, tiled=True)
    back, query = call(
        total_kernel,
        [ANY],
        [shape((ROWS, CHUNK)), shape((64, CHUNK), F32)],
        [pltpu.VMEM((CTX_COUNT, 320, CHUNK), BF16), pltpu.SemaphoreType.DMA((CTX_COUNT,))],
        moved=4 * 2**20,
    )(parts)
    rows, back = lax.optimization_barrier((rows, back))
    returned = lax.all_to_all(
        back.reshape(EXPERTS, 8, CHUNK), "exp", split_axis=0, concat_axis=0, tiled=True
    ).reshape(ROWS, CHUNK)
    grad_in, grad_out = call(
        weights_kernel,
        [VMEM] * 4,
        [shape((UNITS, D)), shape((UNITS, D))],
        flops=2 * 2 * SLOTS * UNITS * D,
        moved=8 * 2**20,
    )(rows, douts, act, pre_grad)
    weights_grad = jnp.stack([grad_in, grad_out], axis=1)[None]
    returned, weights_grad = lax.optimization_barrier((returned, weights_grad))
    [total] = call(tokens_kernel, [VMEM] * 4, [shape((64, CHUNK))], moved=2**20)(
        returned, even, odd, query
    )
    packs = [total]
    for k in range(1, CTX_COUNT):
        pairs = [
            (2 * i + j, 2 * ((i - k // 2) % 4) + (j + k) % 2) for i in range(4) for j in range(2)
        ]
        packs.append(lax.ppermute(total, CTX, pairs))
    [states_grad] = call(
        norm_grad_kernel,
        [SMEM] + [VMEM] * 11,
        [shape((TOKENS, D))],
        [pltpu.VMEM((TOKENS, D), F32)],
        moved=3 * 2**20,
    )(jnp.stack([y, x]).astype(jnp.int32), *packs, states, grads, norm_gain)
    return states_grad[None], keys_grad[None], values_grad[None], weights_grad


def solution(mesh):
    finer = Mesh(mesh.devices.reshape(4, 2, mesh.shape["exp"]), (*CTX, "exp"))
    return jax.shard_map(
        on_device,
        mesh=finer,
        in_specs=(
            P("exp", None, None),
            P("exp", None, None),
            P("exp", CTX, None),
            P("exp", CTX, None),
            P(),
            P("exp", None, None),
            P("exp", None, None),
            P("exp", CTX, None, None),
        ),
        out_specs=(
            P("exp", None, None),
            P("exp", CTX, None),
            P("exp", CTX, None),
            P("exp", CTX, None, None),
        ),
        check_vma=False,
    )
```

```python
import math

import jax
import jax.numpy as jnp
from jax import lax
from jax.experimental import pallas as pl
from jax.experimental.pallas import tpu as pltpu
from jax.sharding import Mesh
from jax.sharding import PartitionSpec as P

HEADS = 20
HEAD = 128
D = 2560
HALF = 1280
TOKENS = 128
KEYS = 128
UNITS = 256
EXPERTS = 32
ROWS_OF_CTX = 4
ROWS = 256
SLOTS = 256
CHUNK = 640
CTX = ("ctx_0", "ctx_1")
EPSILON = 1e-05
SCALE = HEAD**-0.5
BF16 = jnp.bfloat16
F32 = jnp.float32
VMEM_LIMIT = 40 * 2**20
VMEM_ALL = 60 * 2**20

VMEM = pl.BlockSpec(memory_space=pltpu.VMEM)
SMEM = pl.BlockSpec(memory_space=pltpu.SMEM)
ANY = pl.BlockSpec(memory_space=pl.ANY)


def call(kernel, ins, outs, scratch=(), flops=0, moved=0, places=None, limit=VMEM_LIMIT):
    return pl.pallas_call(
        kernel,
        in_specs=ins,
        out_specs=places or [VMEM] * len(outs),
        out_shape=outs,
        scratch_shapes=list(scratch),
        compiler_params=pltpu.CompilerParams(vmem_limit_bytes=limit),
        cost_estimate=pl.CostEstimate(flops=flops, bytes_accessed=moved, transcendentals=0),
    )


def shape(dims, dtype=BF16):
    return jax.ShapeDtypeStruct(dims, dtype)


def dot(a, b, dims=((1,), (0,))):
    return lax.dot_general(a, b, (dims, ((), ())), preferred_element_type=F32)


def iota(dims, axis):
    return lax.broadcasted_iota(jnp.int32, dims, axis)


def one(mask):
    return jnp.where(mask, 1.0, 0.0).astype(BF16)


def route_kernel(place, states, grads, gain, ids, gates, normed_out, send, table):
    y, x = place[0], place[1]
    inputs = states[...].astype(F32)
    inverse = lax.rsqrt(jnp.mean(inputs * inputs, axis=-1, keepdims=True) + EPSILON)
    normed_out[...] = (inputs * inverse * gain[...].reshape(1, D)).astype(BF16)
    expert = iota((ROWS, TOKENS), 0) // 8
    i = iota((ROWS, TOKENS), 0) % 8
    first = ids[0:1, :] == expert
    second = ids[1:2, :] == expert
    named = first | second
    before = one(iota((TOKENS, TOKENS), 0) < iota((TOKENS, TOKENS), 1))
    slot = dot(one(named), before).astype(jnp.int32)
    slot = jnp.where(named, slot, -1)
    table[...] = one(slot == 8 * x + i)
    mine = slot == 8 * x + 2 * y + i % 2
    gate = jnp.where(first, gates[0:1, :], 0.0) + jnp.where(second, gates[1:2, :], 0.0)
    gate = jnp.sum(jnp.where(mine, gate, 0.0), axis=1, keepdims=True)
    low = i < 4
    is_row = (i // 2) % 2 == 0
    row_low = one(mine & low & is_row)
    row_high = one(mine & (~low) & is_row)
    grad_low = one(mine & low & (~is_row))
    grad_high = one(mine & (~low) & (~is_row))
    rows = dot(row_low, normed_out[:, :HALF]) + dot(row_high, normed_out[:, HALF:])
    douts = dot(grad_low, grads[:, :HALF]) + dot(grad_high, grads[:, HALF:])
    send[...] = (rows + gate * douts).astype(BF16)


def scores_kernel(normed, grads, keys, values, weights_out, slopes_out, stats):
    for h in range(HEADS):
        at = slice(h * HEAD, (h + 1) * HEAD)
        s = dot(keys[:, at], normed[:, at], ((1,), (1,))) * SCALE
        peak = jnp.max(s, axis=0, keepdims=True)
        w = jnp.exp(s - peak)
        slopes = dot(values[:, at], grads[:, at], ((1,), (1,)))
        weights_out[h] = w
        slopes_out[h] = slopes
        stats[h : h + 1, :] = peak
        stats[24 + h : 25 + h, :] = jnp.sum(w, axis=0, keepdims=True)
        stats[48 + h : 49 + h, :] = jnp.sum(w * slopes, axis=0, keepdims=True)
    for part in range(3):
        at = 24 * part + HEADS
        stats[at : at + 4, :] = jnp.zeros((4, TOKENS), F32)


def merged(stats):
    peak = stats[0][:24]
    for one_side in stats[1:]:
        peak = jnp.maximum(peak, one_side[:24])
    total = inner = 0.0
    for one_side in stats:
        factor = jnp.exp(one_side[:24] - peak)
        total = total + one_side[24:48] * factor
        inner = inner + one_side[48:] * factor
    return jnp.concatenate([peak, total, inner], axis=0)


def score_grad_kernel(
    normed, grads, keys, weights, slopes, local, near, far, keys_grad, values_grad, query
):
    peak = jnp.maximum(near[0:24, :], far[0:24, :])
    near_factor = jnp.exp(near[0:24, :] - peak)
    far_factor = jnp.exp(far[0:24, :] - peak)
    total = near[24:48, :] * near_factor + far[24:48, :] * far_factor
    inner = near[48:72, :] * near_factor + far[48:72, :] * far_factor
    total = jnp.where(iota((24, TOKENS), 0) < HEADS, total, 1.0)
    factor = jnp.exp(local[0:24, :] - peak) / total
    delta = inner / total
    for h in range(HEADS):
        at = slice(h * HEAD, (h + 1) * HEAD)
        probs = weights[h] * factor[h : h + 1, :]
        score_grad = (probs * (slopes[h] - delta[h : h + 1, :])).astype(BF16)
        values_grad[:, at] = dot(probs.astype(BF16), grads[:, at]).astype(BF16)
        keys_grad[:, at] = (dot(score_grad, normed[:, at]) * SCALE).astype(BF16)
        query[h // 5, :, (h % 5) * HEAD : (h % 5 + 1) * HEAD] = (
            dot(score_grad, keys[:, at], ((0,), (0,))) * SCALE
        ).astype(BF16)


def expert_kernel(place, *refs):
    given, results, held = refs[:8], refs[8:14], refs[14:]
    shards, weights, sums = held[:4], held[4:6], held[6:10]
    inputs, spread, arrived, left = held[10:]
    y = place[0]
    landing = [*shards[:3], shards[3].at[0:128], shards[3].at[128:256], *weights]
    loads = [pltpu.make_async_copy(given[k], landing[k], arrived.at[k]) for k in range(7)]
    for load in loads:
        load.start()
    stores = [
        pltpu.make_async_copy(inputs, results[4], left.at[0]),
        pltpu.make_async_copy(spread, results[5], left.at[1]),
        *(
            pltpu.make_async_copy(sums[k], results[k].at[0:SLOTS, :], left.at[2 + k])
            for k in range(4)
        ),
        *(
            pltpu.make_async_copy(
                given[7].at[(y + k) % 4], results[k].at[SLOTS : SLOTS + TOKENS, :], left.at[6 + k]
            )
            for k in range(4)
        ),
    ]
    for store in stores[6:]:
        store.start()
    to, source = iota((ROWS, ROWS), 0), iota((ROWS, ROWS), 1)
    order = one(source == 8 * (to % 32) + to // 32)
    for k, step in enumerate((0, -1, 1, 2)):
        for load in loads[k : k + 1] if k < 3 else loads[3:5]:
            load.wait()
        row = (y + step + 4) % 4
        sorted_rows = dot(order, shards[k][...]).astype(BF16)
        for kind in range(2):
            for half in range(2):
                first = 128 * half + 64 * kind
                where = pl.ds(pl.multiple_of(SLOTS * kind + 64 * row, 64), 64)
                inputs[where, HALF * half : HALF * half + HALF] = sorted_rows[first : first + 64, :]
    stores[0].start()
    root = math.sqrt(2 / math.pi)
    even = iota((SLOTS, 2 * UNITS), 1) % 2 == 0
    for g in range(2):
        loads[5 + g].wait()
        v = dot(inputs[0:SLOTS, :], weights[g][...], ((1,), (1,)))
        act_grad = dot(inputs[SLOTS:, :], weights[g][...], ((1,), (1,)))
        act_grad = pltpu.roll(act_grad, 2 * UNITS - 1, 1)
        square = v * v
        t = jnp.tanh(root * (v + 0.044715 * (square * v)))
        act = 0.5 * v * (1.0 + t)
        slope = 0.5 * (1.0 + t) + 0.5 * v * (1.0 - t * t) * (root * (1.0 + 3 * 0.044715 * square))
        at = slice(2 * UNITS * g, 2 * UNITS * g + 2 * UNITS)
        spread[0:SLOTS, at] = jnp.where(even, act_grad * slope, 0.0).astype(BF16)
        spread[SLOTS:, at] = jnp.where(even, 0.0, pltpu.roll(act, 1, 1)).astype(BF16)
    stores[1].start()
    for k in (1, 3, 2, 0):
        lanes = pl.ds(pl.multiple_of(CHUNK * ((y + k) % 4), 128), CHUNK)
        part = dot(spread[0:SLOTS, 0 : 2 * UNITS], weights[0][:, lanes])
        part = part + dot(spread[0:SLOTS, 2 * UNITS :], weights[1][:, lanes])
        sums[k][...] = part.astype(BF16)
        stores[2 + k].start()
    for store in stores:
        store.wait()


def far_weights_kernel(inputs, spread, out):
    out[...] = dot(spread[:, 2 * UNITS :], inputs[...], ((0,), (0,))).astype(BF16)


def own_weights_kernel(inputs, spread, out):
    out[...] = dot(spread[:, : 2 * UNITS], inputs[...], ((0,), (0,)))


def add_kernel(own, far, out):
    out[...] = (own[...] + far[...].astype(F32)).astype(BF16)


def total_kernel(*refs):
    given, back, query, parts, arrived = refs[:4], *refs[4:]
    loads = [
        pltpu.make_async_copy(given[k], parts.at[k], arrived.at[k]) for k in range(ROWS_OF_CTX)
    ]
    for load in loads:
        load.start()
    for load in loads:
        load.wait()
    total = (parts[0].astype(F32) + parts[1].astype(F32)) + (
        parts[2].astype(F32) + parts[3].astype(F32)
    )
    to, source = iota((ROWS, ROWS), 0), iota((ROWS, ROWS), 1)
    order = one(source == 32 * (to % 8) + to // 8)
    back[...] = dot(order, total[0:SLOTS].astype(BF16)).astype(BF16)
    query[...] = total[SLOTS:]


def tokens_kernel(returned, table, query, out):
    out[...] = (dot(table[...], returned[...], ((0,), (0,))) + query[...]).astype(BF16)


def norm_grad_kernel(place, *refs):
    chunks, (states, grads, gain, out, total) = refs[:ROWS_OF_CTX], refs[ROWS_OF_CTX:]
    for k in range(ROWS_OF_CTX):
        lanes = pl.ds(pl.multiple_of(CHUNK * ((place[0] + k) % 4), 128), CHUNK)
        total[:, lanes] = chunks[k][...].astype(F32)
    inputs = states[...].astype(F32)
    inverse = lax.rsqrt(jnp.mean(inputs * inputs, axis=-1, keepdims=True) + EPSILON)
    unit = inputs * inverse
    g = total[...] * gain[...].reshape(1, D)
    g = g - unit * jnp.mean(g * unit, axis=-1, keepdims=True)
    out[...] = (grads[...].astype(F32) + inverse * g).astype(BF16)


def moved_by(array, axis, step):
    count = lax.axis_size(axis)
    return lax.ppermute(array, axis, [(k, (k + step) % count) for k in range(count)])


def on_device(
    states, out_grad, doc_keys, doc_values, norm_gain, expert_ids, gate_values, expert_weights
):
    states, grads, keys, values = states[0], out_grad[0], doc_keys[0], doc_values[0]
    y, x = lax.axis_index("ctx_0"), lax.axis_index("ctx_1")
    place = jnp.stack([y, x]).astype(jnp.int32)
    far_experts = moved_by(expert_weights, "ctx_1", 1).reshape(2 * UNITS, D)
    own_experts = expert_weights.reshape(2 * UNITS, D)
    normed, send, table = call(
        route_kernel,
        [SMEM] + [VMEM] * 5,
        [shape((TOKENS, D)), shape((ROWS, HALF)), shape((ROWS, TOKENS))],
        flops=2 * 4 * ROWS * TOKENS * HALF,
        moved=3 * 2**20,
        limit=VMEM_ALL,
    )(place, states, grads, norm_gain, expert_ids[0].T, gate_values[0].T)
    own = lax.all_to_all(
        send.reshape(EXPERTS, 8, HALF), "exp", split_axis=0, concat_axis=0, tiled=True
    ).reshape(ROWS, HALF)

    weights, slopes, stats = call(
        scores_kernel,
        [VMEM] * 4,
        [shape((HEADS, KEYS, TOKENS), F32), shape((HEADS, KEYS, TOKENS), F32), shape((72, TOKENS), F32)],
        flops=2 * 2 * KEYS * TOKENS * D,
        moved=5 * 2**20,
    )(normed, grads, keys, values)
    near = merged([stats] + [moved_by(stats, "ctx_0", k) for k in (1, 2, 3)])
    far = moved_by(near, "ctx_1", 1)
    keys_grad, values_grad, query_parts = call(
        score_grad_kernel,
        [VMEM] * 8,
        [shape((KEYS, D)), shape((KEYS, D)), shape((ROWS_OF_CTX, TOKENS, CHUNK))],
        flops=3 * 2 * KEYS * TOKENS * D,
        moved=6 * 2**20,
    )(normed, grads, keys, weights, slopes, stats, near, far)

    up, down = moved_by(own, "ctx_0", 1), moved_by(own, "ctx_0", 3)
    across = [moved_by(up[:128], "ctx_0", 1), moved_by(down[128:], "ctx_0", 3)]
    *sums, inputs, spread = call(
        expert_kernel,
        [SMEM] + [ANY] * 8,
        [
            *[shape((SLOTS + TOKENS, CHUNK))] * 4,
            shape((2 * SLOTS, D)),
            shape((2 * SLOTS, 4 * UNITS)),
        ],
        [
            *[pltpu.VMEM((ROWS, HALF), BF16)] * 4,
            *[pltpu.VMEM((2 * UNITS, D), BF16)] * 2,
            *[pltpu.VMEM((SLOTS, CHUNK), BF16)] * 4,
            pltpu.VMEM((2 * SLOTS, D), BF16),
            pltpu.VMEM((2 * SLOTS, 4 * UNITS), BF16),
            pltpu.SemaphoreType.DMA((7,)),
            pltpu.SemaphoreType.DMA((10,)),
        ],
        places=[ANY] * 6,
        flops=2 * 6 * SLOTS * 2 * UNITS * D,
        moved=16 * 2**20,
    )(place, own, up, down, *across, own_experts, far_experts, query_parts)

    parts = [sums[0]] + [moved_by(sums[k], "ctx_0", k) for k in (1, 2, 3)]
    [far_grad] = call(
        far_weights_kernel,
        [VMEM] * 2,
        [shape((2 * UNITS, D))],
        flops=2 * 2 * SLOTS * 2 * UNITS * D,
        moved=6 * 2**20,
    )(inputs, spread)
    far_grad = moved_by(far_grad, "ctx_1", 1)
    [own_grad] = call(
        own_weights_kernel,
        [VMEM] * 2,
        [shape((2 * UNITS, D), F32)],
        flops=2 * 2 * SLOTS * 2 * UNITS * D,
        moved=8 * 2**20,
    )(inputs, spread)
    back, query = call(
        total_kernel,
        [ANY] * 4,
        [shape((ROWS, CHUNK)), shape((TOKENS, CHUNK), F32)],
        [pltpu.VMEM((ROWS_OF_CTX, SLOTS + TOKENS, CHUNK), BF16), pltpu.SemaphoreType.DMA((4,))],
        moved=3 * 2**20,
    )(*parts)
    returned = lax.all_to_all(
        back.reshape(EXPERTS, 8, CHUNK), "exp", split_axis=0, concat_axis=0, tiled=True
    ).reshape(ROWS, CHUNK)
    [partial] = call(tokens_kernel, [VMEM] * 3, [shape((TOKENS, CHUNK))], moved=2**20)(
        returned, table, query
    )
    partner = moved_by(partial, "ctx_1", 1)
    chunk = (partial.astype(F32) + partner.astype(F32)).astype(BF16)
    chunks = [chunk] + [moved_by(chunk, "ctx_0", 4 - k) for k in (1, 2, 3)]
    [states_grad] = call(
        norm_grad_kernel,
        [SMEM] + [VMEM] * 7,
        [shape((TOKENS, D))],
        [pltpu.VMEM((TOKENS, D), F32)],
        moved=3 * 2**20,
    )(place, *chunks, states, grads, norm_gain)
    [weights_grad] = call(add_kernel, [VMEM] * 2, [shape((2 * UNITS, D))], moved=10 * 2**20)(
        own_grad, far_grad
    )
    weights_grad = weights_grad.reshape(1, UNITS, 2, D)
    return states_grad[None], keys_grad[None], values_grad[None], weights_grad


def solution(mesh):
    finer = Mesh(mesh.devices.reshape(4, 2, mesh.shape["exp"]), (*CTX, "exp"))
    return jax.shard_map(
        on_device,
        mesh=finer,
        in_specs=(
            P("exp", None, None),
            P("exp", None, None),
            P("exp", CTX, None),
            P("exp", CTX, None),
            P(),
            P("exp", None, None),
            P("exp", None, None),
            P("exp", CTX, None, None),
        ),
        out_specs=(
            P("exp", None, None),
            P("exp", CTX, None),
            P("exp", CTX, None),
            P("exp", CTX, None, None),
        ),
        check_vma=False,
    )
```

```python
import math

import jax
import jax.numpy as jnp
from jax import lax
from jax.experimental import pallas as pl
from jax.experimental.pallas import tpu as pltpu
from jax.sharding import Mesh
from jax.sharding import PartitionSpec as P

HEADS = 20
HEAD = 128
D = 2560
HALF = 1280
TOKENS = 128
KEYS = 128
UNITS = 256
EXPERTS = 32
CTX_COUNT = 8
ROWS = 256
SLOTS = 256
CHUNK = 640
CTX = ("ctx_0", "ctx_1")
EPSILON = 1e-05
SCALE = HEAD**-0.5
BF16 = jnp.bfloat16
F32 = jnp.float32
VMEM_LIMIT = 24 * 2**20
VMEM_ALL = 60 * 2**20

VMEM = pl.BlockSpec(memory_space=pltpu.VMEM)
SMEM = pl.BlockSpec(memory_space=pltpu.SMEM)


def call(kernel, ins, outs, scratch=(), flops=0, moved=0, limit=VMEM_LIMIT):
    return pl.pallas_call(
        kernel,
        in_specs=ins,
        out_specs=[VMEM] * len(outs),
        out_shape=outs,
        scratch_shapes=list(scratch),
        compiler_params=pltpu.CompilerParams(vmem_limit_bytes=limit),
        cost_estimate=pl.CostEstimate(flops=flops, bytes_accessed=moved, transcendentals=0),
    )


def shape(dims, dtype=BF16):
    return jax.ShapeDtypeStruct(dims, dtype)


def dot(a, b, dims=((1,), (0,))):
    return lax.dot_general(a, b, (dims, ((), ())), preferred_element_type=F32)


def iota(dims, axis):
    return lax.broadcasted_iota(jnp.int32, dims, axis)


def one(mask):
    return jnp.where(mask, 1.0, 0.0).astype(BF16)


def route_kernel(c_ref, states, grads, gain, ids, gates, normed_out, send, even, odd):
    c = c_ref[0]
    x = states[...].astype(F32)
    inverse = lax.rsqrt(jnp.mean(x * x, axis=-1, keepdims=True) + EPSILON)
    normed_out[...] = (x * inverse * gain[...].reshape(1, D)).astype(BF16)
    expert = iota((ROWS, TOKENS), 0) // 8
    i = iota((ROWS, TOKENS), 0) % 8
    first = ids[0:1, :] == expert
    second = ids[1:2, :] == expert
    named = first | second
    before = one(iota((TOKENS, TOKENS), 0) < iota((TOKENS, TOKENS), 1))
    slot = dot(one(named), before).astype(jnp.int32)
    slot = jnp.where(named, slot, -1)
    even[...] = one(slot == 2 * i)
    odd[...] = one(slot == 2 * i + 1)
    mine = slot == 2 * c + i % 2
    gate = jnp.where(first, gates[0:1, :], 0.0) + jnp.where(second, gates[1:2, :], 0.0)
    gate = jnp.sum(jnp.where(mine, gate, 0.0), axis=1, keepdims=True)
    low = i < 4
    is_row = (i // 2) % 2 == 0
    row_low = one(mine & low & is_row)
    row_high = one(mine & (~low) & is_row)
    grad_low = one(mine & low & (~is_row))
    grad_high = one(mine & (~low) & (~is_row))
    rows = dot(row_low, normed_out[:, :HALF]) + dot(row_high, normed_out[:, HALF:])
    douts = dot(grad_low, grads[:, :HALF]) + dot(grad_high, grads[:, HALF:])
    send[...] = (rows + gate * douts).astype(BF16)


def scores_kernel(normed, grads, keys, values, weights_out, slopes_out, stats):
    for h in range(HEADS):
        at = slice(h * HEAD, (h + 1) * HEAD)
        s = dot(keys[:, at], normed[:, at], ((1,), (1,))) * SCALE
        peak = jnp.max(s, axis=0, keepdims=True)
        w = jnp.exp(s - peak)
        slopes = dot(values[:, at], grads[:, at], ((1,), (1,)))
        weights_out[h] = w
        slopes_out[h] = slopes
        stats[h : h + 1, :] = peak
        stats[24 + h : 25 + h, :] = jnp.sum(w, axis=0, keepdims=True)
        stats[48 + h : 49 + h, :] = jnp.sum(w * slopes, axis=0, keepdims=True)
    for part in range(3):
        at = 24 * part + HEADS
        stats[at : at + 4, :] = jnp.zeros((4, TOKENS), F32)


def merged(stats):
    peak = stats[0][:24]
    for one_side in stats[1:]:
        peak = jnp.maximum(peak, one_side[:24])
    total = inner = 0.0
    for one_side in stats:
        factor = jnp.exp(one_side[:24] - peak)
        total = total + one_side[24:48] * factor
        inner = inner + one_side[48:] * factor
    return jnp.concatenate([peak, total, inner], axis=0)


def pack(out, rows, left, right, tail_left, tail_right):
    lane = iota(tail_left(0).shape, 1)
    for f in range(CTX_COUNT):
        out[f, rows, 0:256] = left(f).astype(BF16)
        out[f, rows, 256:512] = right(f).astype(BF16)
    for g in range(CTX_COUNT // 2):
        a, b = tail_left(g), tail_right(g)
        out[2 * g, rows, 512:640] = jnp.where(lane < 64, a, pltpu.roll(b, 64, 1)).astype(BF16)
        out[2 * g + 1, rows, 512:640] = jnp.where(lane < 64, pltpu.roll(a, 64, 1), b).astype(BF16)


def score_grad_kernel(
    normed, grads, keys, weights, slopes, local, near, far, keys_grad, values_grad, query_pack, query
):
    peak = jnp.maximum(near[0:24, :], far[0:24, :])
    near_factor = jnp.exp(near[0:24, :] - peak)
    far_factor = jnp.exp(far[0:24, :] - peak)
    total = near[24:48, :] * near_factor + far[24:48, :] * far_factor
    inner = near[48:72, :] * near_factor + far[48:72, :] * far_factor
    total = jnp.where(iota((24, TOKENS), 0) < HEADS, total, 1.0)
    factor = jnp.exp(local[0:24, :] - peak) / total
    delta = inner / total
    for h in range(HEADS):
        at = slice(h * HEAD, (h + 1) * HEAD)
        probs = weights[h] * factor[h : h + 1, :]
        score_grad = (probs * (slopes[h] - delta[h : h + 1, :])).astype(BF16)
        values_grad[:, at] = dot(probs.astype(BF16), grads[:, at]).astype(BF16)
        keys_grad[:, at] = (dot(score_grad, normed[:, at]) * SCALE).astype(BF16)
        query[:, at] = dot(score_grad, keys[:, at], ((0,), (0,))) * SCALE
    pack(
        query_pack,
        slice(0, 64),
        lambda f: query[0:64, 256 * f : 256 * f + 256],
        lambda f: query[64:128, 256 * f : 256 * f + 256],
        lambda g: query[0:64, 2048 + 128 * g : 2176 + 128 * g],
        lambda g: query[64:128, 2048 + 128 * g : 2176 + 128 * g],
    )


def experts_of(blocks, w_in, w_out, rows, douts, act, pre_grad, put):
    to, source = iota((ROWS, ROWS), 0), iota((ROWS, ROWS), 1)
    order = one(source == 8 * (to % 32) + to // 32)
    for k, block in enumerate(blocks):
        sorted_rows = dot(order, block()).astype(BF16)
        for q in range(2):
            where = slice(128 * q + 32 * k, 128 * q + 32 * k + 32)
            for half in range(2):
                lanes = slice(HALF * half, HALF * half + HALF)
                first = 128 * half + 32 * q
                rows[where, lanes] = sorted_rows[first : first + 32, :]
                douts[where, lanes] = sorted_rows[first + 64 : first + 96, :]
    v = dot(rows[...], w_in[...], ((1,), (1,)))
    act_grad = dot(douts[...], w_out[...], ((1,), (1,)))
    root = math.sqrt(2 / math.pi)
    square = v * v
    t = jnp.tanh(root * (v + 0.044715 * (square * v)))
    act[...] = (0.5 * v * (1.0 + t)).astype(BF16)
    slope = 0.5 * (1.0 + t) + 0.5 * v * (1.0 - t * t) * (root * (1.0 + 3 * 0.044715 * square))
    pre_grad[...] = (act_grad * slope).astype(BF16)
    tails = dot(pre_grad[...], w_in[:, 2048:2560])
    lane = iota((128, 128), 1)
    for f in range(CTX_COUNT):
        part = dot(pre_grad[...], w_in[:, 256 * f : 256 * f + 256])
        put(f, slice(0, 256), part[0:128].astype(BF16))
        put(f, slice(256, 512), part[128:256].astype(BF16))
        tile = slice(128 * (f // 2), 128 * (f // 2) + 128)
        a, b = tails[0:128, tile], tails[128:256, tile]
        if f % 2 == 0:
            tail = jnp.where(lane < 64, a, pltpu.roll(b, 64, 1))
        else:
            tail = jnp.where(lane < 64, pltpu.roll(a, 64, 1), b)
        put(f, slice(512, 640), tail.astype(BF16))


def early_kernel(own, up, down, partner, w_in, w_out, sums, rows, douts, act, pre_grad):
    def put(f, lanes, value):
        sums[f, :, lanes] = value

    blocks = [lambda s=s: s[...] for s in (own, up, down, partner)]
    experts_of(blocks, w_in, w_out, rows, douts, act, pre_grad, put)


def late_kernel(at_ref, *refs):
    shards, (w_in, w_out, early, query_pack) = refs[:6], refs[6:10]
    sums, rows, douts, act, pre_grad = refs[10:]
    where = [pl.ds(pl.multiple_of(32 * at_ref[k], 32), 32) for k in range(CTX_COUNT)]

    def put(f, lanes, value):
        for k in range(4):
            sums[f, where[4 + k], lanes] = value[32 * k : 32 * k + 32]

    blocks = [lambda s=s: s[...] for s in shards[:2]]
    blocks += [
        lambda k=k: jnp.concatenate([shards[k][...], shards[k + 1][...]], axis=0) for k in (2, 4)
    ]
    experts_of(blocks, w_in, w_out, rows, douts, act, pre_grad, put)
    for f in range(CTX_COUNT):
        for k in range(4):
            sums[f, where[k], :] = early[f, 32 * k : 32 * k + 32, :]
        sums[f, 256:320, :] = query_pack[f]


def weights_kernel(*refs):
    (early, late), out = (refs[:4], refs[4:8]), refs[8]
    unit, column = iota((UNITS, 2 * UNITS), 0), iota((UNITS, 2 * UNITS), 1)
    even, odd = one(column == 2 * unit), one(column == 2 * unit + 1)
    terms = []
    for rows, douts, act, pre_grad in (early, late):
        terms.append((dot(pre_grad[...], even).astype(BF16), rows))
        terms.append((dot(act[...], odd).astype(BF16), douts))
    for n in range(D // 512):
        lanes = slice(512 * n, 512 * n + 512)
        out[:, lanes] = sum(dot(a, b[:, lanes], ((0,), (0,))) for a, b in terms).astype(BF16)


def total_kernel(parts, back, query):
    total = parts[0].astype(F32)
    for k in range(1, CTX_COUNT):
        total = total + parts[k].astype(F32)
    to, source = iota((ROWS, ROWS), 0), iota((ROWS, ROWS), 1)
    order = one(source == 32 * (to % 8) + to // 8)
    back[...] = dot(order, total[0:256].astype(BF16)).astype(BF16)
    query[...] = total[256:320]


def tokens_kernel(returned, even, odd, query, out):
    a = dot(even[...], returned[...], ((0,), (0,)))
    b = dot(odd[...], returned[...], ((0,), (0,)))
    wide = a[:, 0:256] + b[:, 256:512]
    tail = a[:, 512:640] + pltpu.roll(b[:, 512:640], 64, 1)
    lane = iota((64, 128), 1)
    tail = jnp.where(lane < 64, tail[0:64], pltpu.roll(tail[64:128], 64, 1))
    left = (wide[0:64] + query[:, 0:256]).astype(BF16)
    right = (wide[64:128] + query[:, 256:512]).astype(BF16)
    tail = (tail + query[:, 512:640]).astype(BF16)
    for f in range(CTX_COUNT):
        out[f, :, 0:256] = left
        out[f, :, 256:512] = right
        out[f, :, 512:640] = tail


def norm_grad_kernel(packs, states, grads, gain, out, total):
    for f in range(CTX_COUNT):
        at = slice(256 * f, 256 * f + 256)
        total[0:64, at] = packs[f, :, 0:256].astype(F32)
        total[64:128, at] = packs[f, :, 256:512].astype(F32)
    lane = iota((64, 128), 1)
    for g in range(CTX_COUNT // 2):
        at = slice(2048 + 128 * g, 2176 + 128 * g)
        a = packs[2 * g, :, 512:640].astype(F32)
        b = packs[2 * g + 1, :, 512:640].astype(F32)
        total[0:64, at] = jnp.where(lane < 64, a, pltpu.roll(b, 64, 1))
        total[64:128, at] = jnp.where(lane < 64, pltpu.roll(a, 64, 1), b)
    x = states[...].astype(F32)
    inverse = lax.rsqrt(jnp.mean(x * x, axis=-1, keepdims=True) + EPSILON)
    unit = x * inverse
    g = total[...] * gain[...].reshape(1, D)
    g = g - unit * jnp.mean(g * unit, axis=-1, keepdims=True)
    out[...] = (grads[...].astype(F32) + inverse * g).astype(BF16)


def moved_by(array, axis, step):
    count = lax.axis_size(axis)
    return lax.ppermute(array, axis, [(k, (k + step) % count) for k in range(count)])


def on_device(
    states, out_grad, doc_keys, doc_values, norm_gain, expert_ids, gate_values, expert_weights
):
    states, grads, keys, values = states[0], out_grad[0], doc_keys[0], doc_values[0]
    y, x = lax.axis_index("ctx_0"), lax.axis_index("ctx_1")
    here = (2 * y + x).astype(jnp.int32)
    normed, send, even, odd = call(
        route_kernel,
        [SMEM] + [VMEM] * 5,
        [shape((TOKENS, D)), shape((ROWS, HALF)), shape((ROWS, TOKENS)), shape((ROWS, TOKENS))],
        flops=2 * 4 * ROWS * TOKENS * HALF,
        moved=3 * 2**20,
        limit=VMEM_ALL,
    )(here.reshape(1), states, grads, norm_gain, expert_ids[0].T, gate_values[0].T)
    own = lax.all_to_all(
        send.reshape(EXPERTS, 8, HALF), "exp", split_axis=0, concat_axis=0, tiled=True
    ).reshape(ROWS, HALF)

    weights, slopes, stats = call(
        scores_kernel,
        [VMEM] * 4,
        [shape((HEADS, KEYS, TOKENS), F32), shape((HEADS, KEYS, TOKENS), F32), shape((72, TOKENS), F32)],
        flops=2 * 2 * KEYS * TOKENS * D,
        moved=5 * 2**20,
    )(normed, grads, keys, values)
    near = merged([stats] + [moved_by(stats, "ctx_0", k) for k in (1, 2, 3)])
    far = moved_by(near, "ctx_1", 1)
    keys_grad, values_grad, query_pack = call(
        score_grad_kernel,
        [VMEM] * 8,
        [shape((KEYS, D)), shape((KEYS, D)), shape((CTX_COUNT, 64, CHUNK))],
        [pltpu.VMEM((TOKENS, D), F32)],
        flops=3 * 2 * KEYS * TOKENS * D,
        moved=6 * 2**20,
        limit=VMEM_ALL,
    )(normed, grads, keys, weights, slopes, stats, near, far)

    up, down = moved_by(own, "ctx_0", 1), moved_by(own, "ctx_0", 3)
    partner = moved_by(own, "ctx_1", 1)
    across = [moved_by(up[:128], "ctx_0", 1), moved_by(down[128:], "ctx_0", 3)]
    partner_up, partner_down = moved_by(partner, "ctx_0", 1), moved_by(partner, "ctx_0", 3)
    partner_across = [moved_by(piece, "ctx_1", 1) for piece in across]
    places = [(0, 0), (-1, 0), (1, 0), (0, 1), (-1, 1), (1, 1), (2, 0), (2, 1)]
    at = jnp.stack([2 * ((y + a + 4) % 4) + (x + b) % 2 for a, b in places]).astype(jnp.int32)
    w_in, w_out = expert_weights[0, :, 0, :], expert_weights[0, :, 1, :]
    kept = [shape((SLOTS, D))] * 2 + [shape((SLOTS, UNITS))] * 2
    early_sums, *early = call(
        early_kernel,
        [VMEM] * 6,
        [shape((CTX_COUNT, SLOTS // 2, CHUNK)), *kept],
        flops=2 * 3 * SLOTS * UNITS * D,
        moved=8 * 2**20,
    )(own, up, down, partner, w_in, w_out)
    sums, *late = call(
        late_kernel,
        [SMEM] + [VMEM] * 10,
        [shape((CTX_COUNT, 320, CHUNK)), *kept],
        flops=2 * 3 * SLOTS * UNITS * D,
        moved=12 * 2**20,
    )(at, partner_up, partner_down, *across, *partner_across, w_in, w_out, early_sums, query_pack)
    parts = lax.all_to_all(sums, CTX, split_axis=0, concat_axis=0, tiled=True)
    back, query = call(
        total_kernel,
        [VMEM],
        [shape((ROWS, CHUNK)), shape((64, CHUNK), F32)],
        moved=4 * 2**20,
    )(parts)
    late[3], back = lax.optimization_barrier((late[3], back))
    returned = lax.all_to_all(
        back.reshape(EXPERTS, 8, CHUNK), "exp", split_axis=0, concat_axis=0, tiled=True
    ).reshape(ROWS, CHUNK)
    [weights_grad] = call(
        weights_kernel,
        [VMEM] * 8,
        [shape((2 * UNITS, D))],
        flops=2 * 4 * SLOTS * UNITS * D,
        moved=8 * 2**20,
        limit=VMEM_ALL,
    )(*early, *late)
    weights_grad = weights_grad.reshape(1, UNITS, 2, D)
    returned, weights_grad = lax.optimization_barrier((returned, weights_grad))
    [total] = call(tokens_kernel, [VMEM] * 4, [shape((CTX_COUNT, 64, CHUNK))], moved=2**20)(
        returned, even, odd, query
    )
    packs = lax.all_to_all(total, CTX, split_axis=0, concat_axis=0, tiled=True)
    [states_grad] = call(
        norm_grad_kernel,
        [VMEM] * 4,
        [shape((TOKENS, D))],
        [pltpu.VMEM((TOKENS, D), F32)],
        moved=3 * 2**20,
    )(packs, states, grads, norm_gain)
    return states_grad[None], keys_grad[None], values_grad[None], weights_grad


def solution(mesh):
    finer = Mesh(mesh.devices.reshape(4, 2, mesh.shape["exp"]), (*CTX, "exp"))
    return jax.shard_map(
        on_device,
        mesh=finer,
        in_specs=(
            P("exp", None, None),
            P("exp", None, None),
            P("exp", CTX, None),
            P("exp", CTX, None),
            P(),
            P("exp", None, None),
            P("exp", None, None),
            P("exp", CTX, None, None),
        ),
        out_specs=(
            P("exp", None, None),
            P("exp", CTX, None),
            P("exp", CTX, None),
            P("exp", CTX, None, None),
        ),
        check_vma=False,
    )
```

```python
import math

import jax
import jax.numpy as jnp
from jax import lax
from jax.experimental import pallas as pl
from jax.experimental.pallas import tpu as pltpu
from jax.sharding import Mesh
from jax.sharding import PartitionSpec as P

HEADS = 20
HEAD = 128
D = 2560
HALF = 1280
TOKENS = 128
KEYS = 128
UNITS = 256
EXPERTS = 32
CTX_COUNT = 8
ROWS = 256
SLOTS = 256
CHUNK = 640
CTX = ("ctx_0", "ctx_1")
EPSILON = 1e-05
SCALE = HEAD**-0.5
BF16 = jnp.bfloat16
F32 = jnp.float32
VMEM_LIMIT = 24 * 2**20
VMEM_ALL = 60 * 2**20

VMEM = pl.BlockSpec(memory_space=pltpu.VMEM)
SMEM = pl.BlockSpec(memory_space=pltpu.SMEM)
ANY = pl.BlockSpec(memory_space=pl.ANY)


def call(kernel, ins, outs, scratch=(), flops=0, moved=0, places=None, limit=VMEM_LIMIT):
    return pl.pallas_call(
        kernel,
        in_specs=ins,
        out_specs=places or [VMEM] * len(outs),
        out_shape=outs,
        scratch_shapes=list(scratch),
        compiler_params=pltpu.CompilerParams(vmem_limit_bytes=limit),
        cost_estimate=pl.CostEstimate(flops=flops, bytes_accessed=moved, transcendentals=0),
    )


def shape(dims, dtype=BF16):
    return jax.ShapeDtypeStruct(dims, dtype)


def dot(a, b, dims=((1,), (0,))):
    return lax.dot_general(a, b, (dims, ((), ())), preferred_element_type=F32)


def iota(dims, axis):
    return lax.broadcasted_iota(jnp.int32, dims, axis)


def one(mask):
    return jnp.where(mask, 1.0, 0.0).astype(BF16)


def route_kernel(place, states, grads, gain, ids, gates, normed_out, send, even, odd):
    c = 2 * place[0] + place[1]
    x = states[...].astype(F32)
    inverse = lax.rsqrt(jnp.mean(x * x, axis=-1, keepdims=True) + EPSILON)
    normed_out[...] = (x * inverse * gain[...].reshape(1, D)).astype(BF16)
    expert = iota((ROWS, TOKENS), 0) // 8
    i = iota((ROWS, TOKENS), 0) % 8
    first = ids[0:1, :] == expert
    second = ids[1:2, :] == expert
    named = first | second
    before = one(iota((TOKENS, TOKENS), 0) < iota((TOKENS, TOKENS), 1))
    slot = dot(one(named), before).astype(jnp.int32)
    slot = jnp.where(named, slot, -1)
    even[...] = one(slot == 2 * i)
    odd[...] = one(slot == 2 * i + 1)
    mine = slot == 2 * c + i % 2
    gate = jnp.where(first, gates[0:1, :], 0.0) + jnp.where(second, gates[1:2, :], 0.0)
    gate = jnp.sum(jnp.where(mine, gate, 0.0), axis=1, keepdims=True)
    low = i < 4
    is_row = (i // 2) % 2 == 0
    row_low = one(mine & low & is_row)
    row_high = one(mine & (~low) & is_row)
    grad_low = one(mine & low & (~is_row))
    grad_high = one(mine & (~low) & (~is_row))
    rows = dot(row_low, normed_out[:, :HALF]) + dot(row_high, normed_out[:, HALF:])
    douts = dot(grad_low, grads[:, :HALF]) + dot(grad_high, grads[:, HALF:])
    send[...] = (rows + gate * douts).astype(BF16)


def scores_kernel(normed, grads, keys, values, weights_out, slopes_out, stats):
    for h in range(HEADS):
        at = slice(h * HEAD, (h + 1) * HEAD)
        s = dot(keys[:, at], normed[:, at], ((1,), (1,))) * SCALE
        peak = jnp.max(s, axis=0, keepdims=True)
        w = jnp.exp(s - peak)
        slopes = dot(values[:, at], grads[:, at], ((1,), (1,)))
        weights_out[h] = w
        slopes_out[h] = slopes
        stats[h : h + 1, :] = peak
        stats[24 + h : 25 + h, :] = jnp.sum(w, axis=0, keepdims=True)
        stats[48 + h : 49 + h, :] = jnp.sum(w * slopes, axis=0, keepdims=True)
    for part in range(3):
        at = 24 * part + HEADS
        stats[at : at + 4, :] = jnp.zeros((4, TOKENS), F32)


def merged(stats):
    peak = stats[0][:24]
    for one_side in stats[1:]:
        peak = jnp.maximum(peak, one_side[:24])
    total = inner = 0.0
    for one_side in stats:
        factor = jnp.exp(one_side[:24] - peak)
        total = total + one_side[24:48] * factor
        inner = inner + one_side[48:] * factor
    return jnp.concatenate([peak, total, inner], axis=0)


def score_grad_kernel(
    place, normed, grads, keys, weights, slopes, local, near, far, keys_grad, values_grad, query_pack, query
):
    peak = jnp.maximum(near[0:24, :], far[0:24, :])
    near_factor = jnp.exp(near[0:24, :] - peak)
    far_factor = jnp.exp(far[0:24, :] - peak)
    total = near[24:48, :] * near_factor + far[24:48, :] * far_factor
    inner = near[48:72, :] * near_factor + far[48:72, :] * far_factor
    total = jnp.where(iota((24, TOKENS), 0) < HEADS, total, 1.0)
    factor = jnp.exp(local[0:24, :] - peak) / total
    delta = inner / total
    for h in range(HEADS):
        at = slice(h * HEAD, (h + 1) * HEAD)
        probs = weights[h] * factor[h : h + 1, :]
        score_grad = (probs * (slopes[h] - delta[h : h + 1, :])).astype(BF16)
        values_grad[:, at] = dot(probs.astype(BF16), grads[:, at]).astype(BF16)
        keys_grad[:, at] = (dot(score_grad, normed[:, at]) * SCALE).astype(BF16)
        query[:, at] = dot(score_grad, keys[:, at], ((0,), (0,))) * SCALE
    lane = iota((64, 128), 1)
    for f in range(CTX_COUNT):
        column, row = (f + place[1] + 1) % 2, (f // 2 - place[0] + 4) % 4
        at = slice(256 * f, 256 * f + 256)
        query_pack[column, row, :, 0:256] = query[0:64, at].astype(BF16)
        query_pack[column, row, :, 256:512] = query[64:128, at].astype(BF16)
        tile = slice(2048 + 128 * (f // 2), 2176 + 128 * (f // 2))
        a, b = query[0:64, tile], query[64:128, tile]
        if f % 2 == 0:
            tail = jnp.where(lane < 64, a, pltpu.roll(b, 64, 1))
        else:
            tail = jnp.where(lane < 64, pltpu.roll(a, 64, 1), b)
        query_pack[column, row, :, 512:640] = tail.astype(BF16)


def join_kernel(query_pack, far, *outs):
    for k in range(4):
        outs[k][...] = (query_pack[1, k].astype(F32) + far[k].astype(F32)).astype(BF16)


def experts_of(blocks, w_in, w_out, rows, douts, act, pre_grad, put, after=lambda step: None):
    to, source = iota((ROWS, ROWS), 0), iota((ROWS, ROWS), 1)
    order = one(source == 8 * (to % 32) + to // 32)
    for k, block in enumerate(blocks):
        sorted_rows = dot(order, block()).astype(BF16)
        for q in range(2):
            where = slice(128 * q + 32 * k, 128 * q + 32 * k + 32)
            for half in range(2):
                lanes = slice(HALF * half, HALF * half + HALF)
                first = 128 * half + 32 * q
                rows[where, lanes] = sorted_rows[first : first + 32, :]
                douts[where, lanes] = sorted_rows[first + 64 : first + 96, :]
    after("rows")
    v = dot(rows[...], w_in[...], ((1,), (1,)))
    act_grad = dot(douts[...], w_out[...], ((1,), (1,)))
    root = math.sqrt(2 / math.pi)
    square = v * v
    t = jnp.tanh(root * (v + 0.044715 * (square * v)))
    act[...] = (0.5 * v * (1.0 + t)).astype(BF16)
    slope = 0.5 * (1.0 + t) + 0.5 * v * (1.0 - t * t) * (root * (1.0 + 3 * 0.044715 * square))
    pre_grad[...] = (act_grad * slope).astype(BF16)
    after("units")
    tails = dot(pre_grad[...], w_in[:, 2048:2560])
    lane = iota((128, 128), 1)
    for f in range(CTX_COUNT):
        part = dot(pre_grad[...], w_in[:, 256 * f : 256 * f + 256])
        put(f, slice(0, 256), part[0:128].astype(BF16))
        put(f, slice(256, 512), part[128:256].astype(BF16))
        tile = slice(128 * (f // 2), 128 * (f // 2) + 128)
        a, b = tails[0:128, tile], tails[128:256, tile]
        if f % 2 == 0:
            tail = jnp.where(lane < 64, a, pltpu.roll(b, 64, 1))
        else:
            tail = jnp.where(lane < 64, pltpu.roll(a, 64, 1), b)
        put(f, slice(512, 640), tail.astype(BF16))
        after(f)


def early_kernel(own, up, down, partner, w_in, w_out, sums, rows, douts, act, pre_grad):
    def put(f, lanes, value):
        sums[f, :, lanes] = value

    blocks = [lambda s=s: s[...] for s in (own, up, down, partner)]
    experts_of(blocks, w_in, w_out, rows, douts, act, pre_grad, put)


def late_kernel(at_ref, *refs):
    given, results, held = refs[:9], refs[9:14], refs[14:]
    shards, (w_in, w_out), sums, kept = held[:4], held[4:6], held[6], held[7:11]
    arrived, left = held[11:]
    where = [pl.ds(pl.multiple_of(32 * at_ref[k], 32), 32) for k in range(CTX_COUNT)]
    landing = [
        *shards[:2],
        *(shards[k].at[128 * j : 128 * j + 128] for k in (2, 3) for j in range(2)),
        w_in,
        w_out,
    ]
    loads = [pltpu.make_async_copy(given[k], landing[k], arrived.at[k]) for k in range(8)]
    for load in loads:
        load.start()
    stores = [pltpu.make_async_copy(kept[k], results[1 + k], left.at[k]) for k in range(4)]
    stores += [
        pltpu.make_async_copy(
            given[8].at[:, 32 * k : 32 * k + 32, :], results[0].at[:, where[k], :], left.at[4 + k]
        )
        for k in range(4)
    ]
    for store in stores[4:]:
        store.start()
    for k in range(4):
        stores += [
            pltpu.make_async_copy(
                sums.at[f, 32 * k : 32 * k + 32, :],
                results[0].at[f, where[4 + k], :],
                left.at[8 + CTX_COUNT * k + f],
            )
            for f in range(CTX_COUNT)
        ]

    def block(k):
        for load in loads[k : k + 1] if k < 2 else loads[2 * k - 2 : 2 * k]:
            load.wait()
        return shards[k][...]

    def put(f, lanes, value):
        sums[f, :, lanes] = value

    def after(step):
        if step == "rows":
            stores[0].start()
            stores[1].start()
            loads[6].wait()
            loads[7].wait()
        elif step == "units":
            stores[2].start()
            stores[3].start()
        else:
            for k in range(4):
                stores[8 + CTX_COUNT * k + step].start()

    blocks = [lambda k=k: block(k) for k in range(4)]
    experts_of(blocks, w_in, w_out, *kept, put, after)
    for store in stores:
        store.wait()


def weights_kernel(*refs):
    given, out, held, arrived = refs[:8], refs[8], refs[9:17], refs[17]
    loads = [pltpu.make_async_copy(given[k], held[k], arrived.at[k]) for k in range(8)]
    for load in loads:
        load.start()
    unit, column = iota((UNITS, 2 * UNITS), 0), iota((UNITS, 2 * UNITS), 1)
    even, odd = one(column == 2 * unit), one(column == 2 * unit + 1)
    for load in loads:
        load.wait()
    terms = []
    for rows, douts, act, pre_grad in (held[:4], held[4:]):
        terms.append((dot(pre_grad[...], even).astype(BF16), rows))
        terms.append((dot(act[...], odd).astype(BF16), douts))
    for n in range(D // 512):
        lanes = slice(512 * n, 512 * n + 512)
        out[:, lanes] = sum(dot(a, b[:, lanes], ((0,), (0,))) for a, b in terms).astype(BF16)


def total_kernel(parts, back):
    total = parts[0].astype(F32)
    for k in range(1, CTX_COUNT):
        total = total + parts[k].astype(F32)
    to, source = iota((ROWS, ROWS), 0), iota((ROWS, ROWS), 1)
    order = one(source == 32 * (to % 8) + to // 8)
    back[...] = dot(order, total.astype(BF16)).astype(BF16)


def tokens_kernel(returned, even, odd, own, below, across, above, out):
    query = (own[...].astype(F32) + across[...].astype(F32)) + (
        below[...].astype(F32) + above[...].astype(F32)
    )
    a = dot(even[...], returned[...], ((0,), (0,)))
    b = dot(odd[...], returned[...], ((0,), (0,)))
    wide = a[:, 0:256] + b[:, 256:512]
    tail = a[:, 512:640] + pltpu.roll(b[:, 512:640], 64, 1)
    lane = iota((64, 128), 1)
    tail = jnp.where(lane < 64, tail[0:64], pltpu.roll(tail[64:128], 64, 1))
    left = (wide[0:64] + query[:, 0:256]).astype(BF16)
    right = (wide[64:128] + query[:, 256:512]).astype(BF16)
    tail = (tail + query[:, 512:640]).astype(BF16)
    for f in range(CTX_COUNT):
        out[f, :, 0:256] = left
        out[f, :, 256:512] = right
        out[f, :, 512:640] = tail


def norm_grad_kernel(packs, states, grads, gain, out, total):
    for f in range(CTX_COUNT):
        at = slice(256 * f, 256 * f + 256)
        total[0:64, at] = packs[f, :, 0:256].astype(F32)
        total[64:128, at] = packs[f, :, 256:512].astype(F32)
    lane = iota((64, 128), 1)
    for g in range(CTX_COUNT // 2):
        at = slice(2048 + 128 * g, 2176 + 128 * g)
        a = packs[2 * g, :, 512:640].astype(F32)
        b = packs[2 * g + 1, :, 512:640].astype(F32)
        total[0:64, at] = jnp.where(lane < 64, a, pltpu.roll(b, 64, 1))
        total[64:128, at] = jnp.where(lane < 64, pltpu.roll(a, 64, 1), b)
    x = states[...].astype(F32)
    inverse = lax.rsqrt(jnp.mean(x * x, axis=-1, keepdims=True) + EPSILON)
    unit = x * inverse
    g = total[...] * gain[...].reshape(1, D)
    g = g - unit * jnp.mean(g * unit, axis=-1, keepdims=True)
    out[...] = (grads[...].astype(F32) + inverse * g).astype(BF16)


def moved_by(array, axis, step):
    count = lax.axis_size(axis)
    return lax.ppermute(array, axis, [(k, (k + step) % count) for k in range(count)])


def on_device(
    states, out_grad, doc_keys, doc_values, norm_gain, expert_ids, gate_values, expert_weights
):
    states, grads, keys, values = states[0], out_grad[0], doc_keys[0], doc_values[0]
    y, x = lax.axis_index("ctx_0"), lax.axis_index("ctx_1")
    place = jnp.stack([y, x]).astype(jnp.int32)
    normed, send, even, odd = call(
        route_kernel,
        [SMEM] + [VMEM] * 5,
        [shape((TOKENS, D)), shape((ROWS, HALF)), shape((ROWS, TOKENS)), shape((ROWS, TOKENS))],
        flops=2 * 4 * ROWS * TOKENS * HALF,
        moved=3 * 2**20,
        limit=VMEM_ALL,
    )(place, states, grads, norm_gain, expert_ids[0].T, gate_values[0].T)
    own = lax.all_to_all(
        send.reshape(EXPERTS, 8, HALF), "exp", split_axis=0, concat_axis=0, tiled=True
    ).reshape(ROWS, HALF)

    weights, slopes, stats = call(
        scores_kernel,
        [VMEM] * 4,
        [shape((HEADS, KEYS, TOKENS), F32), shape((HEADS, KEYS, TOKENS), F32), shape((72, TOKENS), F32)],
        flops=2 * 2 * KEYS * TOKENS * D,
        moved=5 * 2**20,
    )(normed, grads, keys, values)
    near = merged([stats] + [moved_by(stats, "ctx_0", k) for k in (1, 2, 3)])
    far = moved_by(near, "ctx_1", 1)
    keys_grad, values_grad, query_pack = call(
        score_grad_kernel,
        [SMEM] + [VMEM] * 8,
        [shape((KEYS, D)), shape((KEYS, D)), shape((2, 4, 64, CHUNK))],
        [pltpu.VMEM((TOKENS, D), F32)],
        flops=3 * 2 * KEYS * TOKENS * D,
        moved=6 * 2**20,
        limit=VMEM_ALL,
    )(place, normed, grads, keys, weights, slopes, stats, near, far)


    up, down = moved_by(own, "ctx_0", 1), moved_by(own, "ctx_0", 3)
    partner = moved_by(own, "ctx_1", 1)
    up, down, partner, query_pack = lax.optimization_barrier((up, down, partner, query_pack))
    across = [moved_by(up[:128], "ctx_0", 1), moved_by(down[128:], "ctx_0", 3)]
    far_query = moved_by(query_pack[0], "ctx_1", 1)
    *across, expert_weights = lax.optimization_barrier((*across, expert_weights))
    partner_up, partner_down = moved_by(partner, "ctx_0", 1), moved_by(partner, "ctx_0", 3)
    partner_across = [moved_by(piece, "ctx_1", 1) for piece in across]
    w_in, w_out = expert_weights[0, :, 0, :], expert_weights[0, :, 1, :]
    places = [(0, 0), (-1, 0), (1, 0), (0, 1), (-1, 1), (1, 1), (2, 0), (2, 1)]
    at = jnp.stack([2 * ((y + a + 4) % 4) + (x + b) % 2 for a, b in places]).astype(jnp.int32)
    kept = [shape((SLOTS, D))] * 2 + [shape((SLOTS, UNITS))] * 2
    early_sums, *early = call(
        early_kernel,
        [VMEM] * 6,
        [shape((CTX_COUNT, SLOTS // 2, CHUNK)), *kept],
        flops=2 * 3 * SLOTS * UNITS * D,
        moved=8 * 2**20,
        limit=VMEM_ALL,
    )(own, up, down, partner, w_in, w_out)
    sums, *late = call(
        late_kernel,
        [SMEM] + [ANY] * 9,
        [shape((CTX_COUNT, ROWS, CHUNK)), *kept],
        [
            *[pltpu.VMEM((ROWS, HALF), BF16)] * 4,
            *[pltpu.VMEM((UNITS, D), BF16)] * 2,
            pltpu.VMEM((CTX_COUNT, SLOTS // 2, CHUNK), BF16),
            *[pltpu.VMEM(k.shape, BF16) for k in kept],
            pltpu.SemaphoreType.DMA((8,)),
            pltpu.SemaphoreType.DMA((8 + 4 * CTX_COUNT,)),
        ],
        flops=2 * 3 * SLOTS * UNITS * D,
        moved=12 * 2**20,
        places=[ANY] * 5,
        limit=VMEM_ALL,
    )(at, partner_up, partner_down, *across, *partner_across, w_in, w_out, early_sums)
    sums, far_query = lax.optimization_barrier((sums, far_query))
    parts = lax.all_to_all(sums, CTX, split_axis=0, concat_axis=0, tiled=True)
    [weights_grad] = call(
        weights_kernel,
        [ANY] * 8,
        [shape((2 * UNITS, D))],
        [pltpu.VMEM(k.shape, BF16) for k in (*kept, *kept)] + [pltpu.SemaphoreType.DMA((8,))],
        flops=2 * 4 * SLOTS * UNITS * D,
        moved=8 * 2**20,
        limit=VMEM_ALL,
    )(*early, *late)
    weights_grad = weights_grad.reshape(1, UNITS, 2, D)
    parts, weights_grad = lax.optimization_barrier((parts, weights_grad))
    [back] = call(total_kernel, [VMEM], [shape((ROWS, CHUNK))], moved=3 * 2**20)(parts)
    back, far_query = lax.optimization_barrier((back, far_query))
    returned = lax.all_to_all(
        back.reshape(EXPERTS, 8, CHUNK), "exp", split_axis=0, concat_axis=0, tiled=True
    ).reshape(ROWS, CHUNK)
    queries = call(join_kernel, [VMEM] * 2, [shape((64, CHUNK))] * 4, moved=2**20)(query_pack, far_query)
    queries = [queries[0]] + [moved_by(queries[k], "ctx_0", k) for k in (1, 2, 3)]
    [total] = call(tokens_kernel, [VMEM] * 7, [shape((CTX_COUNT, 64, CHUNK))], moved=2**20)(
        returned, even, odd, *queries
    )
    packs = lax.all_to_all(total, CTX, split_axis=0, concat_axis=0, tiled=True)
    [states_grad] = call(
        norm_grad_kernel,
        [VMEM] * 4,
        [shape((TOKENS, D))],
        [pltpu.VMEM((TOKENS, D), F32)],
        moved=3 * 2**20,
    )(packs, states, grads, norm_gain)
    return states_grad[None], keys_grad[None], values_grad[None], weights_grad


def solution(mesh):
    finer = Mesh(mesh.devices.reshape(4, 2, mesh.shape["exp"]), (*CTX, "exp"))
    return jax.shard_map(
        on_device,
        mesh=finer,
        in_specs=(
            P("exp", None, None),
            P("exp", None, None),
            P("exp", CTX, None),
            P("exp", CTX, None),
            P(),
            P("exp", None, None),
            P("exp", None, None),
            P("exp", CTX, None, None),
        ),
        out_specs=(
            P("exp", None, None),
            P("exp", CTX, None),
            P("exp", CTX, None),
            P("exp", CTX, None, None),
        ),
        check_vma=False,
    )
```

```python
import math

import jax
import jax.numpy as jnp
from jax import lax
from jax.experimental import pallas as pl
from jax.experimental.pallas import tpu as pltpu
from jax.sharding import Mesh
from jax.sharding import PartitionSpec as P

HEADS = 20
HEAD = 128
D = 2560
HALF = 1280
TOKENS = 128
KEYS = 128
UNITS = 256
EXPERTS = 32
CTX_COUNT = 8
ROWS = 256
SLOTS = 256
CHUNK = 640
CTX = ("ctx_0", "ctx_1")
EPSILON = 1e-05
SCALE = HEAD**-0.5
BF16 = jnp.bfloat16
F32 = jnp.float32
VMEM_LIMIT = 24 * 2**20
VMEM_ALL = 60 * 2**20

VMEM = pl.BlockSpec(memory_space=pltpu.VMEM)
SMEM = pl.BlockSpec(memory_space=pltpu.SMEM)
ANY = pl.BlockSpec(memory_space=pl.ANY)


def call(kernel, ins, outs, scratch=(), flops=0, moved=0, places=None, limit=VMEM_LIMIT):
    return pl.pallas_call(
        kernel,
        in_specs=ins,
        out_specs=places or [VMEM] * len(outs),
        out_shape=outs,
        scratch_shapes=list(scratch),
        compiler_params=pltpu.CompilerParams(vmem_limit_bytes=limit),
        cost_estimate=pl.CostEstimate(flops=flops, bytes_accessed=moved, transcendentals=0),
    )


def shape(dims, dtype=BF16):
    return jax.ShapeDtypeStruct(dims, dtype)


def dot(a, b, dims=((1,), (0,))):
    return lax.dot_general(a, b, (dims, ((), ())), preferred_element_type=F32)


def iota(dims, axis):
    return lax.broadcasted_iota(jnp.int32, dims, axis)


def one(mask):
    return jnp.where(mask, 1.0, 0.0).astype(BF16)


def route_kernel(place, states, grads, gain, ids, gates, normed_out, send, even, odd):
    c = place[0]
    x = states[...].astype(F32)
    inverse = lax.rsqrt(jnp.mean(x * x, axis=-1, keepdims=True) + EPSILON)
    normed_out[...] = (x * inverse * gain[...].reshape(1, D)).astype(BF16)
    expert = iota((ROWS, TOKENS), 0) // 8
    i = iota((ROWS, TOKENS), 0) % 8
    first = ids[0:1, :] == expert
    second = ids[1:2, :] == expert
    named = first | second
    before = one(iota((TOKENS, TOKENS), 0) < iota((TOKENS, TOKENS), 1))
    slot = dot(one(named), before).astype(jnp.int32)
    slot = jnp.where(named, slot, -1)
    even[...] = one(slot == 2 * i)
    odd[...] = one(slot == 2 * i + 1)
    mine = slot == 2 * c + i % 2
    gate = jnp.where(first, gates[0:1, :], 0.0) + jnp.where(second, gates[1:2, :], 0.0)
    gate = jnp.sum(jnp.where(mine, gate, 0.0), axis=1, keepdims=True)
    low = i < 4
    is_row = (i // 2) % 2 == 0
    row_low = one(mine & low & is_row)
    row_high = one(mine & (~low) & is_row)
    grad_low = one(mine & low & (~is_row))
    grad_high = one(mine & (~low) & (~is_row))
    rows = dot(row_low, normed_out[:, :HALF]) + dot(row_high, normed_out[:, HALF:])
    douts = dot(grad_low, grads[:, :HALF]) + dot(grad_high, grads[:, HALF:])
    send[...] = (rows + gate * douts).astype(BF16)


def scores_kernel(normed, grads, keys, values, weights_out, slopes_out, stats):
    for h in range(HEADS):
        at = slice(h * HEAD, (h + 1) * HEAD)
        s = dot(keys[:, at], normed[:, at], ((1,), (1,))) * SCALE
        peak = jnp.max(s, axis=0, keepdims=True)
        w = jnp.exp(s - peak)
        slopes = dot(values[:, at], grads[:, at], ((1,), (1,)))
        weights_out[h] = w
        slopes_out[h] = slopes
        stats[h : h + 1, :] = peak
        stats[24 + h : 25 + h, :] = jnp.sum(w, axis=0, keepdims=True)
        stats[48 + h : 49 + h, :] = jnp.sum(w * slopes, axis=0, keepdims=True)
    for part in range(3):
        at = 24 * part + HEADS
        stats[at : at + 4, :] = jnp.zeros((4, TOKENS), F32)


def merged(stats):
    peak = stats[0][:24]
    for one_side in stats[1:]:
        peak = jnp.maximum(peak, one_side[:24])
    total = inner = 0.0
    for one_side in stats:
        factor = jnp.exp(one_side[:24] - peak)
        total = total + one_side[24:48] * factor
        inner = inner + one_side[48:] * factor
    return jnp.concatenate([peak, total, inner], axis=0)


def score_grad_kernel(
    place, normed, grads, keys, weights, slopes, local, near, far, keys_grad, values_grad, query_pack, query
):
    peak = jnp.maximum(near[0:24, :], far[0:24, :])
    near_factor = jnp.exp(near[0:24, :] - peak)
    far_factor = jnp.exp(far[0:24, :] - peak)
    total = near[24:48, :] * near_factor + far[24:48, :] * far_factor
    inner = near[48:72, :] * near_factor + far[48:72, :] * far_factor
    total = jnp.where(iota((24, TOKENS), 0) < HEADS, total, 1.0)
    factor = jnp.exp(local[0:24, :] - peak) / total
    delta = inner / total
    for h in range(HEADS):
        at = slice(h * HEAD, (h + 1) * HEAD)
        probs = weights[h] * factor[h : h + 1, :]
        score_grad = (probs * (slopes[h] - delta[h : h + 1, :])).astype(BF16)
        values_grad[:, at] = dot(probs.astype(BF16), grads[:, at]).astype(BF16)
        keys_grad[:, at] = (dot(score_grad, normed[:, at]) * SCALE).astype(BF16)
        query[:, at] = dot(score_grad, keys[:, at], ((0,), (0,))) * SCALE
    lane = iota((64, 128), 1)
    for f in range(CTX_COUNT):
        column, row = (f + place[0] + 1) % 2, (f // 2 - place[0] // 2 + 4) % 4
        at = slice(256 * f, 256 * f + 256)
        query_pack[column, row, :, 0:256] = query[0:64, at].astype(BF16)
        query_pack[column, row, :, 256:512] = query[64:128, at].astype(BF16)
        tile = slice(2048 + 128 * (f // 2), 2176 + 128 * (f // 2))
        a, b = query[0:64, tile], query[64:128, tile]
        if f % 2 == 0:
            tail = jnp.where(lane < 64, a, pltpu.roll(b, 64, 1))
        else:
            tail = jnp.where(lane < 64, pltpu.roll(a, 64, 1), b)
        query_pack[column, row, :, 512:640] = tail.astype(BF16)


def join_kernel(query_pack, far, *outs):
    for k in range(4):
        outs[k][...] = (query_pack[1, k].astype(F32) + far[k].astype(F32)).astype(BF16)


def experts_of(blocks, w_in, w_out, rows, douts, act, pre_grad, put, after=lambda step: None):
    to, source = iota((ROWS, ROWS), 0), iota((ROWS, ROWS), 1)
    order = one(source == 8 * (to % 32) + to // 32)
    for k, block in enumerate(blocks):
        sorted_rows = dot(order, block()).astype(BF16)
        for q in range(2):
            where = slice(128 * q + 32 * k, 128 * q + 32 * k + 32)
            for half in range(2):
                lanes = slice(HALF * half, HALF * half + HALF)
                first = 128 * half + 32 * q
                rows[where, lanes] = sorted_rows[first : first + 32, :]
                douts[where, lanes] = sorted_rows[first + 64 : first + 96, :]
    after("rows")
    v = dot(rows[...], w_in[...], ((1,), (1,)))
    act_grad = dot(douts[...], w_out[...], ((1,), (1,)))
    root = math.sqrt(2 / math.pi)
    square = v * v
    t = jnp.tanh(root * (v + 0.044715 * (square * v)))
    act[...] = (0.5 * v * (1.0 + t)).astype(BF16)
    slope = 0.5 * (1.0 + t) + 0.5 * v * (1.0 - t * t) * (root * (1.0 + 3 * 0.044715 * square))
    pre_grad[...] = (act_grad * slope).astype(BF16)
    after("units")
    tails = dot(pre_grad[...], w_in[:, 2048:2560])
    lane = iota((128, 128), 1)
    for f in range(CTX_COUNT):
        part = dot(pre_grad[...], w_in[:, 256 * f : 256 * f + 256])
        put(f, slice(0, 256), part[0:128].astype(BF16))
        put(f, slice(256, 512), part[128:256].astype(BF16))
        tile = slice(128 * (f // 2), 128 * (f // 2) + 128)
        a, b = tails[0:128, tile], tails[128:256, tile]
        if f % 2 == 0:
            tail = jnp.where(lane < 64, a, pltpu.roll(b, 64, 1))
        else:
            tail = jnp.where(lane < 64, pltpu.roll(a, 64, 1), b)
        put(f, slice(512, 640), tail.astype(BF16))
        after(f)


def early_kernel(own, up, down, partner, w_in, w_out, sums, rows, douts, act, pre_grad):
    def put(f, lanes, value):
        sums[f, :, lanes] = value

    blocks = [lambda s=s: s[...] for s in (own, up, down, partner)]
    experts_of(blocks, w_in, w_out, rows, douts, act, pre_grad, put)


def late_kernel(at_ref, *refs):
    given, results, held = refs[:9], refs[9:14], refs[14:]
    shards, (w_in, w_out), sums, kept = held[:4], held[4:6], held[6], held[7:11]
    arrived, left = held[11:]
    where = [pl.ds(pl.multiple_of(32 * at_ref[k], 32), 32) for k in range(CTX_COUNT)]
    landing = [
        *shards[:2],
        *(shards[k].at[128 * j : 128 * j + 128] for k in (2, 3) for j in range(2)),
        w_in,
        w_out,
    ]
    loads = [pltpu.make_async_copy(given[k], landing[k], arrived.at[k]) for k in range(8)]
    for load in loads:
        load.start()
    early = [
        pltpu.make_async_copy(
            given[8].at[:, 32 * k : 32 * k + 32, :], sums.at[:, where[k], :], arrived.at[8 + k]
        )
        for k in range(4)
    ]
    for load in early:
        load.start()
    stores = [pltpu.make_async_copy(kept[k], results[1 + k], left.at[k]) for k in range(4)]
    stores += [
        pltpu.make_async_copy(sums.at[f], results[0].at[f], left.at[4 + f])
        for f in range(CTX_COUNT)
    ]

    def block(k):
        for load in loads[k : k + 1] if k < 2 else loads[2 * k - 2 : 2 * k]:
            load.wait()
        return shards[k][...]

    def put(f, lanes, value):
        for k in range(4):
            sums[f, where[4 + k], lanes] = value[32 * k : 32 * k + 32]

    def after(step):
        if step == "rows":
            stores[0].start()
            stores[1].start()
            loads[6].wait()
            loads[7].wait()
        elif step == "units":
            stores[2].start()
            stores[3].start()
            for load in early:
                load.wait()
        else:
            stores[4 + step].start()

    blocks = [lambda k=k: block(k) for k in range(4)]
    experts_of(blocks, w_in, w_out, *kept, put, after)
    for store in stores:
        store.wait()


def weights_kernel(*refs):
    given, out, held, arrived = refs[:8], refs[8], refs[9:17], refs[17]
    loads = [pltpu.make_async_copy(given[k], held[k], arrived.at[k]) for k in range(8)]
    for load in loads:
        load.start()
    unit, column = iota((UNITS, 2 * UNITS), 0), iota((UNITS, 2 * UNITS), 1)
    even, odd = one(column == 2 * unit), one(column == 2 * unit + 1)
    for load in loads:
        load.wait()
    terms = []
    for rows, douts, act, pre_grad in (held[:4], held[4:]):
        terms.append((dot(pre_grad[...], even).astype(BF16), rows))
        terms.append((dot(act[...], odd).astype(BF16), douts))
    for n in range(D // 512):
        lanes = slice(512 * n, 512 * n + 512)
        out[:, lanes] = sum(dot(a, b[:, lanes], ((0,), (0,))) for a, b in terms).astype(BF16)


def total_kernel(parts, back):
    total = parts[0].astype(F32)
    for k in range(1, CTX_COUNT):
        total = total + parts[k].astype(F32)
    to, source = iota((ROWS, ROWS), 0), iota((ROWS, ROWS), 1)
    order = one(source == 32 * (to % 8) + to // 8)
    back[...] = dot(order, total.astype(BF16)).astype(BF16)


def tokens_kernel(returned, even, odd, own, below, across, above, out):
    query = (own[...].astype(F32) + across[...].astype(F32)) + (
        below[...].astype(F32) + above[...].astype(F32)
    )
    a = dot(even[...], returned[...], ((0,), (0,)))
    b = dot(odd[...], returned[...], ((0,), (0,)))
    wide = a[:, 0:256] + b[:, 256:512]
    tail = a[:, 512:640] + pltpu.roll(b[:, 512:640], 64, 1)
    lane = iota((64, 128), 1)
    tail = jnp.where(lane < 64, tail[0:64], pltpu.roll(tail[64:128], 64, 1))
    left = (wide[0:64] + query[:, 0:256]).astype(BF16)
    right = (wide[64:128] + query[:, 256:512]).astype(BF16)
    tail = (tail + query[:, 512:640]).astype(BF16)
    for f in range(CTX_COUNT):
        out[f, :, 0:256] = left
        out[f, :, 256:512] = right
        out[f, :, 512:640] = tail


def norm_grad_kernel(packs, states, grads, gain, out, total):
    for f in range(CTX_COUNT):
        at = slice(256 * f, 256 * f + 256)
        total[0:64, at] = packs[f, :, 0:256].astype(F32)
        total[64:128, at] = packs[f, :, 256:512].astype(F32)
    lane = iota((64, 128), 1)
    for g in range(CTX_COUNT // 2):
        at = slice(2048 + 128 * g, 2176 + 128 * g)
        a = packs[2 * g, :, 512:640].astype(F32)
        b = packs[2 * g + 1, :, 512:640].astype(F32)
        total[0:64, at] = jnp.where(lane < 64, a, pltpu.roll(b, 64, 1))
        total[64:128, at] = jnp.where(lane < 64, pltpu.roll(a, 64, 1), b)
    x = states[...].astype(F32)
    inverse = lax.rsqrt(jnp.mean(x * x, axis=-1, keepdims=True) + EPSILON)
    unit = x * inverse
    g = total[...] * gain[...].reshape(1, D)
    g = g - unit * jnp.mean(g * unit, axis=-1, keepdims=True)
    out[...] = (grads[...].astype(F32) + inverse * g).astype(BF16)


def moved_by(array, axis, step):
    count = lax.axis_size(axis)
    return lax.ppermute(array, axis, [(k, (k + step) % count) for k in range(count)])


def on_device(
    states, out_grad, doc_keys, doc_values, norm_gain, expert_ids, gate_values, expert_weights
):
    states, grads, keys, values = states[0], out_grad[0], doc_keys[0], doc_values[0]
    y, x = lax.axis_index("ctx_0"), lax.axis_index("ctx_1")
    place = (2 * y + x).astype(jnp.int32).reshape(1)
    normed, send, even, odd = call(
        route_kernel,
        [SMEM] + [VMEM] * 5,
        [shape((TOKENS, D)), shape((ROWS, HALF)), shape((ROWS, TOKENS)), shape((ROWS, TOKENS))],
        flops=2 * 4 * ROWS * TOKENS * HALF,
        moved=3 * 2**20,
        limit=VMEM_ALL,
    )(place, states, grads, norm_gain, expert_ids[0].T, gate_values[0].T)
    own = lax.all_to_all(
        send.reshape(EXPERTS, 8, HALF), "exp", split_axis=0, concat_axis=0, tiled=True
    ).reshape(ROWS, HALF)

    weights, slopes, stats = call(
        scores_kernel,
        [VMEM] * 4,
        [shape((HEADS, KEYS, TOKENS), F32), shape((HEADS, KEYS, TOKENS), F32), shape((72, TOKENS), F32)],
        flops=2 * 2 * KEYS * TOKENS * D,
        moved=5 * 2**20,
    )(normed, grads, keys, values)
    near = merged([stats] + [moved_by(stats, "ctx_0", k) for k in (1, 2, 3)])
    far = moved_by(near, "ctx_1", 1)
    up, down = moved_by(own, "ctx_0", 1), moved_by(own, "ctx_0", 3)
    partner = moved_by(own, "ctx_1", 1)
    across = [moved_by(up[:128], "ctx_0", 1), moved_by(down[128:], "ctx_0", 3)]
    partner_up, partner_down = moved_by(partner, "ctx_0", 1), moved_by(partner, "ctx_0", 3)
    partner_across = [moved_by(piece, "ctx_1", 1) for piece in across]
    w_in, w_out = expert_weights[0, :, 0, :], expert_weights[0, :, 1, :]
    places = [(0, 0), (-1, 0), (1, 0), (0, 1), (-1, 1), (1, 1), (2, 0), (2, 1)]
    at = jnp.stack([2 * ((y + a + 4) % 4) + (x + b) % 2 for a, b in places]).astype(jnp.int32)
    kept = [shape((SLOTS, D))] * 2 + [shape((SLOTS, UNITS))] * 2
    ready, far = lax.optimization_barrier((partner, far))
    early_sums, *early = call(
        early_kernel,
        [VMEM] * 6,
        [shape((CTX_COUNT, SLOTS // 2, CHUNK)), *kept],
        flops=2 * 3 * SLOTS * UNITS * D,
        moved=8 * 2**20,
        limit=VMEM_ALL,
    )(own, up, down, ready, w_in, w_out)
    sums, *late = call(
        late_kernel,
        [SMEM] + [ANY] * 9,
        [shape((CTX_COUNT, ROWS, CHUNK)), *kept],
        [
            *[pltpu.VMEM((ROWS, HALF), BF16)] * 4,
            *[pltpu.VMEM((UNITS, D), BF16)] * 2,
            pltpu.VMEM((CTX_COUNT, ROWS, CHUNK), BF16),
            *[pltpu.VMEM(k.shape, BF16) for k in kept],
            pltpu.SemaphoreType.DMA((12,)),
            pltpu.SemaphoreType.DMA((4 + CTX_COUNT,)),
        ],
        flops=2 * 3 * SLOTS * UNITS * D,
        moved=12 * 2**20,
        places=[ANY] * 5,
        limit=VMEM_ALL,
    )(at, partner_up, partner_down, *across, *partner_across, w_in, w_out, early_sums)
    parts = lax.all_to_all(sums, CTX, split_axis=0, concat_axis=0, tiled=True)
    keys_grad, values_grad, query_pack = call(
        score_grad_kernel,
        [SMEM] + [VMEM] * 8,
        [shape((KEYS, D)), shape((KEYS, D)), shape((2, 4, 64, CHUNK))],
        [pltpu.VMEM((TOKENS, D), F32)],
        flops=3 * 2 * KEYS * TOKENS * D,
        moved=6 * 2**20,
        limit=VMEM_ALL,
    )(place, normed, grads, keys, weights, slopes, stats, near, far)
    [weights_grad] = call(
        weights_kernel,
        [ANY] * 8,
        [shape((2 * UNITS, D))],
        [pltpu.VMEM(k.shape, BF16) for k in (*kept, *kept)] + [pltpu.SemaphoreType.DMA((8,))],
        flops=2 * 4 * SLOTS * UNITS * D,
        moved=8 * 2**20,
        limit=VMEM_ALL,
    )(*early, *late)
    weights_grad = weights_grad.reshape(1, UNITS, 2, D)
    far_query = moved_by(query_pack[0], "ctx_1", 1)
    parts, weights_grad = lax.optimization_barrier((parts, weights_grad))
    [back] = call(total_kernel, [VMEM], [shape((ROWS, CHUNK))], moved=3 * 2**20)(parts)
    back, far_query = lax.optimization_barrier((back, far_query))
    returned = lax.all_to_all(
        back.reshape(EXPERTS, 8, CHUNK), "exp", split_axis=0, concat_axis=0, tiled=True
    ).reshape(ROWS, CHUNK)
    queries = call(join_kernel, [VMEM] * 2, [shape((64, CHUNK))] * 4, moved=2**20)(query_pack, far_query)
    queries = [queries[0]] + [moved_by(queries[k], "ctx_0", k) for k in (1, 2, 3)]
    [total] = call(tokens_kernel, [VMEM] * 7, [shape((CTX_COUNT, 64, CHUNK))], moved=2**20)(
        returned, even, odd, *queries
    )
    packs = lax.all_to_all(total, CTX, split_axis=0, concat_axis=0, tiled=True)
    [states_grad] = call(
        norm_grad_kernel,
        [VMEM] * 4,
        [shape((TOKENS, D))],
        [pltpu.VMEM((TOKENS, D), F32)],
        moved=3 * 2**20,
    )(packs, states, grads, norm_gain)
    return states_grad[None], keys_grad[None], values_grad[None], weights_grad


def solution(mesh):
    finer = Mesh(mesh.devices.reshape(4, 2, mesh.shape["exp"]), (*CTX, "exp"))
    return jax.shard_map(
        on_device,
        mesh=finer,
        in_specs=(
            P("exp", None, None),
            P("exp", None, None),
            P("exp", CTX, None),
            P("exp", CTX, None),
            P(),
            P("exp", None, None),
            P("exp", None, None),
            P("exp", CTX, None, None),
        ),
        out_specs=(
            P("exp", None, None),
            P("exp", CTX, None),
            P("exp", CTX, None),
            P("exp", CTX, None, None),
        ),
        check_vma=False,
    )
```

```python
import math

import jax
import jax.numpy as jnp
from jax import lax
from jax.experimental import pallas as pl
from jax.experimental.pallas import tpu as pltpu
from jax.sharding import Mesh
from jax.sharding import PartitionSpec as P

HEADS = 20
HEAD = 128
D = 2560
HALF = 1280
TOKENS = 128
KEYS = 128
UNITS = 256
EXPERTS = 32
CTX_COUNT = 8
ROWS = 256
SLOTS = 256
CHUNK = 640
CTX = ("ctx_0", "ctx_1")
EPSILON = 1e-05
SCALE = HEAD**-0.5
BF16 = jnp.bfloat16
F32 = jnp.float32
VMEM_LIMIT = 24 * 2**20
VMEM_ALL = 60 * 2**20

VMEM = pl.BlockSpec(memory_space=pltpu.VMEM)
SMEM = pl.BlockSpec(memory_space=pltpu.SMEM)
ANY = pl.BlockSpec(memory_space=pl.ANY)


def call(kernel, ins, outs, scratch=(), flops=0, moved=0, places=None, limit=VMEM_LIMIT):
    return pl.pallas_call(
        kernel,
        in_specs=ins,
        out_specs=places or [VMEM] * len(outs),
        out_shape=outs,
        scratch_shapes=list(scratch),
        compiler_params=pltpu.CompilerParams(vmem_limit_bytes=limit),
        cost_estimate=pl.CostEstimate(flops=flops, bytes_accessed=moved, transcendentals=0),
    )


def shape(dims, dtype=BF16):
    return jax.ShapeDtypeStruct(dims, dtype)


def dot(a, b, dims=((1,), (0,))):
    return lax.dot_general(a, b, (dims, ((), ())), preferred_element_type=F32)


def iota(dims, axis):
    return lax.broadcasted_iota(jnp.int32, dims, axis)


def one(mask):
    return jnp.where(mask, 1.0, 0.0).astype(BF16)


def route_kernel(place, states, grads, gain, ids, gates, normed_out, send, even, odd):
    c = place[0]
    x = states[...].astype(F32)
    inverse = lax.rsqrt(jnp.mean(x * x, axis=-1, keepdims=True) + EPSILON)
    normed_out[...] = (x * inverse * gain[...].reshape(1, D)).astype(BF16)
    expert = iota((ROWS, TOKENS), 0) // 8
    i = iota((ROWS, TOKENS), 0) % 8
    first = ids[0:1, :] == expert
    second = ids[1:2, :] == expert
    named = first | second
    before = one(iota((TOKENS, TOKENS), 0) < iota((TOKENS, TOKENS), 1))
    slot = dot(one(named), before).astype(jnp.int32)
    slot = jnp.where(named, slot, -1)
    even[...] = one(slot == 2 * i)
    odd[...] = one(slot == 2 * i + 1)
    mine = slot == 2 * c + i % 2
    gate = jnp.where(first, gates[0:1, :], 0.0) + jnp.where(second, gates[1:2, :], 0.0)
    gate = jnp.sum(jnp.where(mine, gate, 0.0), axis=1, keepdims=True)
    low = i < 4
    is_row = (i // 2) % 2 == 0
    row_low = one(mine & low & is_row)
    row_high = one(mine & (~low) & is_row)
    grad_low = one(mine & low & (~is_row))
    grad_high = one(mine & (~low) & (~is_row))
    rows = dot(row_low, normed_out[:, :HALF]) + dot(row_high, normed_out[:, HALF:])
    douts = dot(grad_low, grads[:, :HALF]) + dot(grad_high, grads[:, HALF:])
    send[...] = (rows + gate * douts).astype(BF16)


def scores_kernel(normed, grads, keys, values, weights_out, slopes_out, stats):
    for h in range(HEADS):
        at = slice(h * HEAD, (h + 1) * HEAD)
        s = dot(keys[:, at], normed[:, at], ((1,), (1,))) * SCALE
        peak = jnp.max(s, axis=0, keepdims=True)
        w = jnp.exp(s - peak)
        slopes = dot(values[:, at], grads[:, at], ((1,), (1,)))
        weights_out[h] = w
        slopes_out[h] = slopes
        stats[h : h + 1, :] = peak
        stats[24 + h : 25 + h, :] = jnp.sum(w, axis=0, keepdims=True)
        stats[48 + h : 49 + h, :] = jnp.sum(w * slopes, axis=0, keepdims=True)
    for part in range(3):
        at = 24 * part + HEADS
        stats[at : at + 4, :] = jnp.zeros((4, TOKENS), F32)


def merged(stats):
    peak = stats[0][:24]
    for one_side in stats[1:]:
        peak = jnp.maximum(peak, one_side[:24])
    total = inner = 0.0
    for one_side in stats:
        factor = jnp.exp(one_side[:24] - peak)
        total = total + one_side[24:48] * factor
        inner = inner + one_side[48:] * factor
    return jnp.concatenate([peak, total, inner], axis=0)


def score_grad_kernel(
    place,
    normed,
    grads,
    keys,
    weights,
    slopes,
    local,
    near,
    far,
    keys_grad,
    values_grad,
    own_pack,
    far_pack,
    query,
):
    peak = jnp.maximum(near[0:24, :], far[0:24, :])
    near_factor = jnp.exp(near[0:24, :] - peak)
    far_factor = jnp.exp(far[0:24, :] - peak)
    total = near[24:48, :] * near_factor + far[24:48, :] * far_factor
    inner = near[48:72, :] * near_factor + far[48:72, :] * far_factor
    total = jnp.where(iota((24, TOKENS), 0) < HEADS, total, 1.0)
    factor = jnp.exp(local[0:24, :] - peak) / total
    delta = inner / total
    for h in range(HEADS):
        at = slice(h * HEAD, (h + 1) * HEAD)
        probs = weights[h] * factor[h : h + 1, :]
        score_grad = (probs * (slopes[h] - delta[h : h + 1, :])).astype(BF16)
        values_grad[:, at] = dot(probs.astype(BF16), grads[:, at]).astype(BF16)
        keys_grad[:, at] = (dot(score_grad, normed[:, at]) * SCALE).astype(BF16)
        query[:, at] = dot(score_grad, keys[:, at], ((0,), (0,))) * SCALE
    lane = iota((64, 128), 1)
    first = place[0] % 2 == 0
    for g in range(CTX_COUNT // 2):
        row = (g - place[0] // 2 + 4) % 4
        tile = slice(2048 + 128 * g, 2176 + 128 * g)
        a, b = query[0:64, tile], query[64:128, tile]
        packs = []
        for f, tail in (
            (2 * g, jnp.where(lane < 64, a, pltpu.roll(b, 64, 1))),
            (2 * g + 1, jnp.where(lane < 64, pltpu.roll(a, 64, 1), b)),
        ):
            at = slice(256 * f, 256 * f + 256)
            packs.append(jnp.concatenate([query[0:64, at], query[64:128, at], tail], axis=1))
        own_pack[row] = jnp.where(first, packs[0], packs[1]).astype(BF16)
        far_pack[row] = jnp.where(first, packs[1], packs[0]).astype(BF16)


def join_kernel(own, far, *outs):
    for k in range(4):
        outs[k][...] = (own[k].astype(F32) + far[k].astype(F32)).astype(BF16)


def experts_of(blocks, w_in, w_out, rows, douts, act, pre_grad, put, after=lambda step: None):
    to, source = iota((ROWS, ROWS), 0), iota((ROWS, ROWS), 1)
    order = one(source == 8 * (to % 32) + to // 32)
    for k, block in enumerate(blocks):
        sorted_rows = dot(order, block()).astype(BF16)
        for q in range(2):
            where = slice(128 * q + 32 * k, 128 * q + 32 * k + 32)
            for half in range(2):
                lanes = slice(HALF * half, HALF * half + HALF)
                first = 128 * half + 32 * q
                rows[where, lanes] = sorted_rows[first : first + 32, :]
                douts[where, lanes] = sorted_rows[first + 64 : first + 96, :]
    after("rows")
    v = dot(rows[...], w_in[...], ((1,), (1,)))
    act_grad = dot(douts[...], w_out[...], ((1,), (1,)))
    root = math.sqrt(2 / math.pi)
    square = v * v
    t = jnp.tanh(root * (v + 0.044715 * (square * v)))
    act[...] = (0.5 * v * (1.0 + t)).astype(BF16)
    slope = 0.5 * (1.0 + t) + 0.5 * v * (1.0 - t * t) * (root * (1.0 + 3 * 0.044715 * square))
    pre_grad[...] = (act_grad * slope).astype(BF16)
    after("units")
    tails = dot(pre_grad[...], w_in[:, 2048:2560])
    lane = iota((128, 128), 1)
    for f in range(CTX_COUNT):
        part = dot(pre_grad[...], w_in[:, 256 * f : 256 * f + 256])
        put(f, slice(0, 256), part[0:128].astype(BF16))
        put(f, slice(256, 512), part[128:256].astype(BF16))
        tile = slice(128 * (f // 2), 128 * (f // 2) + 128)
        a, b = tails[0:128, tile], tails[128:256, tile]
        if f % 2 == 0:
            tail = jnp.where(lane < 64, a, pltpu.roll(b, 64, 1))
        else:
            tail = jnp.where(lane < 64, pltpu.roll(a, 64, 1), b)
        put(f, slice(512, 640), tail.astype(BF16))
        after(f)


def early_kernel(own, up, down, partner, w_in, w_out, sums, rows, douts, act, pre_grad):
    def put(f, lanes, value):
        sums[f, :, lanes] = value

    blocks = [lambda s=s: s[...] for s in (own, up, down, partner)]
    experts_of(blocks, w_in, w_out, rows, douts, act, pre_grad, put)


def late_kernel(at_ref, *refs):
    given, results, held = refs[:9], refs[9:14], refs[14:]
    shards, (w_in, w_out), sums, kept = held[:4], held[4:6], held[6], held[7:11]
    arrived, left = held[11:]
    where = [pl.ds(pl.multiple_of(32 * at_ref[k], 32), 32) for k in range(CTX_COUNT)]
    landing = [
        *shards[:2],
        *(shards[k].at[128 * j : 128 * j + 128] for k in (2, 3) for j in range(2)),
        w_in,
        w_out,
    ]
    loads = [pltpu.make_async_copy(given[k], landing[k], arrived.at[k]) for k in range(8)]
    for load in loads:
        load.start()
    early = [
        pltpu.make_async_copy(
            given[8].at[:, 32 * k : 32 * k + 32, :], sums.at[:, where[k], :], arrived.at[8 + k]
        )
        for k in range(4)
    ]
    for load in early:
        load.start()
    stores = [pltpu.make_async_copy(kept[k], results[1 + k], left.at[k]) for k in range(4)]
    stores += [
        pltpu.make_async_copy(sums.at[f], results[0].at[f], left.at[4 + f])
        for f in range(CTX_COUNT)
    ]

    def block(k):
        for load in loads[k : k + 1] if k < 2 else loads[2 * k - 2 : 2 * k]:
            load.wait()
        return shards[k][...]

    def put(f, lanes, value):
        for k in range(4):
            sums[f, where[4 + k], lanes] = value[32 * k : 32 * k + 32]

    def after(step):
        if step == "rows":
            stores[0].start()
            stores[1].start()
            loads[6].wait()
            loads[7].wait()
        elif step == "units":
            stores[2].start()
            stores[3].start()
            for load in early:
                load.wait()
        else:
            stores[4 + step].start()

    blocks = [lambda k=k: block(k) for k in range(4)]
    experts_of(blocks, w_in, w_out, *kept, put, after)
    for store in stores:
        store.wait()


def weights_kernel(*refs):
    given, out, held, arrived = refs[:8], refs[8], refs[9:17], refs[17]
    loads = [pltpu.make_async_copy(given[k], held[k], arrived.at[k]) for k in range(8)]
    for load in loads:
        load.start()
    unit, column = iota((UNITS, 2 * UNITS), 0), iota((UNITS, 2 * UNITS), 1)
    even, odd = one(column == 2 * unit), one(column == 2 * unit + 1)
    for load in loads:
        load.wait()
    terms = []
    for rows, douts, act, pre_grad in (held[:4], held[4:]):
        terms.append((dot(pre_grad[...], even).astype(BF16), rows))
        terms.append((dot(act[...], odd).astype(BF16), douts))
    for n in range(D // 512):
        lanes = slice(512 * n, 512 * n + 512)
        out[:, lanes] = sum(dot(a, b[:, lanes], ((0,), (0,))) for a, b in terms).astype(BF16)


def total_kernel(parts, back):
    total = parts[0].astype(F32)
    for k in range(1, CTX_COUNT):
        total = total + parts[k].astype(F32)
    to, source = iota((ROWS, ROWS), 0), iota((ROWS, ROWS), 1)
    order = one(source == 32 * (to % 8) + to // 8)
    back[...] = dot(order, total.astype(BF16)).astype(BF16)


def tokens_kernel(returned, even, odd, own, below, across, above, out):
    query = (own[...].astype(F32) + across[...].astype(F32)) + (
        below[...].astype(F32) + above[...].astype(F32)
    )
    a = dot(even[...], returned[...], ((0,), (0,)))
    b = dot(odd[...], returned[...], ((0,), (0,)))
    wide = a[:, 0:256] + b[:, 256:512]
    tail = a[:, 512:640] + pltpu.roll(b[:, 512:640], 64, 1)
    lane = iota((64, 128), 1)
    tail = jnp.where(lane < 64, tail[0:64], pltpu.roll(tail[64:128], 64, 1))
    left = (wide[0:64] + query[:, 0:256]).astype(BF16)
    right = (wide[64:128] + query[:, 256:512]).astype(BF16)
    tail = (tail + query[:, 512:640]).astype(BF16)
    for f in range(CTX_COUNT):
        out[f, :, 0:256] = left
        out[f, :, 256:512] = right
        out[f, :, 512:640] = tail


def norm_grad_kernel(packs, states, grads, gain, out, total):
    for f in range(CTX_COUNT):
        at = slice(256 * f, 256 * f + 256)
        total[0:64, at] = packs[f, :, 0:256].astype(F32)
        total[64:128, at] = packs[f, :, 256:512].astype(F32)
    lane = iota((64, 128), 1)
    for g in range(CTX_COUNT // 2):
        at = slice(2048 + 128 * g, 2176 + 128 * g)
        a = packs[2 * g, :, 512:640].astype(F32)
        b = packs[2 * g + 1, :, 512:640].astype(F32)
        total[0:64, at] = jnp.where(lane < 64, a, pltpu.roll(b, 64, 1))
        total[64:128, at] = jnp.where(lane < 64, pltpu.roll(a, 64, 1), b)
    x = states[...].astype(F32)
    inverse = lax.rsqrt(jnp.mean(x * x, axis=-1, keepdims=True) + EPSILON)
    unit = x * inverse
    g = total[...] * gain[...].reshape(1, D)
    g = g - unit * jnp.mean(g * unit, axis=-1, keepdims=True)
    out[...] = (grads[...].astype(F32) + inverse * g).astype(BF16)


def moved_by(array, axis, step):
    count = lax.axis_size(axis)
    return lax.ppermute(array, axis, [(k, (k + step) % count) for k in range(count)])


def on_device(
    states, out_grad, doc_keys, doc_values, norm_gain, expert_ids, gate_values, expert_weights
):
    states, grads, keys, values = states[0], out_grad[0], doc_keys[0], doc_values[0]
    y, x = lax.axis_index("ctx_0"), lax.axis_index("ctx_1")
    place = (2 * y + x).astype(jnp.int32).reshape(1)
    normed, send, even, odd = call(
        route_kernel,
        [SMEM] + [VMEM] * 5,
        [shape((TOKENS, D)), shape((ROWS, HALF)), shape((ROWS, TOKENS)), shape((ROWS, TOKENS))],
        flops=2 * 4 * ROWS * TOKENS * HALF,
        moved=3 * 2**20,
        limit=VMEM_ALL,
    )(place, states, grads, norm_gain, expert_ids[0].T, gate_values[0].T)
    own = lax.all_to_all(
        send.reshape(EXPERTS, 8, HALF), "exp", split_axis=0, concat_axis=0, tiled=True
    ).reshape(ROWS, HALF)

    normed, expert_weights = lax.optimization_barrier((normed, expert_weights))
    w_in, w_out = expert_weights[0, :, 0, :], expert_weights[0, :, 1, :]
    keys, w_in, w_out = lax.optimization_barrier((keys, w_in, w_out))

    weights, slopes, stats = call(
        scores_kernel,
        [VMEM] * 4,
        [shape((HEADS, KEYS, TOKENS), F32), shape((HEADS, KEYS, TOKENS), F32), shape((72, TOKENS), F32)],
        flops=2 * 2 * KEYS * TOKENS * D,
        moved=5 * 2**20,
    )(normed, grads, keys, values)
    near = merged([stats] + [moved_by(stats, "ctx_0", k) for k in (1, 2, 3)])
    own, near = lax.optimization_barrier((own, near))
    far = moved_by(near, "ctx_1", 1)
    up, down = moved_by(own, "ctx_0", 1), moved_by(own, "ctx_0", 3)
    after_far, far = lax.optimization_barrier((own, far))
    partner = moved_by(after_far, "ctx_1", 1)
    keys_grad, values_grad, own_pack, far_pack = call(
        score_grad_kernel,
        [SMEM] + [VMEM] * 8,
        [shape((KEYS, D)), shape((KEYS, D)), *[shape((4, 64, CHUNK))] * 2],
        [pltpu.VMEM((TOKENS, D), F32)],
        flops=3 * 2 * KEYS * TOKENS * D,
        moved=6 * 2**20,
        limit=VMEM_ALL,
    )(place, normed, grads, keys, weights, slopes, stats, near, far)
    up, down, far_pack = lax.optimization_barrier((up, down, far_pack))
    across = [moved_by(up[:128], "ctx_0", 1), moved_by(down[128:], "ctx_0", 3)]
    partner_up, partner_down = moved_by(partner, "ctx_0", 1), moved_by(partner, "ctx_0", 3)
    partner_across = [moved_by(piece, "ctx_1", 1) for piece in across]
    places = [(0, 0), (-1, 0), (1, 0), (0, 1), (-1, 1), (1, 1), (2, 0), (2, 1)]
    at = jnp.stack([2 * ((y + a + 4) % 4) + (x + b) % 2 for a, b in places]).astype(jnp.int32)
    kept = [shape((SLOTS, D))] * 2 + [shape((SLOTS, UNITS))] * 2
    early_sums, *early = call(
        early_kernel,
        [VMEM] * 6,
        [shape((CTX_COUNT, SLOTS // 2, CHUNK)), *kept],
        flops=2 * 3 * SLOTS * UNITS * D,
        moved=8 * 2**20,
        limit=VMEM_ALL,
    )(own, up, down, partner, w_in, w_out)
    early_sums, far_pack = lax.optimization_barrier((early_sums, far_pack))
    far_query = moved_by(far_pack, "ctx_1", 1)
    sums, *late = call(
        late_kernel,
        [SMEM] + [ANY] * 9,
        [shape((CTX_COUNT, ROWS, CHUNK)), *kept],
        [
            *[pltpu.VMEM((ROWS, HALF), BF16)] * 4,
            *[pltpu.VMEM((UNITS, D), BF16)] * 2,
            pltpu.VMEM((CTX_COUNT, ROWS, CHUNK), BF16),
            *[pltpu.VMEM(k.shape, BF16) for k in kept],
            pltpu.SemaphoreType.DMA((12,)),
            pltpu.SemaphoreType.DMA((4 + CTX_COUNT,)),
        ],
        flops=2 * 3 * SLOTS * UNITS * D,
        moved=12 * 2**20,
        places=[ANY] * 5,
        limit=VMEM_ALL,
    )(at, partner_up, partner_down, *across, *partner_across, w_in, w_out, early_sums)
    sums, far_query = lax.optimization_barrier((sums, far_query))
    parts = lax.all_to_all(sums, CTX, split_axis=0, concat_axis=0, tiled=True)
    [weights_grad] = call(
        weights_kernel,
        [ANY] * 8,
        [shape((2 * UNITS, D))],
        [pltpu.VMEM(k.shape, BF16) for k in (*kept, *kept)] + [pltpu.SemaphoreType.DMA((8,))],
        flops=2 * 4 * SLOTS * UNITS * D,
        moved=8 * 2**20,
        limit=VMEM_ALL,
    )(*early, *late)
    weights_grad = weights_grad.reshape(1, UNITS, 2, D)
    parts, weights_grad = lax.optimization_barrier((parts, weights_grad))
    [back] = call(total_kernel, [VMEM], [shape((ROWS, CHUNK))], moved=3 * 2**20)(parts)
    back, far_query = lax.optimization_barrier((back, far_query))
    returned = lax.all_to_all(
        back.reshape(EXPERTS, 8, CHUNK), "exp", split_axis=0, concat_axis=0, tiled=True
    ).reshape(ROWS, CHUNK)
    queries = call(join_kernel, [VMEM] * 2, [shape((64, CHUNK))] * 4, moved=2**20)(own_pack, far_query)
    queries = [queries[0]] + [moved_by(queries[k], "ctx_0", k) for k in (1, 2, 3)]
    [total] = call(tokens_kernel, [VMEM] * 7, [shape((CTX_COUNT, 64, CHUNK))], moved=2**20)(
        returned, even, odd, *queries
    )
    packs = lax.all_to_all(total, CTX, split_axis=0, concat_axis=0, tiled=True)
    [states_grad] = call(
        norm_grad_kernel,
        [VMEM] * 4,
        [shape((TOKENS, D))],
        [pltpu.VMEM((TOKENS, D), F32)],
        moved=3 * 2**20,
    )(packs, states, grads, norm_gain)
    return states_grad[None], keys_grad[None], values_grad[None], weights_grad


def solution(mesh):
    finer = Mesh(mesh.devices.reshape(4, 2, mesh.shape["exp"]), (*CTX, "exp"))
    return jax.shard_map(
        on_device,
        mesh=finer,
        in_specs=(
            P("exp", None, None),
            P("exp", None, None),
            P("exp", CTX, None),
            P("exp", CTX, None),
            P(),
            P("exp", None, None),
            P("exp", None, None),
            P("exp", CTX, None, None),
        ),
        out_specs=(
            P("exp", None, None),
            P("exp", CTX, None),
            P("exp", CTX, None),
            P("exp", CTX, None, None),
        ),
        check_vma=False,
    )
```

```python
import math

import jax
import jax.numpy as jnp
from jax import lax
from jax.experimental import pallas as pl
from jax.experimental.pallas import tpu as pltpu
from jax.sharding import Mesh
from jax.sharding import PartitionSpec as P

HEADS = 20
HEAD = 128
D = 2560
HALF = 1280
TOKENS = 128
KEYS = 128
UNITS = 256
EXPERTS = 32
CTX_COUNT = 8
ROWS = 256
SLOTS = 256
CHUNK = 640
CTX = ("ctx_0", "ctx_1")
EPSILON = 1e-05
SCALE = HEAD**-0.5
BF16 = jnp.bfloat16
F32 = jnp.float32
VMEM_LIMIT = 24 * 2**20
VMEM_ALL = 60 * 2**20

VMEM = pl.BlockSpec(memory_space=pltpu.VMEM)
SMEM = pl.BlockSpec(memory_space=pltpu.SMEM)
ANY = pl.BlockSpec(memory_space=pl.ANY)


def call(kernel, ins, outs, scratch=(), flops=0, moved=0, places=None, limit=VMEM_LIMIT):
    return pl.pallas_call(
        kernel,
        in_specs=ins,
        out_specs=places or [VMEM] * len(outs),
        out_shape=outs,
        scratch_shapes=list(scratch),
        compiler_params=pltpu.CompilerParams(vmem_limit_bytes=limit),
        cost_estimate=pl.CostEstimate(flops=flops, bytes_accessed=moved, transcendentals=0),
    )


def shape(dims, dtype=BF16):
    return jax.ShapeDtypeStruct(dims, dtype)


def dot(a, b, dims=((1,), (0,))):
    return lax.dot_general(a, b, (dims, ((), ())), preferred_element_type=F32)


def iota(dims, axis):
    return lax.broadcasted_iota(jnp.int32, dims, axis)


def one(mask):
    return jnp.where(mask, 1.0, 0.0).astype(BF16)


def route_kernel(place, states, grads, gain, ids, gates, normed_out, send, even, odd):
    c = place[0]
    x = states[...].astype(F32)
    inverse = lax.rsqrt(jnp.mean(x * x, axis=-1, keepdims=True) + EPSILON)
    normed_out[...] = (x * inverse * gain[...].reshape(1, D)).astype(BF16)
    expert = iota((ROWS, TOKENS), 0) // 8
    i = iota((ROWS, TOKENS), 0) % 8
    first = ids[0:1, :] == expert
    second = ids[1:2, :] == expert
    named = first | second
    before = one(iota((TOKENS, TOKENS), 0) < iota((TOKENS, TOKENS), 1))
    slot = dot(one(named), before).astype(jnp.int32)
    slot = jnp.where(named, slot, -1)
    even[...] = one(slot == 2 * i)
    odd[...] = one(slot == 2 * i + 1)
    mine = slot == 2 * c + i % 2
    gate = jnp.where(first, gates[0:1, :], 0.0) + jnp.where(second, gates[1:2, :], 0.0)
    gate = jnp.sum(jnp.where(mine, gate, 0.0), axis=1, keepdims=True)
    low = i < 4
    is_row = (i // 2) % 2 == 0
    row_low = one(mine & low & is_row)
    row_high = one(mine & (~low) & is_row)
    grad_low = one(mine & low & (~is_row))
    grad_high = one(mine & (~low) & (~is_row))
    rows = dot(row_low, normed_out[:, :HALF]) + dot(row_high, normed_out[:, HALF:])
    douts = dot(grad_low, grads[:, :HALF]) + dot(grad_high, grads[:, HALF:])
    send[...] = (rows + gate * douts).astype(BF16)


def scores_kernel(normed, grads, keys, values, weights_out, slopes_out, stats):
    for h in range(HEADS):
        at = slice(h * HEAD, (h + 1) * HEAD)
        s = dot(keys[:, at], normed[:, at], ((1,), (1,))) * SCALE
        peak = jnp.max(s, axis=0, keepdims=True)
        w = jnp.exp(s - peak)
        slopes = dot(values[:, at], grads[:, at], ((1,), (1,)))
        weights_out[h] = w
        slopes_out[h] = slopes
        stats[h : h + 1, :] = peak
        stats[24 + h : 25 + h, :] = jnp.sum(w, axis=0, keepdims=True)
        stats[48 + h : 49 + h, :] = jnp.sum(w * slopes, axis=0, keepdims=True)
    for part in range(3):
        at = 24 * part + HEADS
        stats[at : at + 4, :] = jnp.zeros((4, TOKENS), F32)


def merged(stats):
    peak = stats[0][:24]
    for one_side in stats[1:]:
        peak = jnp.maximum(peak, one_side[:24])
    total = inner = 0.0
    for one_side in stats:
        factor = jnp.exp(one_side[:24] - peak)
        total = total + one_side[24:48] * factor
        inner = inner + one_side[48:] * factor
    return jnp.concatenate([peak, total, inner], axis=0)


def score_grad_kernel(
    place,
    normed,
    grads,
    keys,
    weights,
    slopes,
    local,
    near,
    far,
    keys_grad,
    values_grad,
    own_pack,
    far_pack,
    query,
):
    peak = jnp.maximum(near[0:24, :], far[0:24, :])
    near_factor = jnp.exp(near[0:24, :] - peak)
    far_factor = jnp.exp(far[0:24, :] - peak)
    total = near[24:48, :] * near_factor + far[24:48, :] * far_factor
    inner = near[48:72, :] * near_factor + far[48:72, :] * far_factor
    total = jnp.where(iota((24, TOKENS), 0) < HEADS, total, 1.0)
    factor = jnp.exp(local[0:24, :] - peak) / total
    delta = inner / total
    for h in range(HEADS):
        at = slice(h * HEAD, (h + 1) * HEAD)
        probs = weights[h] * factor[h : h + 1, :]
        score_grad = (probs * (slopes[h] - delta[h : h + 1, :])).astype(BF16)
        values_grad[:, at] = dot(probs.astype(BF16), grads[:, at]).astype(BF16)
        keys_grad[:, at] = (dot(score_grad, normed[:, at]) * SCALE).astype(BF16)
        query[:, at] = dot(score_grad, keys[:, at], ((0,), (0,))) * SCALE
    lane = iota((64, 128), 1)
    first = place[0] % 2 == 0
    for g in range(CTX_COUNT // 2):
        row = (g - place[0] // 2 + 4) % 4
        tile = slice(2048 + 128 * g, 2176 + 128 * g)
        a, b = query[0:64, tile], query[64:128, tile]
        packs = []
        for f, tail in (
            (2 * g, jnp.where(lane < 64, a, pltpu.roll(b, 64, 1))),
            (2 * g + 1, jnp.where(lane < 64, pltpu.roll(a, 64, 1), b)),
        ):
            at = slice(256 * f, 256 * f + 256)
            packs.append(jnp.concatenate([query[0:64, at], query[64:128, at], tail], axis=1))
        own_pack[row] = jnp.where(first, packs[0], packs[1]).astype(BF16)
        far_pack[row] = jnp.where(first, packs[1], packs[0]).astype(BF16)


def join_kernel(own, far, *outs):
    for k in range(4):
        outs[k][...] = (own[k].astype(F32) + far[k].astype(F32)).astype(BF16)


def experts_of(blocks, w_in, w_out, rows, douts, act, pre_grad, put, after=lambda step: None):
    to, source = iota((ROWS, ROWS), 0), iota((ROWS, ROWS), 1)
    order = one(source == 8 * (to % 32) + to // 32)
    for k, block in enumerate(blocks):
        sorted_rows = dot(order, block()).astype(BF16)
        for q in range(2):
            where = slice(128 * q + 32 * k, 128 * q + 32 * k + 32)
            for half in range(2):
                lanes = slice(HALF * half, HALF * half + HALF)
                first = 128 * half + 32 * q
                rows[where, lanes] = sorted_rows[first : first + 32, :]
                douts[where, lanes] = sorted_rows[first + 64 : first + 96, :]
    after("rows")
    v = dot(rows[...], w_in[...], ((1,), (1,)))
    act_grad = dot(douts[...], w_out[...], ((1,), (1,)))
    root = math.sqrt(2 / math.pi)
    square = v * v
    t = jnp.tanh(root * (v + 0.044715 * (square * v)))
    act[...] = (0.5 * v * (1.0 + t)).astype(BF16)
    slope = 0.5 * (1.0 + t) + 0.5 * v * (1.0 - t * t) * (root * (1.0 + 3 * 0.044715 * square))
    pre_grad[...] = (act_grad * slope).astype(BF16)
    after("units")
    tails = dot(pre_grad[...], w_in[:, 2048:2560])
    lane = iota((128, 128), 1)
    for f in range(CTX_COUNT):
        part = dot(pre_grad[...], w_in[:, 256 * f : 256 * f + 256])
        put(f, slice(0, 256), part[0:128].astype(BF16))
        put(f, slice(256, 512), part[128:256].astype(BF16))
        tile = slice(128 * (f // 2), 128 * (f // 2) + 128)
        a, b = tails[0:128, tile], tails[128:256, tile]
        if f % 2 == 0:
            tail = jnp.where(lane < 64, a, pltpu.roll(b, 64, 1))
        else:
            tail = jnp.where(lane < 64, pltpu.roll(a, 64, 1), b)
        put(f, slice(512, 640), tail.astype(BF16))
        after(f)


def early_kernel(*refs):
    own, up, up_rest, down_rest, down, partner, w_in, w_out, sums = refs[:9]

    def put(f, lanes, value):
        sums[f, :, lanes] = value

    blocks = [
        lambda: own[...],
        lambda: jnp.concatenate([up[...], up_rest[...]], axis=0),
        lambda: jnp.concatenate([down_rest[...], down[...]], axis=0),
        lambda: partner[...],
    ]
    experts_of(blocks, w_in, w_out, *refs[9:], put)


def late_kernel(at_ref, *refs):
    given, results, held = refs[:9], refs[9:14], refs[14:]
    shards, (w_in, w_out), sums, kept = held[:4], held[4:6], held[6], held[7:11]
    arrived, left = held[11:]
    where = [pl.ds(pl.multiple_of(32 * at_ref[k], 32), 32) for k in range(CTX_COUNT)]
    landing = [
        *shards[:2],
        *(shards[k].at[128 * j : 128 * j + 128] for k in (2, 3) for j in range(2)),
        w_in,
        w_out,
    ]
    loads = [pltpu.make_async_copy(given[k], landing[k], arrived.at[k]) for k in range(8)]
    for load in loads:
        load.start()
    early = [
        pltpu.make_async_copy(
            given[8].at[:, 32 * k : 32 * k + 32, :], sums.at[:, where[k], :], arrived.at[8 + k]
        )
        for k in range(4)
    ]
    for load in early:
        load.start()
    stores = [pltpu.make_async_copy(kept[k], results[1 + k], left.at[k]) for k in range(4)]
    stores += [
        pltpu.make_async_copy(sums.at[f], results[0].at[f], left.at[4 + f])
        for f in range(CTX_COUNT)
    ]

    def block(k):
        for load in loads[k : k + 1] if k < 2 else loads[2 * k - 2 : 2 * k]:
            load.wait()
        return shards[k][...]

    def put(f, lanes, value):
        for k in range(4):
            sums[f, where[4 + k], lanes] = value[32 * k : 32 * k + 32]

    def after(step):
        if step == "rows":
            stores[0].start()
            stores[1].start()
            loads[6].wait()
            loads[7].wait()
        elif step == "units":
            stores[2].start()
            stores[3].start()
            for load in early:
                load.wait()
        else:
            stores[4 + step].start()

    blocks = [lambda k=k: block(k) for k in range(4)]
    experts_of(blocks, w_in, w_out, *kept, put, after)
    for store in stores:
        store.wait()


def weights_kernel(*refs):
    given, out, held, arrived = refs[:8], refs[8], refs[9:17], refs[17]
    loads = [pltpu.make_async_copy(given[k], held[k], arrived.at[k]) for k in range(8)]
    for load in loads:
        load.start()
    unit, column = iota((UNITS, 2 * UNITS), 0), iota((UNITS, 2 * UNITS), 1)
    even, odd = one(column == 2 * unit), one(column == 2 * unit + 1)
    for load in loads:
        load.wait()
    terms = []
    for rows, douts, act, pre_grad in (held[:4], held[4:]):
        terms.append((dot(pre_grad[...], even).astype(BF16), rows))
        terms.append((dot(act[...], odd).astype(BF16), douts))
    for n in range(D // 512):
        lanes = slice(512 * n, 512 * n + 512)
        out[:, lanes] = sum(dot(a, b[:, lanes], ((0,), (0,))) for a, b in terms).astype(BF16)


def total_kernel(parts, back):
    total = parts[0].astype(F32)
    for k in range(1, CTX_COUNT):
        total = total + parts[k].astype(F32)
    to, source = iota((ROWS, ROWS), 0), iota((ROWS, ROWS), 1)
    order = one(source == 32 * (to % 8) + to // 8)
    back[...] = dot(order, total.astype(BF16)).astype(BF16)


def tokens_kernel(returned, even, odd, own, below, across, above, out):
    query = (own[...].astype(F32) + across[...].astype(F32)) + (
        below[...].astype(F32) + above[...].astype(F32)
    )
    a = dot(even[...], returned[...], ((0,), (0,)))
    b = dot(odd[...], returned[...], ((0,), (0,)))
    wide = a[:, 0:256] + b[:, 256:512]
    tail = a[:, 512:640] + pltpu.roll(b[:, 512:640], 64, 1)
    lane = iota((64, 128), 1)
    tail = jnp.where(lane < 64, tail[0:64], pltpu.roll(tail[64:128], 64, 1))
    left = (wide[0:64] + query[:, 0:256]).astype(BF16)
    right = (wide[64:128] + query[:, 256:512]).astype(BF16)
    tail = (tail + query[:, 512:640]).astype(BF16)
    for f in range(CTX_COUNT):
        out[f, :, 0:256] = left
        out[f, :, 256:512] = right
        out[f, :, 512:640] = tail


def norm_grad_kernel(packs, states, grads, gain, out, total):
    for f in range(CTX_COUNT):
        at = slice(256 * f, 256 * f + 256)
        total[0:64, at] = packs[f, :, 0:256].astype(F32)
        total[64:128, at] = packs[f, :, 256:512].astype(F32)
    lane = iota((64, 128), 1)
    for g in range(CTX_COUNT // 2):
        at = slice(2048 + 128 * g, 2176 + 128 * g)
        a = packs[2 * g, :, 512:640].astype(F32)
        b = packs[2 * g + 1, :, 512:640].astype(F32)
        total[0:64, at] = jnp.where(lane < 64, a, pltpu.roll(b, 64, 1))
        total[64:128, at] = jnp.where(lane < 64, pltpu.roll(a, 64, 1), b)
    x = states[...].astype(F32)
    inverse = lax.rsqrt(jnp.mean(x * x, axis=-1, keepdims=True) + EPSILON)
    unit = x * inverse
    g = total[...] * gain[...].reshape(1, D)
    g = g - unit * jnp.mean(g * unit, axis=-1, keepdims=True)
    out[...] = (grads[...].astype(F32) + inverse * g).astype(BF16)


def moved_by(array, axis, step):
    count = lax.axis_size(axis)
    return lax.ppermute(array, axis, [(k, (k + step) % count) for k in range(count)])


def on_device(
    states, out_grad, doc_keys, doc_values, norm_gain, expert_ids, gate_values, expert_weights
):
    states, grads, keys, values = states[0], out_grad[0], doc_keys[0], doc_values[0]
    y, x = lax.axis_index("ctx_0"), lax.axis_index("ctx_1")
    place = (2 * y + x).astype(jnp.int32).reshape(1)
    normed, send, even, odd = call(
        route_kernel,
        [SMEM] + [VMEM] * 5,
        [shape((TOKENS, D)), shape((ROWS, HALF)), shape((ROWS, TOKENS)), shape((ROWS, TOKENS))],
        flops=2 * 4 * ROWS * TOKENS * HALF,
        moved=3 * 2**20,
        limit=VMEM_ALL,
    )(place, states, grads, norm_gain, expert_ids[0].T, gate_values[0].T)
    own = lax.all_to_all(
        send.reshape(EXPERTS, 8, HALF), "exp", split_axis=0, concat_axis=0, tiled=True
    ).reshape(ROWS, HALF)

    normed, expert_weights = lax.optimization_barrier((normed, expert_weights))
    w_in, w_out = expert_weights[0, :, 0, :], expert_weights[0, :, 1, :]
    keys, w_in, w_out = lax.optimization_barrier((keys, w_in, w_out))

    weights, slopes, stats = call(
        scores_kernel,
        [VMEM] * 4,
        [shape((HEADS, KEYS, TOKENS), F32), shape((HEADS, KEYS, TOKENS), F32), shape((72, TOKENS), F32)],
        flops=2 * 2 * KEYS * TOKENS * D,
        moved=5 * 2**20,
    )(normed, grads, keys, values)
    near = merged([stats] + [moved_by(stats, "ctx_0", k) for k in (1, 2, 3)])
    far = moved_by(near, "ctx_1", 1)
    own, near, far = lax.optimization_barrier((own, near, far))
    low, high = own[:128], own[128:]
    up, down = moved_by(low, "ctx_0", 1), moved_by(high, "ctx_0", 3)
    up_rest, down_rest = moved_by(high, "ctx_0", 1), moved_by(low, "ctx_0", 3)
    partner = moved_by(own, "ctx_1", 1)
    keys_grad, values_grad, own_pack, far_pack = call(
        score_grad_kernel,
        [SMEM] + [VMEM] * 8,
        [shape((KEYS, D)), shape((KEYS, D)), *[shape((4, 64, CHUNK))] * 2],
        [pltpu.VMEM((TOKENS, D), F32)],
        flops=3 * 2 * KEYS * TOKENS * D,
        moved=6 * 2**20,
        limit=VMEM_ALL,
    )(place, normed, grads, keys, weights, slopes, stats, near, far)
    up, down, far_pack = lax.optimization_barrier((up, down, far_pack))
    across = [moved_by(up, "ctx_0", 1), moved_by(down, "ctx_0", 3)]
    partner_up, partner_down = moved_by(partner, "ctx_0", 1), moved_by(partner, "ctx_0", 3)
    partner_across = [moved_by(piece, "ctx_1", 1) for piece in across]
    places = [(0, 0), (-1, 0), (1, 0), (0, 1), (-1, 1), (1, 1), (2, 0), (2, 1)]
    at = jnp.stack([2 * ((y + a + 4) % 4) + (x + b) % 2 for a, b in places]).astype(jnp.int32)
    kept = [shape((SLOTS, D))] * 2 + [shape((SLOTS, UNITS))] * 2
    early_sums, *early = call(
        early_kernel,
        [VMEM] * 8,
        [shape((CTX_COUNT, SLOTS // 2, CHUNK)), *kept],
        flops=2 * 3 * SLOTS * UNITS * D,
        moved=8 * 2**20,
        limit=VMEM_ALL,
    )(own, up, up_rest, down_rest, down, partner, w_in, w_out)
    early_sums, far_pack = lax.optimization_barrier((early_sums, far_pack))
    far_query = moved_by(far_pack, "ctx_1", 1)
    sums, *late = call(
        late_kernel,
        [SMEM] + [ANY] * 9,
        [shape((CTX_COUNT, ROWS, CHUNK)), *kept],
        [
            *[pltpu.VMEM((ROWS, HALF), BF16)] * 4,
            *[pltpu.VMEM((UNITS, D), BF16)] * 2,
            pltpu.VMEM((CTX_COUNT, ROWS, CHUNK), BF16),
            *[pltpu.VMEM(k.shape, BF16) for k in kept],
            pltpu.SemaphoreType.DMA((12,)),
            pltpu.SemaphoreType.DMA((4 + CTX_COUNT,)),
        ],
        flops=2 * 3 * SLOTS * UNITS * D,
        moved=12 * 2**20,
        places=[ANY] * 5,
        limit=VMEM_ALL,
    )(at, partner_up, partner_down, *across, *partner_across, w_in, w_out, early_sums)
    sums, far_query = lax.optimization_barrier((sums, far_query))
    parts = lax.all_to_all(sums, CTX, split_axis=0, concat_axis=0, tiled=True)
    [weights_grad] = call(
        weights_kernel,
        [ANY] * 8,
        [shape((2 * UNITS, D))],
        [pltpu.VMEM(k.shape, BF16) for k in (*kept, *kept)] + [pltpu.SemaphoreType.DMA((8,))],
        flops=2 * 4 * SLOTS * UNITS * D,
        moved=8 * 2**20,
        limit=VMEM_ALL,
    )(*early, *late)
    weights_grad = weights_grad.reshape(1, UNITS, 2, D)
    parts, weights_grad = lax.optimization_barrier((parts, weights_grad))
    [back] = call(total_kernel, [VMEM], [shape((ROWS, CHUNK))], moved=3 * 2**20)(parts)
    back, far_query = lax.optimization_barrier((back, far_query))
    returned = lax.all_to_all(
        back.reshape(EXPERTS, 8, CHUNK), "exp", split_axis=0, concat_axis=0, tiled=True
    ).reshape(ROWS, CHUNK)
    queries = call(join_kernel, [VMEM] * 2, [shape((64, CHUNK))] * 4, moved=2**20)(own_pack, far_query)
    queries = [queries[0]] + [moved_by(queries[k], "ctx_0", k) for k in (1, 2, 3)]
    [total] = call(tokens_kernel, [VMEM] * 7, [shape((CTX_COUNT, 64, CHUNK))], moved=2**20)(
        returned, even, odd, *queries
    )
    packs = lax.all_to_all(total, CTX, split_axis=0, concat_axis=0, tiled=True)
    [states_grad] = call(
        norm_grad_kernel,
        [VMEM] * 4,
        [shape((TOKENS, D))],
        [pltpu.VMEM((TOKENS, D), F32)],
        moved=3 * 2**20,
    )(packs, states, grads, norm_gain)
    return states_grad[None], keys_grad[None], values_grad[None], weights_grad


def solution(mesh):
    finer = Mesh(mesh.devices.reshape(4, 2, mesh.shape["exp"]), (*CTX, "exp"))
    return jax.shard_map(
        on_device,
        mesh=finer,
        in_specs=(
            P("exp", None, None),
            P("exp", None, None),
            P("exp", CTX, None),
            P("exp", CTX, None),
            P(),
            P("exp", None, None),
            P("exp", None, None),
            P("exp", CTX, None, None),
        ),
        out_specs=(
            P("exp", None, None),
            P("exp", CTX, None),
            P("exp", CTX, None),
            P("exp", CTX, None, None),
        ),
        check_vma=False,
    )
```

```python
import math

import jax
import jax.numpy as jnp
from jax import lax
from jax.experimental import pallas as pl
from jax.experimental.pallas import tpu as pltpu
from jax.sharding import Mesh
from jax.sharding import PartitionSpec as P

HEADS = 20
HEAD = 128
D = 2560
HALF = 1280
TOKENS = 128
KEYS = 128
UNITS = 256
EXPERTS = 32
CTX_COUNT = 8
ROWS = 256
SLOTS = 256
CHUNK = 640
CTX = ("ctx_0", "ctx_1")
EPSILON = 1e-05
SCALE = HEAD**-0.5
BF16 = jnp.bfloat16
F32 = jnp.float32
VMEM_LIMIT = 24 * 2**20
VMEM_ALL = 60 * 2**20
VMEM_MOST = 50 * 2**20

VMEM = pl.BlockSpec(memory_space=pltpu.VMEM)
SMEM = pl.BlockSpec(memory_space=pltpu.SMEM)
ANY = pl.BlockSpec(memory_space=pl.ANY)


def call(kernel, ins, outs, scratch=(), flops=0, moved=0, places=None, limit=VMEM_LIMIT):
    return pl.pallas_call(
        kernel,
        in_specs=ins,
        out_specs=places or [VMEM] * len(outs),
        out_shape=outs,
        scratch_shapes=list(scratch),
        compiler_params=pltpu.CompilerParams(vmem_limit_bytes=limit),
        cost_estimate=pl.CostEstimate(flops=flops, bytes_accessed=moved, transcendentals=0),
    )


def shape(dims, dtype=BF16):
    return jax.ShapeDtypeStruct(dims, dtype)


def dot(a, b, dims=((1,), (0,))):
    return lax.dot_general(a, b, (dims, ((), ())), preferred_element_type=F32)


def iota(dims, axis):
    return lax.broadcasted_iota(jnp.int32, dims, axis)


def one(mask):
    return jnp.where(mask, 1.0, 0.0).astype(BF16)


def route_kernel(place, states, grads, gain, ids, gates, normed_out, send, even, odd):
    c = place[0]
    x = states[...].astype(F32)
    inverse = lax.rsqrt(jnp.mean(x * x, axis=-1, keepdims=True) + EPSILON)
    normed_out[...] = (x * inverse * gain[...].reshape(1, D)).astype(BF16)
    expert = iota((ROWS, TOKENS), 0) // 8
    i = iota((ROWS, TOKENS), 0) % 8
    first = ids[0:1, :] == expert
    second = ids[1:2, :] == expert
    named = first | second
    before = one(iota((TOKENS, TOKENS), 0) < iota((TOKENS, TOKENS), 1))
    slot = dot(one(named), before).astype(jnp.int32)
    slot = jnp.where(named, slot, -1)
    even[...] = one(slot == 2 * i)
    odd[...] = one(slot == 2 * i + 1)
    mine = slot == 2 * c + i % 2
    gate = jnp.where(first, gates[0:1, :], 0.0) + jnp.where(second, gates[1:2, :], 0.0)
    gate = jnp.sum(jnp.where(mine, gate, 0.0), axis=1, keepdims=True)
    low = i < 4
    is_row = (i // 2) % 2 == 0
    row_low = one(mine & low & is_row)
    row_high = one(mine & (~low) & is_row)
    grad_low = one(mine & low & (~is_row))
    grad_high = one(mine & (~low) & (~is_row))
    rows = dot(row_low, normed_out[:, :HALF]) + dot(row_high, normed_out[:, HALF:])
    douts = dot(grad_low, grads[:, :HALF]) + dot(grad_high, grads[:, HALF:])
    send[...] = (rows + gate * douts).astype(BF16)


def scores_kernel(normed, grads, keys, values, weights_out, slopes_out, stats):
    for h in range(HEADS):
        at = slice(h * HEAD, (h + 1) * HEAD)
        s = dot(keys[:, at], normed[:, at], ((1,), (1,))) * SCALE
        peak = jnp.max(s, axis=0, keepdims=True)
        w = jnp.exp(s - peak)
        slopes = dot(values[:, at], grads[:, at], ((1,), (1,)))
        weights_out[h] = w
        slopes_out[h] = slopes
        stats[h : h + 1, :] = peak
        stats[24 + h : 25 + h, :] = jnp.sum(w, axis=0, keepdims=True)
        stats[48 + h : 49 + h, :] = jnp.sum(w * slopes, axis=0, keepdims=True)
    for part in range(3):
        at = 24 * part + HEADS
        stats[at : at + 4, :] = jnp.zeros((4, TOKENS), F32)


def merged(stats):
    peak = stats[0][:24]
    for one_side in stats[1:]:
        peak = jnp.maximum(peak, one_side[:24])
    total = inner = 0.0
    for one_side in stats:
        factor = jnp.exp(one_side[:24] - peak)
        total = total + one_side[24:48] * factor
        inner = inner + one_side[48:] * factor
    return jnp.concatenate([peak, total, inner], axis=0)


def score_grad_kernel(
    place,
    normed,
    grads,
    keys,
    weights,
    slopes,
    local,
    near,
    far,
    keys_grad,
    values_grad,
    own_pack,
    far_pack,
    query,
):
    peak = jnp.maximum(near[0:24, :], far[0:24, :])
    near_factor = jnp.exp(near[0:24, :] - peak)
    far_factor = jnp.exp(far[0:24, :] - peak)
    total = near[24:48, :] * near_factor + far[24:48, :] * far_factor
    inner = near[48:72, :] * near_factor + far[48:72, :] * far_factor
    total = jnp.where(iota((24, TOKENS), 0) < HEADS, total, 1.0)
    factor = jnp.exp(local[0:24, :] - peak) / total
    delta = inner / total
    for h in range(HEADS):
        at = slice(h * HEAD, (h + 1) * HEAD)
        probs = weights[h] * factor[h : h + 1, :]
        score_grad = (probs * (slopes[h] - delta[h : h + 1, :])).astype(BF16)
        values_grad[:, at] = dot(probs.astype(BF16), grads[:, at]).astype(BF16)
        keys_grad[:, at] = (dot(score_grad, normed[:, at]) * SCALE).astype(BF16)
        query[:, at] = dot(score_grad, keys[:, at], ((0,), (0,))) * SCALE
    lane = iota((64, 128), 1)
    first = place[0] % 2 == 0
    for g in range(CTX_COUNT // 2):
        row = (g - place[0] // 2 + 4) % 4
        tile = slice(2048 + 128 * g, 2176 + 128 * g)
        a, b = query[0:64, tile], query[64:128, tile]
        packs = []
        for f, tail in (
            (2 * g, jnp.where(lane < 64, a, pltpu.roll(b, 64, 1))),
            (2 * g + 1, jnp.where(lane < 64, pltpu.roll(a, 64, 1), b)),
        ):
            at = slice(256 * f, 256 * f + 256)
            packs.append(jnp.concatenate([query[0:64, at], query[64:128, at], tail], axis=1))
        own_pack[row] = jnp.where(first, packs[0], packs[1]).astype(BF16)
        far_pack[row] = jnp.where(first, packs[1], packs[0]).astype(BF16)


def join_kernel(own, far, *outs):
    for k in range(4):
        outs[k][...] = (own[k].astype(F32) + far[k].astype(F32)).astype(BF16)


def experts_of(blocks, w_in, w_out, rows, douts, act, pre_grad, put, after=lambda step: None):
    to, source = iota((ROWS, ROWS), 0), iota((ROWS, ROWS), 1)
    order = one(source == 8 * (to % 32) + to // 32)
    for k, block in enumerate(blocks):
        sorted_rows = dot(order, block()).astype(BF16)
        for q in range(2):
            where = slice(128 * q + 32 * k, 128 * q + 32 * k + 32)
            for half in range(2):
                lanes = slice(HALF * half, HALF * half + HALF)
                first = 128 * half + 32 * q
                rows[where, lanes] = sorted_rows[first : first + 32, :]
                douts[where, lanes] = sorted_rows[first + 64 : first + 96, :]
    after("rows")
    v = dot(rows[...], w_in[...], ((1,), (1,)))
    act_grad = dot(douts[...], w_out[...], ((1,), (1,)))
    root = math.sqrt(2 / math.pi)
    square = v * v
    t = jnp.tanh(root * (v + 0.044715 * (square * v)))
    act[...] = (0.5 * v * (1.0 + t)).astype(BF16)
    slope = 0.5 * (1.0 + t) + 0.5 * v * (1.0 - t * t) * (root * (1.0 + 3 * 0.044715 * square))
    pre_grad[...] = (act_grad * slope).astype(BF16)
    after("units")
    tails = dot(pre_grad[...], w_in[:, 2048:2560])
    lane = iota((128, 128), 1)
    for f in range(CTX_COUNT):
        part = dot(pre_grad[...], w_in[:, 256 * f : 256 * f + 256])
        put(f, slice(0, 256), part[0:128].astype(BF16))
        put(f, slice(256, 512), part[128:256].astype(BF16))
        tile = slice(128 * (f // 2), 128 * (f // 2) + 128)
        a, b = tails[0:128, tile], tails[128:256, tile]
        if f % 2 == 0:
            tail = jnp.where(lane < 64, a, pltpu.roll(b, 64, 1))
        else:
            tail = jnp.where(lane < 64, pltpu.roll(a, 64, 1), b)
        put(f, slice(512, 640), tail.astype(BF16))
        after(f)


def early_kernel(*refs):
    own, up, up_rest, down_rest, down, partner, w_in, w_out, sums = refs[:9]

    def put(f, lanes, value):
        sums[f, :, lanes] = value

    blocks = [
        lambda: own[...],
        lambda: jnp.concatenate([up[...], up_rest[...]], axis=0),
        lambda: jnp.concatenate([down_rest[...], down[...]], axis=0),
        lambda: partner[...],
    ]
    experts_of(blocks, w_in, w_out, *refs[9:], put)


def late_kernel(at_ref, *refs):
    given, results, held = refs[:9], refs[9:14], refs[14:]
    shards, (w_in, w_out), sums, kept = held[:4], held[4:6], held[6], held[7:11]
    arrived, left = held[11:]
    where = [pl.ds(pl.multiple_of(32 * at_ref[k], 32), 32) for k in range(CTX_COUNT)]
    landing = [
        *shards[:2],
        *(shards[k].at[128 * j : 128 * j + 128] for k in (2, 3) for j in range(2)),
        w_in,
        w_out,
    ]
    loads = [pltpu.make_async_copy(given[k], landing[k], arrived.at[k]) for k in range(8)]
    for load in loads:
        load.start()
    early = [
        pltpu.make_async_copy(
            given[8].at[:, 32 * k : 32 * k + 32, :], sums.at[:, where[k], :], arrived.at[8 + k]
        )
        for k in range(4)
    ]
    for load in early:
        load.start()
    stores = [pltpu.make_async_copy(kept[k], results[1 + k], left.at[k]) for k in range(4)]
    stores += [
        pltpu.make_async_copy(sums.at[f], results[0].at[f], left.at[4 + f])
        for f in range(CTX_COUNT)
    ]

    def block(k):
        for load in loads[k : k + 1] if k < 2 else loads[2 * k - 2 : 2 * k]:
            load.wait()
        return shards[k][...]

    def put(f, lanes, value):
        for k in range(4):
            sums[f, where[4 + k], lanes] = value[32 * k : 32 * k + 32]

    def after(step):
        if step == "rows":
            stores[0].start()
            stores[1].start()
            loads[6].wait()
            loads[7].wait()
        elif step == "units":
            stores[2].start()
            stores[3].start()
            for load in early:
                load.wait()
        else:
            stores[4 + step].start()

    blocks = [lambda k=k: block(k) for k in range(4)]
    experts_of(blocks, w_in, w_out, *kept, put, after)
    for store in stores:
        store.wait()


def weights_kernel(*refs):
    given, out, held, arrived = refs[:8], refs[8], refs[9:17], refs[17]
    loads = [pltpu.make_async_copy(given[k], held[k], arrived.at[k]) for k in range(8)]
    for load in loads:
        load.start()
    unit, column = iota((UNITS, 2 * UNITS), 0), iota((UNITS, 2 * UNITS), 1)
    even, odd = one(column == 2 * unit), one(column == 2 * unit + 1)
    for load in loads:
        load.wait()
    terms = []
    for rows, douts, act, pre_grad in (held[:4], held[4:]):
        terms.append((dot(pre_grad[...], even).astype(BF16), rows))
        terms.append((dot(act[...], odd).astype(BF16), douts))
    for n in range(D // 512):
        lanes = slice(512 * n, 512 * n + 512)
        out[:, lanes] = sum(dot(a, b[:, lanes], ((0,), (0,))) for a, b in terms).astype(BF16)


def total_kernel(parts, back):
    total = parts[0].astype(F32)
    for k in range(1, CTX_COUNT):
        total = total + parts[k].astype(F32)
    to, source = iota((ROWS, ROWS), 0), iota((ROWS, ROWS), 1)
    order = one(source == 32 * (to % 8) + to // 8)
    back[...] = dot(order, total.astype(BF16)).astype(BF16)


def tokens_kernel(returned, even, odd, own, below, across, above, out):
    query = (own[...].astype(F32) + across[...].astype(F32)) + (
        below[...].astype(F32) + above[...].astype(F32)
    )
    a = dot(even[...], returned[...], ((0,), (0,)))
    b = dot(odd[...], returned[...], ((0,), (0,)))
    wide = a[:, 0:256] + b[:, 256:512]
    tail = a[:, 512:640] + pltpu.roll(b[:, 512:640], 64, 1)
    lane = iota((64, 128), 1)
    tail = jnp.where(lane < 64, tail[0:64], pltpu.roll(tail[64:128], 64, 1))
    left = (wide[0:64] + query[:, 0:256]).astype(BF16)
    right = (wide[64:128] + query[:, 256:512]).astype(BF16)
    tail = (tail + query[:, 512:640]).astype(BF16)
    for f in range(CTX_COUNT):
        out[f, :, 0:256] = left
        out[f, :, 256:512] = right
        out[f, :, 512:640] = tail


def norm_grad_kernel(packs, states, grads, gain, out, total):
    for f in range(CTX_COUNT):
        at = slice(256 * f, 256 * f + 256)
        total[0:64, at] = packs[f, :, 0:256].astype(F32)
        total[64:128, at] = packs[f, :, 256:512].astype(F32)
    lane = iota((64, 128), 1)
    for g in range(CTX_COUNT // 2):
        at = slice(2048 + 128 * g, 2176 + 128 * g)
        a = packs[2 * g, :, 512:640].astype(F32)
        b = packs[2 * g + 1, :, 512:640].astype(F32)
        total[0:64, at] = jnp.where(lane < 64, a, pltpu.roll(b, 64, 1))
        total[64:128, at] = jnp.where(lane < 64, pltpu.roll(a, 64, 1), b)
    x = states[...].astype(F32)
    inverse = lax.rsqrt(jnp.mean(x * x, axis=-1, keepdims=True) + EPSILON)
    unit = x * inverse
    g = total[...] * gain[...].reshape(1, D)
    g = g - unit * jnp.mean(g * unit, axis=-1, keepdims=True)
    out[...] = (grads[...].astype(F32) + inverse * g).astype(BF16)


def moved_by(array, axis, step):
    count = lax.axis_size(axis)
    return lax.ppermute(array, axis, [(k, (k + step) % count) for k in range(count)])


def on_device(
    states, out_grad, doc_keys, doc_values, norm_gain, expert_ids, gate_values, expert_weights
):
    states, grads, keys, values = states[0], out_grad[0], doc_keys[0], doc_values[0]
    y, x = lax.axis_index("ctx_0"), lax.axis_index("ctx_1")
    place = (2 * y + x).astype(jnp.int32).reshape(1)
    normed, send, even, odd = call(
        route_kernel,
        [SMEM] + [VMEM] * 5,
        [shape((TOKENS, D)), shape((ROWS, HALF)), shape((ROWS, TOKENS)), shape((ROWS, TOKENS))],
        flops=2 * 4 * ROWS * TOKENS * HALF,
        moved=3 * 2**20,
        limit=VMEM_ALL,
    )(place, states, grads, norm_gain, expert_ids[0].T, gate_values[0].T)
    own = lax.all_to_all(
        send.reshape(EXPERTS, 8, HALF), "exp", split_axis=0, concat_axis=0, tiled=True
    ).reshape(ROWS, HALF)

    normed, expert_weights = lax.optimization_barrier((normed, expert_weights))
    w_in, w_out = expert_weights[0, :, 0, :], expert_weights[0, :, 1, :]
    keys, w_in, w_out = lax.optimization_barrier((keys, w_in, w_out))

    weights, slopes, stats = call(
        scores_kernel,
        [VMEM] * 4,
        [shape((HEADS, KEYS, TOKENS), F32), shape((HEADS, KEYS, TOKENS), F32), shape((72, TOKENS), F32)],
        flops=2 * 2 * KEYS * TOKENS * D,
        moved=5 * 2**20,
    )(normed, grads, keys, values)
    near = merged([stats] + [moved_by(stats, "ctx_0", k) for k in (1, 2, 3)])
    far = moved_by(near, "ctx_1", 1)
    own, near, far = lax.optimization_barrier((own, near, far))
    low, high = own[:128], own[128:]
    up, down = moved_by(low, "ctx_0", 1), moved_by(high, "ctx_0", 3)
    up_rest, down_rest = moved_by(high, "ctx_0", 1), moved_by(low, "ctx_0", 3)
    partner = moved_by(own, "ctx_1", 1)
    keys_grad, values_grad, own_pack, far_pack = call(
        score_grad_kernel,
        [SMEM] + [VMEM] * 8,
        [shape((KEYS, D)), shape((KEYS, D)), *[shape((4, 64, CHUNK))] * 2],
        [pltpu.VMEM((TOKENS, D), F32)],
        flops=3 * 2 * KEYS * TOKENS * D,
        moved=6 * 2**20,
        limit=VMEM_ALL,
    )(place, normed, grads, keys, weights, slopes, stats, near, far)
    up, down, far_pack = lax.optimization_barrier((up, down, far_pack))
    across = [moved_by(up, "ctx_0", 1), moved_by(down, "ctx_0", 3)]
    partner_up, partner_down = moved_by(partner, "ctx_0", 1), moved_by(partner, "ctx_0", 3)
    partner_across = [moved_by(piece, "ctx_1", 1) for piece in across]
    places = [(0, 0), (-1, 0), (1, 0), (0, 1), (-1, 1), (1, 1), (2, 0), (2, 1)]
    at = jnp.stack([2 * ((y + a + 4) % 4) + (x + b) % 2 for a, b in places]).astype(jnp.int32)
    kept = [shape((SLOTS, D))] * 2 + [shape((SLOTS, UNITS))] * 2
    early_sums, *early = call(
        early_kernel,
        [VMEM] * 8,
        [shape((CTX_COUNT, SLOTS // 2, CHUNK)), *kept],
        flops=2 * 3 * SLOTS * UNITS * D,
        moved=8 * 2**20,
        limit=VMEM_ALL,
    )(own, up, up_rest, down_rest, down, partner, w_in, w_out)
    *partner_across, far_pack = lax.optimization_barrier((*partner_across, far_pack))
    far_query = moved_by(far_pack, "ctx_1", 1)
    sums, *late = call(
        late_kernel,
        [SMEM] + [ANY] * 9,
        [shape((CTX_COUNT, ROWS, CHUNK)), *kept],
        [
            *[pltpu.VMEM((ROWS, HALF), BF16)] * 4,
            *[pltpu.VMEM((UNITS, D), BF16)] * 2,
            pltpu.VMEM((CTX_COUNT, ROWS, CHUNK), BF16),
            *[pltpu.VMEM(k.shape, BF16) for k in kept],
            pltpu.SemaphoreType.DMA((12,)),
            pltpu.SemaphoreType.DMA((4 + CTX_COUNT,)),
        ],
        flops=2 * 3 * SLOTS * UNITS * D,
        moved=12 * 2**20,
        places=[ANY] * 5,
        limit=VMEM_MOST,
    )(at, partner_up, partner_down, *across, *partner_across, w_in, w_out, early_sums)
    sums, far_query = lax.optimization_barrier((sums, far_query))
    parts = lax.all_to_all(sums, CTX, split_axis=0, concat_axis=0, tiled=True)
    [weights_grad] = call(
        weights_kernel,
        [ANY] * 8,
        [shape((2 * UNITS, D))],
        [pltpu.VMEM(k.shape, BF16) for k in (*kept, *kept)] + [pltpu.SemaphoreType.DMA((8,))],
        flops=2 * 4 * SLOTS * UNITS * D,
        moved=8 * 2**20,
        limit=VMEM_ALL,
    )(*early, *late)
    weights_grad = weights_grad.reshape(1, UNITS, 2, D)
    parts, weights_grad = lax.optimization_barrier((parts, weights_grad))
    [back] = call(total_kernel, [VMEM], [shape((ROWS, CHUNK))], moved=3 * 2**20)(parts)
    back, far_query = lax.optimization_barrier((back, far_query))
    returned = lax.all_to_all(
        back.reshape(EXPERTS, 8, CHUNK), "exp", split_axis=0, concat_axis=0, tiled=True
    ).reshape(ROWS, CHUNK)
    queries = call(join_kernel, [VMEM] * 2, [shape((64, CHUNK))] * 4, moved=2**20)(own_pack, far_query)
    queries = [queries[0]] + [moved_by(queries[k], "ctx_0", k) for k in (1, 2, 3)]
    [total] = call(tokens_kernel, [VMEM] * 7, [shape((CTX_COUNT, 64, CHUNK))], moved=2**20)(
        returned, even, odd, *queries
    )
    packs = lax.all_to_all(total, CTX, split_axis=0, concat_axis=0, tiled=True)
    [states_grad] = call(
        norm_grad_kernel,
        [VMEM] * 4,
        [shape((TOKENS, D))],
        [pltpu.VMEM((TOKENS, D), F32)],
        moved=3 * 2**20,
    )(packs, states, grads, norm_gain)
    return states_grad[None], keys_grad[None], values_grad[None], weights_grad


def solution(mesh):
    finer = Mesh(mesh.devices.reshape(4, 2, mesh.shape["exp"]), (*CTX, "exp"))
    return jax.shard_map(
        on_device,
        mesh=finer,
        in_specs=(
            P("exp", None, None),
            P("exp", None, None),
            P("exp", CTX, None),
            P("exp", CTX, None),
            P(),
            P("exp", None, None),
            P("exp", None, None),
            P("exp", CTX, None, None),
        ),
        out_specs=(
            P("exp", None, None),
            P("exp", CTX, None),
            P("exp", CTX, None),
            P("exp", CTX, None, None),
        ),
        check_vma=False,
    )
```

```python
import math

import jax
import jax.numpy as jnp
from jax import lax
from jax.experimental import pallas as pl
from jax.experimental.pallas import tpu as pltpu
from jax.sharding import Mesh
from jax.sharding import PartitionSpec as P

HEADS = 20
HEAD = 128
D = 2560
HALF = 1280
TOKENS = 128
KEYS = 128
UNITS = 256
EXPERTS = 32
CTX_COUNT = 8
ROWS = 256
SLOTS = 256
CHUNK = 640
CTX = ("ctx_0", "ctx_1")
EPSILON = 1e-05
SCALE = HEAD**-0.5
BF16 = jnp.bfloat16
F32 = jnp.float32
VMEM_LIMIT = 24 * 2**20
VMEM_ALL = 60 * 2**20
VMEM_MOST = 50 * 2**20

VMEM = pl.BlockSpec(memory_space=pltpu.VMEM)
SMEM = pl.BlockSpec(memory_space=pltpu.SMEM)
ANY = pl.BlockSpec(memory_space=pl.ANY)


def call(kernel, ins, outs, scratch=(), flops=0, moved=0, places=None, limit=VMEM_LIMIT):
    return pl.pallas_call(
        kernel,
        in_specs=ins,
        out_specs=places or [VMEM] * len(outs),
        out_shape=outs,
        scratch_shapes=list(scratch),
        compiler_params=pltpu.CompilerParams(vmem_limit_bytes=limit),
        cost_estimate=pl.CostEstimate(flops=flops, bytes_accessed=moved, transcendentals=0),
    )


def shape(dims, dtype=BF16):
    return jax.ShapeDtypeStruct(dims, dtype)


def dot(a, b, dims=((1,), (0,))):
    return lax.dot_general(a, b, (dims, ((), ())), preferred_element_type=F32)


def iota(dims, axis):
    return lax.broadcasted_iota(jnp.int32, dims, axis)


def one(mask):
    return jnp.where(mask, 1.0, 0.0).astype(BF16)


def route_kernel(place, states, grads, gain, ids, gates, normed_out, send, even, odd):
    c = place[0]
    x = states[...].astype(F32)
    inverse = lax.rsqrt(jnp.mean(x * x, axis=-1, keepdims=True) + EPSILON)
    normed_out[...] = (x * inverse * gain[...].reshape(1, D)).astype(BF16)
    expert = iota((ROWS, TOKENS), 0) // 8
    i = iota((ROWS, TOKENS), 0) % 8
    first = ids[0:1, :] == expert
    second = ids[1:2, :] == expert
    named = first | second
    before = one(iota((TOKENS, TOKENS), 0) < iota((TOKENS, TOKENS), 1))
    slot = dot(one(named), before).astype(jnp.int32)
    slot = jnp.where(named, slot, -1)
    even[...] = one(slot == 2 * i)
    odd[...] = one(slot == 2 * i + 1)
    mine = slot == 2 * c + i % 2
    gate = jnp.where(first, gates[0:1, :], 0.0) + jnp.where(second, gates[1:2, :], 0.0)
    gate = jnp.sum(jnp.where(mine, gate, 0.0), axis=1, keepdims=True)
    low = i < 4
    is_row = (i // 2) % 2 == 0
    row_low = one(mine & low & is_row)
    row_high = one(mine & (~low) & is_row)
    grad_low = one(mine & low & (~is_row))
    grad_high = one(mine & (~low) & (~is_row))
    rows = dot(row_low, normed_out[:, :HALF]) + dot(row_high, normed_out[:, HALF:])
    douts = dot(grad_low, grads[:, :HALF]) + dot(grad_high, grads[:, HALF:])
    send[...] = (rows + gate * douts).astype(BF16)


def scores_kernel(normed, grads, keys, values, weights_out, slopes_out, stats):
    for h in range(HEADS):
        at = slice(h * HEAD, (h + 1) * HEAD)
        s = dot(keys[:, at], normed[:, at], ((1,), (1,))) * SCALE
        peak = jnp.max(s, axis=0, keepdims=True)
        w = jnp.exp(s - peak)
        slopes = dot(values[:, at], grads[:, at], ((1,), (1,)))
        weights_out[h] = w
        slopes_out[h] = slopes
        stats[h : h + 1, :] = peak
        stats[24 + h : 25 + h, :] = jnp.sum(w, axis=0, keepdims=True)
        stats[48 + h : 49 + h, :] = jnp.sum(w * slopes, axis=0, keepdims=True)
    for part in range(3):
        at = 24 * part + HEADS
        stats[at : at + 4, :] = jnp.zeros((4, TOKENS), F32)


def merged(stats):
    peak = stats[0][:24]
    for one_side in stats[1:]:
        peak = jnp.maximum(peak, one_side[:24])
    total = inner = 0.0
    for one_side in stats:
        factor = jnp.exp(one_side[:24] - peak)
        total = total + one_side[24:48] * factor
        inner = inner + one_side[48:] * factor
    return jnp.concatenate([peak, total, inner], axis=0)


def score_grad_kernel(
    place,
    normed,
    grads,
    keys,
    weights,
    slopes,
    local,
    near,
    far,
    keys_grad,
    values_grad,
    own_pack,
    far_pack,
    query,
):
    peak = jnp.maximum(near[0:24, :], far[0:24, :])
    near_factor = jnp.exp(near[0:24, :] - peak)
    far_factor = jnp.exp(far[0:24, :] - peak)
    total = near[24:48, :] * near_factor + far[24:48, :] * far_factor
    inner = near[48:72, :] * near_factor + far[48:72, :] * far_factor
    total = jnp.where(iota((24, TOKENS), 0) < HEADS, total, 1.0)
    factor = jnp.exp(local[0:24, :] - peak) / total
    delta = inner / total
    for h in range(HEADS):
        at = slice(h * HEAD, (h + 1) * HEAD)
        probs = weights[h] * factor[h : h + 1, :]
        score_grad = (probs * (slopes[h] - delta[h : h + 1, :])).astype(BF16)
        values_grad[:, at] = dot(probs.astype(BF16), grads[:, at]).astype(BF16)
        keys_grad[:, at] = (dot(score_grad, normed[:, at]) * SCALE).astype(BF16)
        query[:, at] = dot(score_grad, keys[:, at], ((0,), (0,))) * SCALE
    lane = iota((64, 128), 1)
    first = place[0] % 2 == 0
    for g in range(CTX_COUNT // 2):
        row = (g - place[0] // 2 + 4) % 4
        tile = slice(2048 + 128 * g, 2176 + 128 * g)
        a, b = query[0:64, tile], query[64:128, tile]
        packs = []
        for f, tail in (
            (2 * g, jnp.where(lane < 64, a, pltpu.roll(b, 64, 1))),
            (2 * g + 1, jnp.where(lane < 64, pltpu.roll(a, 64, 1), b)),
        ):
            at = slice(256 * f, 256 * f + 256)
            packs.append(jnp.concatenate([query[0:64, at], query[64:128, at], tail], axis=1))
        own_pack[row] = jnp.where(first, packs[0], packs[1]).astype(BF16)
        far_pack[row] = jnp.where(first, packs[1], packs[0]).astype(BF16)


def join_kernel(own, far, *outs):
    for k in range(4):
        outs[k][...] = (own[k].astype(F32) + far[k].astype(F32)).astype(BF16)


def experts_of(blocks, w_in, w_out, rows, douts, act, pre_grad, put, after=lambda step: None):
    to, source = iota((ROWS, ROWS), 0), iota((ROWS, ROWS), 1)
    order = one(source == 8 * (to % 32) + to // 32)
    for k, block in enumerate(blocks):
        sorted_rows = dot(order, block()).astype(BF16)
        for q in range(2):
            where = slice(128 * q + 32 * k, 128 * q + 32 * k + 32)
            for half in range(2):
                lanes = slice(HALF * half, HALF * half + HALF)
                first = 128 * half + 32 * q
                rows[where, lanes] = sorted_rows[first : first + 32, :]
                douts[where, lanes] = sorted_rows[first + 64 : first + 96, :]
    after("rows")
    v = dot(rows[...], w_in[...], ((1,), (1,)))
    act_grad = dot(douts[...], w_out[...], ((1,), (1,)))
    root = math.sqrt(2 / math.pi)
    square = v * v
    t = jnp.tanh(root * (v + 0.044715 * (square * v)))
    act[...] = (0.5 * v * (1.0 + t)).astype(BF16)
    slope = 0.5 * (1.0 + t) + 0.5 * v * (1.0 - t * t) * (root * (1.0 + 3 * 0.044715 * square))
    pre_grad[...] = (act_grad * slope).astype(BF16)
    after("units")
    tails = dot(pre_grad[...], w_in[:, 2048:2560])
    lane = iota((128, 128), 1)
    for f in range(CTX_COUNT):
        part = dot(pre_grad[...], w_in[:, 256 * f : 256 * f + 256])
        put(f, slice(0, 256), part[0:128].astype(BF16))
        put(f, slice(256, 512), part[128:256].astype(BF16))
        tile = slice(128 * (f // 2), 128 * (f // 2) + 128)
        a, b = tails[0:128, tile], tails[128:256, tile]
        if f % 2 == 0:
            tail = jnp.where(lane < 64, a, pltpu.roll(b, 64, 1))
        else:
            tail = jnp.where(lane < 64, pltpu.roll(a, 64, 1), b)
        put(f, slice(512, 640), tail.astype(BF16))
        after(f)


def early_kernel(*refs):
    own, up, up_rest, down_rest, down, partner, w_in, w_out, sums = refs[:9]

    def put(f, lanes, value):
        sums[f, :, lanes] = value

    blocks = [
        lambda: own[...],
        lambda: jnp.concatenate([up[...], up_rest[...]], axis=0),
        lambda: jnp.concatenate([down_rest[...], down[...]], axis=0),
        lambda: partner[...],
    ]
    experts_of(blocks, w_in, w_out, *refs[9:], put)


def late_kernel(at_ref, *refs):
    given, results, held = refs[:9], refs[9:14], refs[14:]
    shards, (w_in, w_out), sums, kept = held[:4], held[4:6], held[6], held[7:11]
    arrived, left = held[11:]
    where = [pl.ds(pl.multiple_of(32 * at_ref[k], 32), 32) for k in range(CTX_COUNT)]
    landing = [
        *shards[:2],
        *(shards[k].at[128 * j : 128 * j + 128] for k in (2, 3) for j in range(2)),
        w_in,
        w_out,
    ]
    loads = [pltpu.make_async_copy(given[k], landing[k], arrived.at[k]) for k in range(8)]
    for load in loads:
        load.start()
    early = [
        pltpu.make_async_copy(
            given[8].at[:, 32 * k : 32 * k + 32, :], sums.at[:, where[k], :], arrived.at[8 + k]
        )
        for k in range(4)
    ]
    for load in early:
        load.start()
    stores = [pltpu.make_async_copy(kept[k], results[1 + k], left.at[k]) for k in range(4)]
    stores += [
        pltpu.make_async_copy(sums.at[f], results[0].at[f], left.at[4 + f])
        for f in range(CTX_COUNT)
    ]

    def block(k):
        for load in loads[k : k + 1] if k < 2 else loads[2 * k - 2 : 2 * k]:
            load.wait()
        return shards[k][...]

    def put(f, lanes, value):
        for k in range(4):
            sums[f, where[4 + k], lanes] = value[32 * k : 32 * k + 32]

    def after(step):
        if step == "rows":
            stores[0].start()
            stores[1].start()
            loads[6].wait()
            loads[7].wait()
        elif step == "units":
            stores[2].start()
            stores[3].start()
            for load in early:
                load.wait()
        else:
            stores[4 + step].start()

    blocks = [lambda k=k: block(k) for k in range(4)]
    experts_of(blocks, w_in, w_out, *kept, put, after)
    for store in stores:
        store.wait()


def weights_kernel(*refs):
    given, out, held, arrived = refs[:8], refs[8], refs[9:17], refs[17]
    loads = [pltpu.make_async_copy(given[k], held[k], arrived.at[k]) for k in range(8)]
    for load in loads:
        load.start()
    unit, column = iota((UNITS, 2 * UNITS), 0), iota((UNITS, 2 * UNITS), 1)
    even, odd = one(column == 2 * unit), one(column == 2 * unit + 1)
    for load in loads:
        load.wait()
    terms = []
    for rows, douts, act, pre_grad in (held[:4], held[4:]):
        terms.append((dot(pre_grad[...], even).astype(BF16), rows))
        terms.append((dot(act[...], odd).astype(BF16), douts))
    for n in range(D // 512):
        lanes = slice(512 * n, 512 * n + 512)
        out[:, lanes] = sum(dot(a, b[:, lanes], ((0,), (0,))) for a, b in terms).astype(BF16)


def total_kernel(parts, back):
    total = parts[0].astype(F32)
    for k in range(1, CTX_COUNT):
        total = total + parts[k].astype(F32)
    to, source = iota((ROWS, ROWS), 0), iota((ROWS, ROWS), 1)
    order = one(source == 32 * (to % 8) + to // 8)
    back[...] = dot(order, total.astype(BF16)).astype(BF16)


def tokens_kernel(returned, even, odd, own, below, across, above, out):
    query = (own[...].astype(F32) + across[...].astype(F32)) + (
        below[...].astype(F32) + above[...].astype(F32)
    )
    a = dot(even[...], returned[...], ((0,), (0,)))
    b = dot(odd[...], returned[...], ((0,), (0,)))
    wide = a[:, 0:256] + b[:, 256:512]
    tail = a[:, 512:640] + pltpu.roll(b[:, 512:640], 64, 1)
    lane = iota((64, 128), 1)
    tail = jnp.where(lane < 64, tail[0:64], pltpu.roll(tail[64:128], 64, 1))
    left = (wide[0:64] + query[:, 0:256]).astype(BF16)
    right = (wide[64:128] + query[:, 256:512]).astype(BF16)
    tail = (tail + query[:, 512:640]).astype(BF16)
    for f in range(CTX_COUNT):
        out[f, :, 0:256] = left
        out[f, :, 256:512] = right
        out[f, :, 512:640] = tail


def norm_grad_kernel(packs, states, grads, gain, out, total):
    for f in range(CTX_COUNT):
        at = slice(256 * f, 256 * f + 256)
        total[0:64, at] = packs[f, :, 0:256].astype(F32)
        total[64:128, at] = packs[f, :, 256:512].astype(F32)
    lane = iota((64, 128), 1)
    for g in range(CTX_COUNT // 2):
        at = slice(2048 + 128 * g, 2176 + 128 * g)
        a = packs[2 * g, :, 512:640].astype(F32)
        b = packs[2 * g + 1, :, 512:640].astype(F32)
        total[0:64, at] = jnp.where(lane < 64, a, pltpu.roll(b, 64, 1))
        total[64:128, at] = jnp.where(lane < 64, pltpu.roll(a, 64, 1), b)
    x = states[...].astype(F32)
    inverse = lax.rsqrt(jnp.mean(x * x, axis=-1, keepdims=True) + EPSILON)
    unit = x * inverse
    g = total[...] * gain[...].reshape(1, D)
    g = g - unit * jnp.mean(g * unit, axis=-1, keepdims=True)
    out[...] = (grads[...].astype(F32) + inverse * g).astype(BF16)


def moved_by(array, axis, step):
    count = lax.axis_size(axis)
    return lax.ppermute(array, axis, [(k, (k + step) % count) for k in range(count)])


def on_device(
    states, out_grad, doc_keys, doc_values, norm_gain, expert_ids, gate_values, expert_weights
):
    states, grads, keys, values = states[0], out_grad[0], doc_keys[0], doc_values[0]
    y, x = lax.axis_index("ctx_0"), lax.axis_index("ctx_1")
    place = (2 * y + x).astype(jnp.int32).reshape(1)
    normed, send, even, odd = call(
        route_kernel,
        [SMEM] + [VMEM] * 5,
        [shape((TOKENS, D)), shape((ROWS, HALF)), shape((ROWS, TOKENS)), shape((ROWS, TOKENS))],
        flops=2 * 4 * ROWS * TOKENS * HALF,
        moved=3 * 2**20,
        limit=VMEM_ALL,
    )(place, states, grads, norm_gain, expert_ids[0].T, gate_values[0].T)
    own = lax.all_to_all(
        send.reshape(EXPERTS, 8, HALF), "exp", split_axis=0, concat_axis=0, tiled=True
    ).reshape(ROWS, HALF)

    normed, expert_weights = lax.optimization_barrier((normed, expert_weights))
    w_in, w_out = expert_weights[0, :, 0, :], expert_weights[0, :, 1, :]
    keys, w_in, w_out = lax.optimization_barrier((keys, w_in, w_out))

    weights, slopes, stats = call(
        scores_kernel,
        [VMEM] * 4,
        [shape((HEADS, KEYS, TOKENS), F32), shape((HEADS, KEYS, TOKENS), F32), shape((72, TOKENS), F32)],
        flops=2 * 2 * KEYS * TOKENS * D,
        moved=5 * 2**20,
    )(normed, grads, keys, values)
    near = merged([stats] + [moved_by(stats, "ctx_0", k) for k in (1, 2, 3)])
    far = moved_by(near, "ctx_1", 1)
    own, near, far = lax.optimization_barrier((own, near, far))
    low, high = own[:128], own[128:]
    up, down = moved_by(low, "ctx_0", 1), moved_by(high, "ctx_0", 3)
    up_rest, down_rest = moved_by(high, "ctx_0", 1), moved_by(low, "ctx_0", 3)
    partner = moved_by(own, "ctx_1", 1)
    keys_grad, values_grad, own_pack, far_pack = call(
        score_grad_kernel,
        [SMEM] + [VMEM] * 8,
        [shape((KEYS, D)), shape((KEYS, D)), *[shape((4, 64, CHUNK))] * 2],
        [pltpu.VMEM((TOKENS, D), F32)],
        flops=3 * 2 * KEYS * TOKENS * D,
        moved=6 * 2**20,
        limit=VMEM_ALL,
    )(place, normed, grads, keys, weights, slopes, stats, near, far)
    up, down, far_pack = lax.optimization_barrier((up, down, far_pack))
    across = [moved_by(up, "ctx_0", 1), moved_by(down, "ctx_0", 3)]
    partner_up, partner_down = moved_by(partner, "ctx_0", 1), moved_by(partner, "ctx_0", 3)
    partner_across = [moved_by(piece, "ctx_1", 1) for piece in across]
    places = [(0, 0), (-1, 0), (1, 0), (0, 1), (-1, 1), (1, 1), (2, 0), (2, 1)]
    at = jnp.stack([2 * ((y + a + 4) % 4) + (x + b) % 2 for a, b in places]).astype(jnp.int32)
    kept = [shape((SLOTS, D))] * 2 + [shape((SLOTS, UNITS))] * 2
    early_sums, *early = call(
        early_kernel,
        [VMEM] * 8,
        [shape((CTX_COUNT, SLOTS // 2, CHUNK)), *kept],
        flops=2 * 3 * SLOTS * UNITS * D,
        moved=8 * 2**20,
        limit=VMEM_ALL,
    )(own, up, up_rest, down_rest, down, partner, w_in, w_out)
    *partner_across, early_sums, far_pack = lax.optimization_barrier(
        (*partner_across, early_sums, far_pack)
    )
    far_query = moved_by(far_pack, "ctx_1", 1)
    sums, *late = call(
        late_kernel,
        [SMEM] + [ANY] * 9,
        [shape((CTX_COUNT, ROWS, CHUNK)), *kept],
        [
            *[pltpu.VMEM((ROWS, HALF), BF16)] * 4,
            *[pltpu.VMEM((UNITS, D), BF16)] * 2,
            pltpu.VMEM((CTX_COUNT, ROWS, CHUNK), BF16),
            *[pltpu.VMEM(k.shape, BF16) for k in kept],
            pltpu.SemaphoreType.DMA((12,)),
            pltpu.SemaphoreType.DMA((4 + CTX_COUNT,)),
        ],
        flops=2 * 3 * SLOTS * UNITS * D,
        moved=12 * 2**20,
        places=[ANY] * 5,
        limit=VMEM_MOST,
    )(at, partner_up, partner_down, *across, *partner_across, w_in, w_out, early_sums)
    sums, far_query = lax.optimization_barrier((sums, far_query))
    parts = lax.all_to_all(sums, CTX, split_axis=0, concat_axis=0, tiled=True)
    [weights_grad] = call(
        weights_kernel,
        [ANY] * 8,
        [shape((2 * UNITS, D))],
        [pltpu.VMEM(k.shape, BF16) for k in (*kept, *kept)] + [pltpu.SemaphoreType.DMA((8,))],
        flops=2 * 4 * SLOTS * UNITS * D,
        moved=8 * 2**20,
        limit=VMEM_ALL,
    )(*early, *late)
    weights_grad = weights_grad.reshape(1, UNITS, 2, D)
    parts, weights_grad = lax.optimization_barrier((parts, weights_grad))
    [back] = call(total_kernel, [VMEM], [shape((ROWS, CHUNK))], moved=3 * 2**20)(parts)
    back, far_query = lax.optimization_barrier((back, far_query))
    returned = lax.all_to_all(
        back.reshape(EXPERTS, 8, CHUNK), "exp", split_axis=0, concat_axis=0, tiled=True
    ).reshape(ROWS, CHUNK)
    queries = call(join_kernel, [VMEM] * 2, [shape((64, CHUNK))] * 4, moved=2**20)(own_pack, far_query)
    queries = [queries[0]] + [moved_by(queries[k], "ctx_0", k) for k in (1, 2, 3)]
    [total] = call(tokens_kernel, [VMEM] * 7, [shape((CTX_COUNT, 64, CHUNK))], moved=2**20)(
        returned, even, odd, *queries
    )
    packs = lax.all_to_all(total, CTX, split_axis=0, concat_axis=0, tiled=True)
    [states_grad] = call(
        norm_grad_kernel,
        [VMEM] * 4,
        [shape((TOKENS, D))],
        [pltpu.VMEM((TOKENS, D), F32)],
        moved=3 * 2**20,
    )(packs, states, grads, norm_gain)
    return states_grad[None], keys_grad[None], values_grad[None], weights_grad


def solution(mesh):
    finer = Mesh(mesh.devices.reshape(4, 2, mesh.shape["exp"]), (*CTX, "exp"))
    return jax.shard_map(
        on_device,
        mesh=finer,
        in_specs=(
            P("exp", None, None),
            P("exp", None, None),
            P("exp", CTX, None),
            P("exp", CTX, None),
            P(),
            P("exp", None, None),
            P("exp", None, None),
            P("exp", CTX, None, None),
        ),
        out_specs=(
            P("exp", None, None),
            P("exp", CTX, None),
            P("exp", CTX, None),
            P("exp", CTX, None, None),
        ),
        check_vma=False,
    )
```

```python
import math

import jax
import jax.numpy as jnp
from jax import lax
from jax.experimental import pallas as pl
from jax.experimental.pallas import tpu as pltpu
from jax.sharding import Mesh
from jax.sharding import PartitionSpec as P

HEADS = 20
HEAD = 128
D = 2560
HALF = 1280
TOKENS = 128
KEYS = 128
UNITS = 256
EXPERTS = 32
CTX_COUNT = 8
ROWS = 256
SLOTS = 256
CHUNK = 640
CTX = ("ctx_0", "ctx_1")
EPSILON = 1e-05
SCALE = HEAD**-0.5
BF16 = jnp.bfloat16
F32 = jnp.float32
VMEM_LIMIT = 24 * 2**20
VMEM_ALL = 60 * 2**20
VMEM_MOST = 50 * 2**20

VMEM = pl.BlockSpec(memory_space=pltpu.VMEM)
SMEM = pl.BlockSpec(memory_space=pltpu.SMEM)
ANY = pl.BlockSpec(memory_space=pl.ANY)


def call(kernel, ins, outs, scratch=(), flops=0, moved=0, places=None, limit=VMEM_LIMIT):
    return pl.pallas_call(
        kernel,
        in_specs=ins,
        out_specs=places or [VMEM] * len(outs),
        out_shape=outs,
        scratch_shapes=list(scratch),
        compiler_params=pltpu.CompilerParams(vmem_limit_bytes=limit),
        cost_estimate=pl.CostEstimate(flops=flops, bytes_accessed=moved, transcendentals=0),
    )


def shape(dims, dtype=BF16):
    return jax.ShapeDtypeStruct(dims, dtype)


def dot(a, b, dims=((1,), (0,))):
    return lax.dot_general(a, b, (dims, ((), ())), preferred_element_type=F32)


def iota(dims, axis):
    return lax.broadcasted_iota(jnp.int32, dims, axis)


def one(mask):
    return jnp.where(mask, 1.0, 0.0).astype(BF16)


def route_kernel(place, states, grads, gain, ids, gates, normed_out, send, even, odd):
    c = place[0]
    x = states[...].astype(F32)
    inverse = lax.rsqrt(jnp.mean(x * x, axis=-1, keepdims=True) + EPSILON)
    normed_out[...] = (x * inverse * gain[...].reshape(1, D)).astype(BF16)
    expert = iota((ROWS, TOKENS), 0) // 8
    i = iota((ROWS, TOKENS), 0) % 8
    first = ids[0:1, :] == expert
    second = ids[1:2, :] == expert
    named = first | second
    before = one(iota((TOKENS, TOKENS), 0) < iota((TOKENS, TOKENS), 1))
    slot = dot(one(named), before).astype(jnp.int32)
    slot = jnp.where(named, slot, -1)
    even[...] = one(slot == 2 * i)
    odd[...] = one(slot == 2 * i + 1)
    mine = slot == 2 * c + i % 2
    gate = jnp.where(first, gates[0:1, :], 0.0) + jnp.where(second, gates[1:2, :], 0.0)
    gate = jnp.sum(jnp.where(mine, gate, 0.0), axis=1, keepdims=True)
    low = i < 4
    is_row = (i // 2) % 2 == 0
    row_low = one(mine & low & is_row)
    row_high = one(mine & (~low) & is_row)
    grad_low = one(mine & low & (~is_row))
    grad_high = one(mine & (~low) & (~is_row))
    rows = dot(row_low, normed_out[:, :HALF]) + dot(row_high, normed_out[:, HALF:])
    douts = dot(grad_low, grads[:, :HALF]) + dot(grad_high, grads[:, HALF:])
    send[...] = (rows + gate * douts).astype(BF16)


def scores_kernel(normed, grads, keys, values, weights_out, slopes_out, stats):
    for h in range(HEADS):
        at = slice(h * HEAD, (h + 1) * HEAD)
        s = dot(keys[:, at], normed[:, at], ((1,), (1,))) * SCALE
        peak = jnp.max(s, axis=0, keepdims=True)
        w = jnp.exp(s - peak)
        slopes = dot(values[:, at], grads[:, at], ((1,), (1,)))
        weights_out[h] = w
        slopes_out[h] = slopes
        stats[h : h + 1, :] = peak
        stats[24 + h : 25 + h, :] = jnp.sum(w, axis=0, keepdims=True)
        stats[48 + h : 49 + h, :] = jnp.sum(w * slopes, axis=0, keepdims=True)
    for part in range(3):
        at = 24 * part + HEADS
        stats[at : at + 4, :] = jnp.zeros((4, TOKENS), F32)


def merged(stats):
    peak = stats[0][:24]
    for one_side in stats[1:]:
        peak = jnp.maximum(peak, one_side[:24])
    total = inner = 0.0
    for one_side in stats:
        factor = jnp.exp(one_side[:24] - peak)
        total = total + one_side[24:48] * factor
        inner = inner + one_side[48:] * factor
    return jnp.concatenate([peak, total, inner], axis=0)


def score_grad_kernel(
    place,
    normed,
    grads,
    keys,
    weights,
    slopes,
    local,
    near,
    far,
    keys_grad,
    values_grad,
    own_pack,
    far_pack,
    query,
):
    peak = jnp.maximum(near[0:24, :], far[0:24, :])
    near_factor = jnp.exp(near[0:24, :] - peak)
    far_factor = jnp.exp(far[0:24, :] - peak)
    total = near[24:48, :] * near_factor + far[24:48, :] * far_factor
    inner = near[48:72, :] * near_factor + far[48:72, :] * far_factor
    total = jnp.where(iota((24, TOKENS), 0) < HEADS, total, 1.0)
    factor = jnp.exp(local[0:24, :] - peak) / total
    delta = inner / total
    for h in range(HEADS):
        at = slice(h * HEAD, (h + 1) * HEAD)
        probs = weights[h] * factor[h : h + 1, :]
        score_grad = (probs * (slopes[h] - delta[h : h + 1, :])).astype(BF16)
        values_grad[:, at] = dot(probs.astype(BF16), grads[:, at]).astype(BF16)
        keys_grad[:, at] = (dot(score_grad, normed[:, at]) * SCALE).astype(BF16)
        query[:, at] = dot(score_grad, keys[:, at], ((0,), (0,))) * SCALE
    lane = iota((64, 128), 1)
    first = place[0] % 2 == 0
    for g in range(CTX_COUNT // 2):
        row = (g - place[0] // 2 + 4) % 4
        tile = slice(2048 + 128 * g, 2176 + 128 * g)
        a, b = query[0:64, tile], query[64:128, tile]
        packs = []
        for f, tail in (
            (2 * g, jnp.where(lane < 64, a, pltpu.roll(b, 64, 1))),
            (2 * g + 1, jnp.where(lane < 64, pltpu.roll(a, 64, 1), b)),
        ):
            at = slice(256 * f, 256 * f + 256)
            packs.append(jnp.concatenate([query[0:64, at], query[64:128, at], tail], axis=1))
        own_pack[row] = jnp.where(first, packs[0], packs[1]).astype(BF16)
        far_pack[row] = jnp.where(first, packs[1], packs[0]).astype(BF16)


def join_kernel(own, far, *outs):
    for k in range(4):
        outs[k][...] = (own[k].astype(F32) + far[k].astype(F32)).astype(BF16)


def experts_of(blocks, w_in, w_out, rows, douts, act, pre_grad, put, after=lambda step: None):
    to, source = iota((ROWS, ROWS), 0), iota((ROWS, ROWS), 1)
    order = one(source == 8 * (to % 32) + to // 32)
    for k, block in enumerate(blocks):
        sorted_rows = dot(order, block()).astype(BF16)
        for q in range(2):
            where = slice(128 * q + 32 * k, 128 * q + 32 * k + 32)
            for half in range(2):
                lanes = slice(HALF * half, HALF * half + HALF)
                first = 128 * half + 32 * q
                rows[where, lanes] = sorted_rows[first : first + 32, :]
                douts[where, lanes] = sorted_rows[first + 64 : first + 96, :]
    after("rows")
    v = dot(rows[...], w_in[...], ((1,), (1,)))
    act_grad = dot(douts[...], w_out[...], ((1,), (1,)))
    root = math.sqrt(2 / math.pi)
    square = v * v
    t = jnp.tanh(root * (v + 0.044715 * (square * v)))
    act[...] = (0.5 * v * (1.0 + t)).astype(BF16)
    slope = 0.5 * (1.0 + t) + 0.5 * v * (1.0 - t * t) * (root * (1.0 + 3 * 0.044715 * square))
    pre_grad[...] = (act_grad * slope).astype(BF16)
    after("units")
    tails = dot(pre_grad[...], w_in[:, 2048:2560])
    lane = iota((128, 128), 1)
    for f in range(CTX_COUNT):
        part = dot(pre_grad[...], w_in[:, 256 * f : 256 * f + 256])
        put(f, slice(0, 256), part[0:128].astype(BF16))
        put(f, slice(256, 512), part[128:256].astype(BF16))
        tile = slice(128 * (f // 2), 128 * (f // 2) + 128)
        a, b = tails[0:128, tile], tails[128:256, tile]
        if f % 2 == 0:
            tail = jnp.where(lane < 64, a, pltpu.roll(b, 64, 1))
        else:
            tail = jnp.where(lane < 64, pltpu.roll(a, 64, 1), b)
        put(f, slice(512, 640), tail.astype(BF16))
        after(f)


def early_kernel(*refs):
    own, up, up_rest, down_rest, down, partner, w_in, w_out, sums = refs[:9]

    def put(f, lanes, value):
        sums[f, :, lanes] = value

    blocks = [
        lambda: own[...],
        lambda: jnp.concatenate([up[...], up_rest[...]], axis=0),
        lambda: jnp.concatenate([down_rest[...], down[...]], axis=0),
        lambda: partner[...],
    ]
    experts_of(blocks, w_in, w_out, *refs[9:], put)


def late_kernel(at_ref, *refs):
    given, results, held = refs[:9], refs[9:14], refs[14:]
    shards, (w_in, w_out), sums, kept = held[:4], held[4:6], held[6], held[7:11]
    arrived, left = held[11:]
    where = [pl.ds(pl.multiple_of(32 * at_ref[k], 32), 32) for k in range(CTX_COUNT)]
    landing = [
        *shards[:2],
        *(shards[k].at[128 * j : 128 * j + 128] for k in (2, 3) for j in range(2)),
        w_in,
        w_out,
    ]
    loads = [pltpu.make_async_copy(given[k], landing[k], arrived.at[k]) for k in range(8)]
    for load in loads:
        load.start()
    early = [
        pltpu.make_async_copy(
            given[8].at[:, 32 * k : 32 * k + 32, :], sums.at[:, where[k], :], arrived.at[8 + k]
        )
        for k in range(4)
    ]
    for load in early:
        load.start()
    stores = [pltpu.make_async_copy(kept[k], results[1 + k], left.at[k]) for k in range(4)]
    stores += [
        pltpu.make_async_copy(sums.at[f], results[0].at[f], left.at[4 + f])
        for f in range(CTX_COUNT)
    ]

    def block(k):
        for load in loads[k : k + 1] if k < 2 else loads[2 * k - 2 : 2 * k]:
            load.wait()
        return shards[k][...]

    def put(f, lanes, value):
        for k in range(4):
            sums[f, where[4 + k], lanes] = value[32 * k : 32 * k + 32]

    def after(step):
        if step == "rows":
            stores[0].start()
            stores[1].start()
            loads[6].wait()
            loads[7].wait()
        elif step == "units":
            stores[2].start()
            stores[3].start()
            for load in early:
                load.wait()
        else:
            stores[4 + step].start()

    blocks = [lambda k=k: block(k) for k in range(4)]
    experts_of(blocks, w_in, w_out, *kept, put, after)
    for store in stores:
        store.wait()


def weights_kernel(*refs):
    given, out, held, arrived = refs[:8], refs[8], refs[9:17], refs[17]
    loads = [pltpu.make_async_copy(given[k], held[k], arrived.at[k]) for k in range(8)]
    for load in loads:
        load.start()
    unit, column = iota((UNITS, 2 * UNITS), 0), iota((UNITS, 2 * UNITS), 1)
    even, odd = one(column == 2 * unit), one(column == 2 * unit + 1)
    for load in loads:
        load.wait()
    terms = []
    for rows, douts, act, pre_grad in (held[:4], held[4:]):
        terms.append((dot(pre_grad[...], even).astype(BF16), rows))
        terms.append((dot(act[...], odd).astype(BF16), douts))
    for n in range(D // 512):
        lanes = slice(512 * n, 512 * n + 512)
        out[:, lanes] = sum(dot(a, b[:, lanes], ((0,), (0,))) for a, b in terms).astype(BF16)


def total_kernel(parts, back):
    total = parts[0].astype(F32)
    for k in range(1, CTX_COUNT):
        total = total + parts[k].astype(F32)
    to, source = iota((ROWS, ROWS), 0), iota((ROWS, ROWS), 1)
    order = one(source == 32 * (to % 8) + to // 8)
    back[...] = dot(order, total.astype(BF16)).astype(BF16)


def tokens_kernel(returned, even, odd, own, below, across, above, out):
    query = (own[...].astype(F32) + across[...].astype(F32)) + (
        below[...].astype(F32) + above[...].astype(F32)
    )
    a = dot(even[...], returned[...], ((0,), (0,)))
    b = dot(odd[...], returned[...], ((0,), (0,)))
    wide = a[:, 0:256] + b[:, 256:512]
    tail = a[:, 512:640] + pltpu.roll(b[:, 512:640], 64, 1)
    lane = iota((64, 128), 1)
    tail = jnp.where(lane < 64, tail[0:64], pltpu.roll(tail[64:128], 64, 1))
    left = (wide[0:64] + query[:, 0:256]).astype(BF16)
    right = (wide[64:128] + query[:, 256:512]).astype(BF16)
    tail = (tail + query[:, 512:640]).astype(BF16)
    for f in range(CTX_COUNT):
        out[f, :, 0:256] = left
        out[f, :, 256:512] = right
        out[f, :, 512:640] = tail


def norm_grad_kernel(packs, states, grads, gain, out, total):
    for f in range(CTX_COUNT):
        at = slice(256 * f, 256 * f + 256)
        total[0:64, at] = packs[f, :, 0:256].astype(F32)
        total[64:128, at] = packs[f, :, 256:512].astype(F32)
    lane = iota((64, 128), 1)
    for g in range(CTX_COUNT // 2):
        at = slice(2048 + 128 * g, 2176 + 128 * g)
        a = packs[2 * g, :, 512:640].astype(F32)
        b = packs[2 * g + 1, :, 512:640].astype(F32)
        total[0:64, at] = jnp.where(lane < 64, a, pltpu.roll(b, 64, 1))
        total[64:128, at] = jnp.where(lane < 64, pltpu.roll(a, 64, 1), b)
    x = states[...].astype(F32)
    inverse = lax.rsqrt(jnp.mean(x * x, axis=-1, keepdims=True) + EPSILON)
    unit = x * inverse
    g = total[...] * gain[...].reshape(1, D)
    g = g - unit * jnp.mean(g * unit, axis=-1, keepdims=True)
    out[...] = (grads[...].astype(F32) + inverse * g).astype(BF16)


def moved_by(array, axis, step):
    count = lax.axis_size(axis)
    return lax.ppermute(array, axis, [(k, (k + step) % count) for k in range(count)])


def on_device(
    states, out_grad, doc_keys, doc_values, norm_gain, expert_ids, gate_values, expert_weights
):
    states, grads, keys, values = states[0], out_grad[0], doc_keys[0], doc_values[0]
    y, x = lax.axis_index("ctx_0"), lax.axis_index("ctx_1")
    place = (2 * y + x).astype(jnp.int32).reshape(1)
    normed, send, even, odd = call(
        route_kernel,
        [SMEM] + [VMEM] * 5,
        [shape((TOKENS, D)), shape((ROWS, HALF)), shape((ROWS, TOKENS)), shape((ROWS, TOKENS))],
        flops=2 * 4 * ROWS * TOKENS * HALF,
        moved=3 * 2**20,
        limit=VMEM_ALL,
    )(place, states, grads, norm_gain, expert_ids[0].T, gate_values[0].T)
    own = lax.all_to_all(
        send.reshape(EXPERTS, 8, HALF), "exp", split_axis=0, concat_axis=0, tiled=True
    ).reshape(ROWS, HALF)

    normed, expert_weights = lax.optimization_barrier((normed, expert_weights))
    w_in, w_out = expert_weights[0, :, 0, :], expert_weights[0, :, 1, :]
    keys, w_in, w_out = lax.optimization_barrier((keys, w_in, w_out))

    weights, slopes, stats = call(
        scores_kernel,
        [VMEM] * 4,
        [shape((HEADS, KEYS, TOKENS), F32), shape((HEADS, KEYS, TOKENS), F32), shape((72, TOKENS), F32)],
        flops=2 * 2 * KEYS * TOKENS * D,
        moved=5 * 2**20,
    )(normed, grads, keys, values)
    near = merged([stats] + [moved_by(stats, "ctx_0", k) for k in (1, 2, 3)])
    far = moved_by(near, "ctx_1", 1)
    own, near, far = lax.optimization_barrier((own, near, far))
    low, high = own[:128], own[128:]
    up, down = moved_by(low, "ctx_0", 1), moved_by(high, "ctx_0", 3)
    up_rest, down_rest = moved_by(high, "ctx_0", 1), moved_by(low, "ctx_0", 3)
    partner = moved_by(own, "ctx_1", 1)
    keys_grad, values_grad, own_pack, far_pack = call(
        score_grad_kernel,
        [SMEM] + [VMEM] * 8,
        [shape((KEYS, D)), shape((KEYS, D)), *[shape((4, 64, CHUNK))] * 2],
        [pltpu.VMEM((TOKENS, D), F32)],
        flops=3 * 2 * KEYS * TOKENS * D,
        moved=6 * 2**20,
        limit=VMEM_ALL,
    )(place, normed, grads, keys, weights, slopes, stats, near, far)
    up, down, far_pack = lax.optimization_barrier((up, down, far_pack))
    across = [moved_by(up, "ctx_0", 1), moved_by(down, "ctx_0", 3)]
    partner_up, partner_down = moved_by(partner, "ctx_0", 1), moved_by(partner, "ctx_0", 3)
    partner_across = [moved_by(piece, "ctx_1", 1) for piece in across]
    places = [(0, 0), (-1, 0), (1, 0), (0, 1), (-1, 1), (1, 1), (2, 0), (2, 1)]
    at = jnp.stack([2 * ((y + a + 4) % 4) + (x + b) % 2 for a, b in places]).astype(jnp.int32)
    kept = [shape((SLOTS, D))] * 2 + [shape((SLOTS, UNITS))] * 2
    early_sums, *early = call(
        early_kernel,
        [VMEM] * 8,
        [shape((CTX_COUNT, SLOTS // 2, CHUNK)), *kept],
        flops=2 * 3 * SLOTS * UNITS * D,
        moved=8 * 2**20,
        limit=VMEM_ALL,
    )(own, up, up_rest, down_rest, down, partner, w_in, w_out)
    early_sums, far_pack = lax.optimization_barrier((early_sums, far_pack))
    far_query = moved_by(far_pack, "ctx_1", 1)
    sums, *late = call(
        late_kernel,
        [SMEM] + [ANY] * 9,
        [shape((CTX_COUNT, ROWS, CHUNK)), *kept],
        [
            *[pltpu.VMEM((ROWS, HALF), BF16)] * 4,
            *[pltpu.VMEM((UNITS, D), BF16)] * 2,
            pltpu.VMEM((CTX_COUNT, ROWS, CHUNK), BF16),
            *[pltpu.VMEM(k.shape, BF16) for k in kept],
            pltpu.SemaphoreType.DMA((12,)),
            pltpu.SemaphoreType.DMA((4 + CTX_COUNT,)),
        ],
        flops=2 * 3 * SLOTS * UNITS * D,
        moved=12 * 2**20,
        places=[ANY] * 5,
        limit=VMEM_MOST,
    )(at, partner_up, partner_down, *across, *partner_across, w_in, w_out, early_sums)
    sums, far_query = lax.optimization_barrier((sums, far_query))
    parts = lax.all_to_all(sums, CTX, split_axis=0, concat_axis=0, tiled=True)
    [weights_grad] = call(
        weights_kernel,
        [ANY] * 8,
        [shape((2 * UNITS, D))],
        [pltpu.VMEM(k.shape, BF16) for k in (*kept, *kept)] + [pltpu.SemaphoreType.DMA((8,))],
        flops=2 * 4 * SLOTS * UNITS * D,
        moved=8 * 2**20,
        limit=VMEM_ALL,
    )(*early, *late)
    weights_grad = weights_grad.reshape(1, UNITS, 2, D)
    parts, weights_grad = lax.optimization_barrier((parts, weights_grad))
    [back] = call(total_kernel, [VMEM], [shape((ROWS, CHUNK))], moved=3 * 2**20)(parts)
    back, far_query = lax.optimization_barrier((back, far_query))
    returned = lax.all_to_all(
        back.reshape(EXPERTS, 8, CHUNK), "exp", split_axis=0, concat_axis=0, tiled=True
    ).reshape(ROWS, CHUNK)
    queries = call(join_kernel, [VMEM] * 2, [shape((64, CHUNK))] * 4, moved=2**20)(own_pack, far_query)
    queries = [queries[0]] + [moved_by(queries[k], "ctx_0", k) for k in (1, 2, 3)]
    [total] = call(tokens_kernel, [VMEM] * 7, [shape((CTX_COUNT, 64, CHUNK))], moved=2**20)(
        returned, even, odd, *queries
    )
    packs = lax.all_to_all(total, CTX, split_axis=0, concat_axis=0, tiled=True)
    [states_grad] = call(
        norm_grad_kernel,
        [VMEM] * 4,
        [shape((TOKENS, D))],
        [pltpu.VMEM((TOKENS, D), F32)],
        moved=3 * 2**20,
    )(packs, states, grads, norm_gain)
    return states_grad[None], keys_grad[None], values_grad[None], weights_grad


def solution(mesh):
    finer = Mesh(mesh.devices.reshape(4, 2, mesh.shape["exp"]), (*CTX, "exp"))
    return jax.shard_map(
        on_device,
        mesh=finer,
        in_specs=(
            P("exp", None, None),
            P("exp", None, None),
            P("exp", CTX, None),
            P("exp", CTX, None),
            P(),
            P("exp", None, None),
            P("exp", None, None),
            P("exp", CTX, None, None),
        ),
        out_specs=(
            P("exp", None, None),
            P("exp", CTX, None),
            P("exp", CTX, None),
            P("exp", CTX, None, None),
        ),
        check_vma=False,
    )
```
